128 devices in a mesh: ops: 8 (over y, core), blk: 16 (over z, x).
Axes of the slice: x: 4, y: 4, z: 4, core: 2. Of those that a mesh axis runs over, the one named last changes fastest.
Arguments:
- wavefunction: bfloat16 [64, 256, 256], P('blk'), as said below
- left_dims: int32 [64], replicated, may hold values from 128 to 256, as said below
- right_dims: int32 [64], replicated, may hold values from 128 to 256, as said below
- left_ops: bfloat16 [8, 512, 256, 256], P('ops', 'blk'), may hold values from -1 to 3
- right_ops: bfloat16 [8, 512, 256, 256], P('ops', 'blk'), may hold values from -1 to 1
- source_block: int32 [8, 4096], P('ops', 'blk'), may hold values from 0 to 63, as said below
- target_slot: int32 [8, 4096], P('ops', 'blk'), may hold values from 0 to 3
- left_index: int32 [8, 4096], P('ops', 'blk'), may hold values from 0 to 31
- right_index: int32 [8, 4096], P('ops', 'blk'), may hold values from 0 to 31
- pair_count: int32 [8, 16], P('ops', 'blk'), may hold values from 32 to 256, as said below
- h_diagonal: float32 [64, 256, 256], P('blk', 'ops'), may hold values from -4 to 4
Outputs:
- sigma_vector: float32 [64, 256, 256], P('blk', 'ops')
- correction: float32 [64, 256, 256], P('blk', 'ops')
The draws below stay inside these ranges and needn't reach their ends.
Inputs may be any that keep to these rules, and one draw needn't show every extreme that they name: `wavefunction`: each block is zero outside its first left_dims rows and first right_dims columns. `left_dims`: some block reaches 256. `right_dims`: some block reaches 256. `pair_count`: some device has all 256 slots live. `source_block`: some slots read the block that they add to.
All inputs are finite; a program needn't handle non-finite values.
Results may differ from the reference program's by a relative error of at most 0.0024.
Values may be sent and summed in bfloat16 or wider, within the bound.
No kernel may reach another device: no remote copies, remote signals or barrier semaphores. Data moves between devices by JAX's collectives and lax.ppermute only.
A program may use at most 128 MiB of HBM per device.

```python
import math
import jax
import jax.numpy as jnp
from jax import lax

DL = 256
DR = 256
BLK_DEV = 4
PAIRS_DEV = 256
LOPS_DEV = 32
ROPS_DEV = 32
NB = 64
GROUPS = 8
HOLDERS = 16
PAIRS = 4096
LSTORE = 512
RSTORE = 512


def sector_extents(key, largest):
    first, second = jax.random.split(key)
    extents = jax.random.randint(first, (NB,), largest // 2, largest + 1)
    widest = jax.random.randint(second, (), 0, NB)
    return extents.at[widest].set(largest).astype(jnp.int32)


def slot_targets(key):
    return jax.random.randint(jax.random.fold_in(key, 11), (GROUPS, PAIRS), 0, BLK_DEV).astype(jnp.int32)


def operator_blocks(key, count, width, noise_scale, diag_lo, diag_hi, outer):
    first, second = jax.random.split(key)
    noise = jnp.clip(jax.random.normal(first, (GROUPS, count, width, width)), -4.0, 4.0)
    weights = jax.random.uniform(second, (GROUPS, count, 1, 1), jnp.float32, diag_lo, diag_hi)
    on_diagonal = jnp.arange(width)[:, None] == jnp.arange(width)[None, :]
    blocks = jnp.where(on_diagonal[None, None], noise * noise_scale + weights, noise * noise_scale)
    return blocks * outer


def draw_left_dims(key, part):
    return sector_extents(jax.random.fold_in(key, 1), DL)


def draw_right_dims(key, part):
    return sector_extents(jax.random.fold_in(key, 2), DR)


def draw_wavefunction(key, part):
    left_live = sector_extents(jax.random.fold_in(key, 1), DL)
    right_live = sector_extents(jax.random.fold_in(key, 2), DR)
    key = jax.random.fold_in(key, 3)
    first, second = jax.random.split(key, 2)
    position = jnp.arange(NB, dtype=jnp.float32) / max(NB - 1, 1)
    block_scale = jnp.exp(position * math.log(3.0)) * jnp.exp(jax.random.uniform(second, (NB,)) * math.log(4.0))
    entries = jax.random.normal(first, (NB, DL, DR))
    row_ids = jnp.arange(DL)[None, :, None]
    column_ids = jnp.arange(DR)[None, None, :]
    inside = (row_ids < left_live[:, None, None]) & (column_ids < right_live[:, None, None])
    entries = jnp.where(inside, entries * block_scale[:, None, None], 0.0)
    return entries.astype(jnp.bfloat16)


def draw_pair_count(key, part):
    key = jax.random.fold_in(key, 5)
    first, second, third = jax.random.split(key, 3)
    counts = jax.random.randint(first, (GROUPS, HOLDERS), PAIRS_DEV // 8, PAIRS_DEV // 2 + 1)
    group_pick = jax.random.randint(second, (), 0, GROUPS)
    holder_pick = jax.random.randint(third, (), 0, HOLDERS)
    return counts.at[group_pick, holder_pick].set(PAIRS_DEV).astype(jnp.int32)


def draw_target_slot(key, part):
    return slot_targets(key)


def draw_source_block(key, part):
    targets = slot_targets(key)
    key = jax.random.fold_in(key, 7)
    first, second = jax.random.split(key)
    spread = jax.random.randint(first, (GROUPS, PAIRS), 0, NB)
    holder = jnp.arange(PAIRS, dtype=jnp.int32)[None, :] // PAIRS_DEV
    own_block = holder * BLK_DEV + targets
    same = jax.random.randint(second, (GROUPS, PAIRS), 0, 4) == 0
    return jnp.where(same, own_block, spread).astype(jnp.int32)


def draw_left_ops(key, part):
    key = jax.random.fold_in(key, 8)
    blocks = operator_blocks(key, LSTORE, DL, DL ** (-0.5), 0.6, 1.4, 1.0)
    return blocks.astype(jnp.bfloat16)


def draw_right_ops(key, part):
    key = jax.random.fold_in(key, 9)
    blocks = operator_blocks(key, RSTORE, DR, DR ** (-0.5), 0.6, 1.4, PAIRS_DEV ** (-0.5))
    return blocks.astype(jnp.bfloat16)


def touch_ends(values, rng, low, high):
    place = [jax.random.randint(jax.random.fold_in(rng, axis), (), 0, length) for axis, length in enumerate(values.shape)]
    longest = values.shape.index(max(values.shape))
    next_to = place[:longest] + [(place[longest] + 1) % values.shape[longest]] + place[longest + 1:]
    return values.at[tuple(place)].set(low).at[tuple(next_to)].set(high)


def shard_levels(rng, extent, cuts, smallest, high):
    def one(dim, shards_of):
        steps = jax.random.uniform(jax.random.fold_in(jax.random.fold_in(rng, 6), dim), (shards_of,), jnp.float32, smallest / len(cuts), high / len(cuts))
        return jnp.repeat(jnp.exp(steps), extent[dim] // shards_of).reshape((-1,) + (1,) * (len(extent) - dim - 1))

    gain = one(*cuts[0])
    for cut in cuts[1:]:
        gain = gain * one(*cut)
    return gain


def setup_inputs(seed: int = 0) -> dict:
    splits = jax.random.split(jax.random.key(seed), 12)
    wavefunction = draw_wavefunction(jax.random.fold_in(splits[11], 71), 0)
    left_dims = draw_left_dims(jax.random.fold_in(splits[11], 71), 0)
    right_dims = draw_right_dims(jax.random.fold_in(splits[11], 71), 0)
    left_ops = draw_left_ops(jax.random.fold_in(splits[11], 71), 0)
    right_ops = draw_right_ops(jax.random.fold_in(splits[11], 71), 0)
    source_block = draw_source_block(jax.random.fold_in(splits[11], 71), 0)
    target_slot = draw_target_slot(jax.random.fold_in(splits[11], 71), 0)
    left_index = touch_ends(jax.random.randint(splits[7], (GROUPS, PAIRS), 0, LOPS_DEV), jax.random.fold_in(splits[7], 1), 0, LOPS_DEV - 1).astype(jnp.int32)
    right_index = touch_ends(jax.random.randint(splits[8], (GROUPS, PAIRS), 0, ROPS_DEV), jax.random.fold_in(splits[8], 1), 0, ROPS_DEV - 1).astype(jnp.int32)
    pair_count = draw_pair_count(jax.random.fold_in(splits[11], 71), 0)
    h_diagonal = jnp.clip(jax.random.uniform(splits[10], (NB, DL, DR), jnp.float32, -4.0, 4.0) * shard_levels(splits[10], (NB, DL, DR), ((0, 16), (1, 8)), -0.4, 0.0), -4.0, 4.0)
    return dict(wavefunction=wavefunction, left_dims=left_dims, right_dims=right_dims, left_ops=left_ops, right_ops=right_ops, source_block=source_block, target_slot=target_slot, left_index=left_index, right_index=right_index, pair_count=pair_count, h_diagonal=h_diagonal)


def reference(wavefunction, left_dims, right_dims, left_ops, right_ops, source_block, target_slot, left_index, right_index, pair_count, h_diagonal):
    group_ids = jnp.broadcast_to(jnp.arange(GROUPS, dtype=jnp.int32)[:, None], (GROUPS, PAIRS))
    slot_ids = jnp.broadcast_to(jnp.arange(PAIRS, dtype=jnp.int32)[None, :], (GROUPS, PAIRS))
    holder = slot_ids // PAIRS_DEV
    within = slot_ids % PAIRS_DEV
    alive = (within < pair_count[group_ids, holder]).astype(jnp.int32).reshape(-1)
    sources = source_block.reshape(-1).astype(jnp.int32)
    targets = (holder * BLK_DEV + target_slot).reshape(-1).astype(jnp.int32)
    lefts = (group_ids * LSTORE + holder * LOPS_DEV + left_index).reshape(-1).astype(jnp.int32)
    rights = (group_ids * RSTORE + holder * ROPS_DEV + right_index).reshape(-1).astype(jnp.int32)
    left_flat = left_ops.reshape(GROUPS * LSTORE, DL, DL)
    right_flat = right_ops.reshape(GROUPS * RSTORE, DR, DR)
    batch_width = 16
    turns = GROUPS * PAIRS // batch_width
    stacked = jnp.stack([sources, targets, lefts, rights, alive], axis=1).reshape(turns, batch_width, 5)

    def accumulate(running, slot_rows):
        left_batch = left_flat[slot_rows[:, 2]].astype(jnp.float32)
        source_batch = wavefunction[slot_rows[:, 0]].astype(jnp.float32)
        right_batch = right_flat[slot_rows[:, 3]].astype(jnp.float32)
        product = jnp.einsum('pik,pkj->pij', left_batch, source_batch, precision=lax.Precision.HIGHEST)
        product = lax.optimization_barrier(product.astype(jnp.bfloat16)).astype(jnp.float32)
        term = jnp.einsum('pik,pjk->pij', product, right_batch, precision=lax.Precision.HIGHEST)
        term = term * slot_rows[:, 4].astype(jnp.float32)[:, None, None]
        return (running.at[slot_rows[:, 1]].add(term), None)
    summed, _ = lax.scan(accumulate, jnp.zeros((NB, DL, DR), jnp.float32), stacked)
    row_ids = jnp.arange(DL, dtype=jnp.int32)
    column_ids = jnp.arange(DR, dtype=jnp.int32)
    inside = (row_ids[None, :, None] < left_dims[:, None, None]) & (column_ids[None, None, :] < right_dims[:, None, None])
    sigma_vector = jnp.where(inside, summed, jnp.zeros_like(summed))
    state_wide = wavefunction.astype(jnp.float32)
    norm_sq = jnp.sum(state_wide * state_wide)
    rayleigh = jnp.sum(state_wide * sigma_vector) / norm_sq
    scaled = (sigma_vector - rayleigh * state_wide) / jnp.maximum(jnp.abs(h_diagonal - rayleigh), 1.0)
    along_state = jnp.sum(state_wide * scaled)
    projected = scaled - along_state / norm_sq * state_wide
    length_sq = jnp.sum(projected * projected)
    correction = projected / jnp.sqrt(length_sq / (NB * DL * DR) + 1e-06)
    return (sigma_vector, correction)
```

```python
import functools

import jax
import jax.numpy as jnp
from jax import lax
from jax.experimental import pallas as pl
from jax.experimental.pallas import tpu as pltpu
from jax.sharding import PartitionSpec as P

UNROLL = 8
F32 = jnp.float32
BF16 = jnp.bfloat16


def slots_kernel(
    rank, src_h, tgt_h, left_h, right_h, count_h, left_ops, right_ops, mine, other, own, out,
    src, tgt, left, right, count, lstore, rstore, blocks, acc, sems,
):
    holders, per_core = mine.shape[0], mine.shape[1]
    near = holders * per_core
    copies = [
        pltpu.make_async_copy(src_h, src, sems.at[0]),
        pltpu.make_async_copy(tgt_h, tgt, sems.at[1]),
        pltpu.make_async_copy(left_h, left, sems.at[2]),
        pltpu.make_async_copy(right_h, right, sems.at[3]),
        pltpu.make_async_copy(count_h, count, sems.at[4]),
        pltpu.make_async_copy(left_ops.at[0], lstore, sems.at[5]),
        pltpu.make_async_copy(right_ops.at[0], rstore, sems.at[6]),
        pltpu.make_async_copy(mine, blocks.at[0], sems.at[7]),
        pltpu.make_async_copy(other, blocks.at[1], sems.at[8]),
    ]
    for copy in copies:
        copy.start()
    acc[...] = jnp.zeros_like(acc)
    for copy in copies:
        copy.wait()
    core = lax.rem(rank[0], 2)
    live = count[0, 0]
    spare = acc.shape[0] - 1

    def step(i, carry):
        for u in range(UNROLL):
            k = i * UNROLL + u
            block = src[0, k]
            slot = lax.rem(block, 2 * per_core)
            side = jnp.where(slot // per_core == core, 0, 1)
            psi = blocks[side, block // (2 * per_core), lax.rem(slot, per_core)]
            product = jnp.dot(lstore[left[0, k]], psi, preferred_element_type=F32).astype(BF16)
            term = lax.dot_general(
                product, rstore[right[0, k]], (((1,), (1,)), ((), ())), preferred_element_type=F32
            )
            place = jnp.where(k < live, tgt[0, k], spare)
            acc[place] += term
        return carry

    lax.fori_loop(0, (live + UNROLL - 1) // UNROLL, step, 0)
    groups, rows = out.shape[0], out.shape[1] - 16
    share = rows // spare
    energy = jnp.zeros((1, 1), F32)
    for b in range(spare):
        part = acc[b]
        energy += jnp.sum(part * own[b].astype(F32), keepdims=True)
        for g in range(groups):
            out[g, b * share:(b + 1) * share, :] = part[g * share:(g + 1) * share].astype(BF16)
    high = energy.astype(BF16).astype(F32)
    mid = (energy - high).astype(BF16).astype(F32)
    low = energy - high - mid
    row = lax.broadcasted_iota(jnp.int32, (16, out.shape[2]), 0)
    note = jnp.where(row == 0, high, jnp.where(row == 1, mid, jnp.where(row == 2, low, 0.0)))
    for g in range(groups):
        out[g, rows:, :] = note.astype(BF16)


def sum_kernel(rank, left_dims, right_dims, arrived, own, sigma, notes):
    groups = arrived.shape[0]
    blocks, share, width = sigma.shape
    row = lax.broadcasted_iota(jnp.int32, (share, width), 0) + rank[0] * share
    column = lax.broadcasted_iota(jnp.int32, (share, width), 1)
    norm = jnp.zeros((1, 1), F32)
    for b in range(blocks):
        total = arrived[0, b * share:(b + 1) * share, :].astype(F32)
        for g in range(1, groups):
            total += arrived[g, b * share:(b + 1) * share, :].astype(F32)
        ident = rank[1] * blocks + b
        inside = (row < left_dims[ident]) & (column < right_dims[ident])
        sigma[b] = jnp.where(inside, total, 0.0)
        wide = own[b].astype(F32)
        norm += jnp.sum(wide * wide, keepdims=True)
    energy = arrived[0, blocks * share:, :].astype(F32)
    for g in range(1, groups):
        energy += arrived[g, blocks * share:, :].astype(F32)
    energy = jnp.sum(energy[:3, :1], keepdims=True)
    at = lax.broadcasted_iota(jnp.int32, notes.shape, 0)
    notes[...] = jnp.where(at == 0, energy, jnp.where(at == 1, norm, 0.0))


def scale_kernel(rank, notes, sigma, own, diagonal, scaled, sums):
    blocks, share, width = sigma.shape
    rayleigh = notes[0:1, 0:1] / notes[1:2, 0:1]
    along = jnp.zeros((1, 1), F32)
    square = jnp.zeros((1, 1), F32)
    start = pl.multiple_of(rank[0] * share, share)
    for b in range(blocks):
        state = own[b, pl.ds(start, share), :].astype(F32)
        value = (sigma[b] - rayleigh * state) / jnp.maximum(jnp.abs(diagonal[b] - rayleigh), 1.0)
        scaled[b] = value
        along += jnp.sum(state * value, keepdims=True)
        square += jnp.sum(value * value, keepdims=True)
    lane = lax.broadcasted_iota(jnp.int32, sums.shape, 1)
    sums[...] = jnp.where(lane == 0, along, jnp.where(lane == 1, square, 0.0))


def finish_kernel(slots_total, rank, arrived, notes, scaled, own, correction):
    blocks, share, width = scaled.shape
    sums = jnp.sum(arrived[...], axis=0, keepdims=True)
    along, square = sums[0:1, 0:1], sums[0:1, 1:2]
    ratio = along / notes[1:2, 0:1]
    length_sq = jnp.maximum(square - along * ratio, 0.0)
    factor = jnp.sqrt(length_sq / slots_total + 1e-06)
    start = pl.multiple_of(rank[0] * share, share)
    for b in range(blocks):
        state = own[b, pl.ds(start, share), :].astype(F32)
        correction[b] = (scaled[b] - ratio * state) / factor


def body(
    wavefunction,
    left_dims,
    right_dims,
    left_ops,
    right_ops,
    source_block,
    target_slot,
    left_index,
    right_index,
    pair_count,
    h_diagonal,
):
    groups = lax.axis_size("ops")
    holders = lax.axis_size("blk")
    group_rank = lax.axis_index("ops")
    rank = jnp.stack([group_rank, lax.axis_index("blk")]).astype(jnp.int32)
    own_blocks, left_width, right_width = wavefunction.shape
    share = left_width // groups
    per_core = own_blocks // 2
    smem = pl.BlockSpec(memory_space=pltpu.SMEM)
    vmem = pl.BlockSpec(memory_space=pltpu.VMEM)
    anywhere = pl.BlockSpec(memory_space=pl.ANY)

    part = lax.dynamic_slice_in_dim(wavefunction, lax.rem(group_rank, 2) * per_core, per_core, 0)
    mine = lax.all_to_all(
        jnp.broadcast_to(part[None], (holders,) + part.shape), "blk", 0, 0
    )
    other = lax.ppermute(mine, "ops", [(i, i ^ 1) for i in range(groups)])

    slots = source_block.shape[1]
    rows = own_blocks * share
    outgoing = pl.pallas_call(
        slots_kernel,
        out_shape=jax.ShapeDtypeStruct((groups, rows + 16, right_width), BF16),
        in_specs=[smem] + [anywhere] * 9 + [vmem],
        out_specs=vmem,
        scratch_shapes=[pltpu.SMEM((1, slots), jnp.int32)] * 4
        + [
            pltpu.SMEM((1, 1), jnp.int32),
            pltpu.VMEM(left_ops.shape[1:], BF16),
            pltpu.VMEM(right_ops.shape[1:], BF16),
            pltpu.VMEM((2,) + mine.shape, BF16),
            pltpu.VMEM((own_blocks + 1, left_width, right_width), F32),
            pltpu.SemaphoreType.DMA((9,)),
        ],
        compiler_params=pltpu.CompilerParams(vmem_limit_bytes=28 * 2**20),
        name="slots",
    )(
        rank, source_block, target_slot, left_index, right_index, pair_count,
        left_ops, right_ops, mine, other, wavefunction,
    )
    arrived = lax.all_to_all(outgoing, "ops", 0, 0)
    shard = jax.ShapeDtypeStruct((own_blocks, share, right_width), F32)
    sigma_vector, notes = pl.pallas_call(
        sum_kernel,
        out_shape=(shard, jax.ShapeDtypeStruct((8, 128), F32)),
        in_specs=[smem, smem, smem, vmem, vmem],
        out_specs=(vmem, vmem),
        name="group_sum",
    )(rank, left_dims, right_dims, arrived, wavefunction)
    for steps in ((1, 3, 2), (4, 12, 8)):
        parts = [lax.ppermute(notes, "blk", [(i, i ^ d) for i in range(holders)]) for d in steps]
        notes = (notes + parts[0]) + (parts[1] + parts[2])
    scaled, sums = pl.pallas_call(
        scale_kernel,
        out_shape=(shard, jax.ShapeDtypeStruct((groups * holders, 128), F32)),
        in_specs=[smem, vmem, vmem, vmem, vmem],
        out_specs=(vmem, vmem),
        name="scale",
    )(rank, notes, sigma_vector, wavefunction, h_diagonal)
    all_sums = lax.all_to_all(sums, ("ops", "blk"), 0, 0, tiled=True)
    correction = pl.pallas_call(
        functools.partial(finish_kernel, left_dims.shape[0] * left_width * right_width),
        out_shape=shard,
        in_specs=[smem, vmem, vmem, vmem, vmem],
        out_specs=vmem,
        name="finish",
    )(rank, all_sums, notes, scaled, wavefunction)
    return (sigma_vector, correction)


def solution(mesh):
    in_specs = (
        P("blk", None, None),
        P(),
        P(),
        P("ops", "blk", None, None),
        P("ops", "blk", None, None),
        P("ops", "blk"),
        P("ops", "blk"),
        P("ops", "blk"),
        P("ops", "blk"),
        P("ops", "blk"),
        P("blk", "ops", None),
    )
    out_specs = (P("blk", "ops", None), P("blk", "ops", None))
    return jax.shard_map(body, mesh=mesh, in_specs=in_specs, out_specs=out_specs, check_vma=False)
```

```python
import functools

import jax
import jax.numpy as jnp
from jax import lax
from jax.experimental import pallas as pl
from jax.experimental.pallas import tpu as pltpu
from jax.sharding import PartitionSpec as P

UNROLL = 16
TAIL = 4
LIST = 264
SPARE = 4
LEFT, RIGHT, TARGET, KIND = 4, 9, 14, 17
STEPS = (
    ((1, 3), (4, 12)),
    ((3, 1), (12, 4)),
    ((4, 12), (1, 3)),
    ((12, 4), (3, 1)),
)
F32 = jnp.float32
BF16 = jnp.bfloat16


def place_kernel(words, counts, lists, totals):
    for group in range(2):
        first, second = 2 * group * LIST, (2 * group + 1) * LIST

        def place(i, filled, group=group, first=first, second=second):
            early, late = filled
            for u in range(8):
                word = words[group, i * 8 + u]
                kind = word >> KIND
                where = jnp.where(
                    kind == 0, first + early, jnp.where(kind == 1, second + late, 4 * LIST)
                )
                lists[0, where] = word
                early += jnp.where(kind == 0, 1, 0)
                late += jnp.where(kind == 1, 1, 0)
            return early, late

        turns = (counts[group, 0] + 7) // 8
        early, late = lax.fori_loop(0, turns, place, (jnp.int32(0), jnp.int32(0)))
        for u in range(TAIL):
            lists[0, first + early + u] = SPARE << TARGET
            lists[0, second + late + u] = SPARE << TARGET
        totals[0, 2 * group] = early
        totals[0, 2 * group + 1] = late


def run_slots(lists, totals, which, lefts, rights, blocks, acc):
    for group in range(2):
        base = (2 * group + which) * LIST
        live = totals[0, 2 * group + which]
        lstore, rstore = lefts[group], rights[group]

        def one(k, lstore=lstore, rstore=rstore):
            word = lists[0, k]
            psi = blocks[(word >> 3) & 1, word & 7]
            product = jnp.dot(
                lstore[0, (word >> LEFT) & 31], psi, preferred_element_type=F32
            ).astype(BF16)
            term = lax.dot_general(
                product, rstore[0, (word >> RIGHT) & 31], (((1,), (1,)), ((), ())),
                preferred_element_type=F32,
            )
            acc[(word >> TARGET) & 7] += term

        def many(i, carry, width, offset, one=one):
            for u in range(width):
                one(offset + i * width + u)
            return carry

        turns = live // UNROLL
        lax.fori_loop(0, turns, functools.partial(many, width=UNROLL, offset=base), 0)
        rest = live - turns * UNROLL
        lax.fori_loop(
            0,
            (rest + TAIL - 1) // TAIL,
            functools.partial(many, width=TAIL, offset=base + turns * UNROLL),
            0,
        )


def early_kernel(
    lists, totals, left0, left1, right0, right1, first, second, acc, blocks, sems
):
    copies = [
        pltpu.make_async_copy(first, blocks.at[0], sems.at[0]),
        pltpu.make_async_copy(second, blocks.at[1], sems.at[1]),
    ]
    for copy in copies:
        copy.start()
    acc[...] = jnp.zeros_like(acc)
    for copy in copies:
        copy.wait()
    run_slots(lists, totals, 0, (left0, left1), (right0, right1), blocks, acc)


def late_kernel(
    lists, totals, left0, left1, right0, right1, first, second, begun, own, out, blocks, acc, sems
):
    copies = [
        pltpu.make_async_copy(first, blocks.at[0], sems.at[0]),
        pltpu.make_async_copy(second, blocks.at[1], sems.at[1]),
    ]
    for copy in copies:
        copy.start()
    acc[...] = begun[...]
    for copy in copies:
        copy.wait()
    run_slots(lists, totals, 1, (left0, left1), (right0, right1), blocks, acc)
    groups, rows = out.shape[0], out.shape[1] - 16
    share = rows // SPARE
    energy = jnp.zeros((1, 1), F32)
    for b in range(SPARE):
        part = acc[b]
        energy += jnp.sum(part * own[b].astype(F32), keepdims=True)
        for g in range(groups):
            out[g, b * share:(b + 1) * share, :] = part[g * share:(g + 1) * share].astype(BF16)
    high = energy.astype(BF16).astype(F32)
    mid = (energy - high).astype(BF16).astype(F32)
    low = energy - high - mid
    row = lax.broadcasted_iota(jnp.int32, (16, out.shape[2]), 0)
    note = jnp.where(row == 0, high, jnp.where(row == 1, mid, jnp.where(row == 2, low, 0.0)))
    for g in range(groups):
        out[g, rows:, :] = note.astype(BF16)


def sum_kernel(rank, left_dims, right_dims, arrived, own, sigma, notes):
    groups = arrived.shape[0]
    blocks, share, width = sigma.shape
    row = lax.broadcasted_iota(jnp.int32, (share, width), 0) + rank[0] * share
    column = lax.broadcasted_iota(jnp.int32, (share, width), 1)
    norm = jnp.zeros((1, 1), F32)
    for b in range(blocks):
        total = arrived[0, b * share:(b + 1) * share, :].astype(F32)
        for g in range(1, groups):
            total += arrived[g, b * share:(b + 1) * share, :].astype(F32)
        ident = rank[1] * blocks + b
        inside = (row < left_dims[ident]) & (column < right_dims[ident])
        sigma[b] = jnp.where(inside, total, 0.0)
        wide = own[b].astype(F32)
        norm += jnp.sum(wide * wide, keepdims=True)
    energy = arrived[0, blocks * share:, :].astype(F32)
    for g in range(1, groups):
        energy += arrived[g, blocks * share:, :].astype(F32)
    energy = jnp.sum(energy[:3, :1], keepdims=True)
    at = lax.broadcasted_iota(jnp.int32, notes.shape, 0)
    notes[...] = jnp.where(at == 0, energy, jnp.where(at == 1, norm, 0.0))


def scale_kernel(rank, notes, sigma, own, diagonal, scaled, sums):
    blocks, share, width = sigma.shape
    rayleigh = notes[0:1, 0:1] / notes[1:2, 0:1]
    along = jnp.zeros((1, 1), F32)
    square = jnp.zeros((1, 1), F32)
    start = pl.multiple_of(rank[0] * share, share)
    for b in range(blocks):
        state = own[b, pl.ds(start, share), :].astype(F32)
        value = (sigma[b] - rayleigh * state) / jnp.maximum(jnp.abs(diagonal[b] - rayleigh), 1.0)
        scaled[b] = value
        along += jnp.sum(state * value, keepdims=True)
        square += jnp.sum(value * value, keepdims=True)
    lane = lax.broadcasted_iota(jnp.int32, sums.shape, 1)
    sums[...] = jnp.where(lane == 0, along, jnp.where(lane == 1, square, 0.0))


def finish_kernel(slots_total, rank, arrived, notes, scaled, own, correction):
    blocks, share, width = scaled.shape
    sums = jnp.sum(arrived[...], axis=0, keepdims=True)
    along, square = sums[0:1, 0:1], sums[0:1, 1:2]
    ratio = along / notes[1:2, 0:1]
    length_sq = jnp.maximum(square - along * ratio, 0.0)
    factor = jnp.sqrt(length_sq / slots_total + 1e-06)
    start = pl.multiple_of(rank[0] * share, share)
    for b in range(blocks):
        state = own[b, pl.ds(start, share), :].astype(F32)
        correction[b] = (scaled[b] - ratio * state) / factor


def body(
    wavefunction,
    left_dims,
    right_dims,
    left_ops,
    right_ops,
    source_block,
    target_slot,
    left_index,
    right_index,
    pair_count,
    h_diagonal,
):
    groups = lax.axis_size("ops")
    holders = lax.axis_size("blk")
    group_rank = lax.axis_index("ops")
    rank = jnp.stack([group_rank, lax.axis_index("blk")]).astype(jnp.int32)
    own_blocks, left_width, right_width = wavefunction.shape
    share = left_width // groups
    per_core = own_blocks // 2
    smem = pl.BlockSpec(memory_space=pltpu.SMEM)
    vmem = pl.BlockSpec(memory_space=pltpu.VMEM)
    anywhere = pl.BlockSpec(memory_space=pl.ANY)

    core = lax.rem(group_rank, 2)
    holder = lax.axis_index("blk")
    pairs = [(i, i ^ 1) for i in range(groups)]
    half = lax.dynamic_slice_in_dim(wavefunction, core * per_core, per_core, 0)
    left_other = lax.ppermute(left_ops, "ops", pairs)
    right_other = lax.ppermute(right_ops, "ops", pairs)
    tables = jnp.stack([source_block, target_slot, left_index, right_index], axis=1)
    counts = jnp.broadcast_to(pair_count, (1, 128))
    tables_other = lax.ppermute(tables, "ops", pairs)
    counts_other = lax.ppermute(counts, "ops", pairs)

    def exchange(x, masks):
        return lax.ppermute(
            x,
            ("ops", "blk"),
            [
                (g * holders + h, g * holders + (h ^ masks[g % 2]))
                for g in range(groups)
                for h in range(holders)
            ],
        )

    first, second = half[:1], half[1:]
    for step, (one, two) in enumerate(STEPS):
        if step:
            first = jnp.concatenate([first, first_new])
            second = jnp.concatenate([second, second_new])
        first_new = exchange(first, one)
        second_new = exchange(second, two)

    tables = jnp.concatenate([tables, tables_other])
    counts = jnp.concatenate([counts, counts_other])
    sources, targets, lefts, rights = (tables[:, i] for i in range(4))
    slots = sources.shape[1]
    away = (sources // own_blocks) ^ holder

    def code(bits):
        gray = bits ^ (bits >> 1)
        return jnp.where(core == 0, gray, ((gray & 1) << 1) | (gray >> 1))

    along_x, along_z = code(away & 3), code(away >> 2)
    within = lax.rem(sources, own_blocks)
    stream = within & 1
    entry = jnp.where(stream == 0, along_x | (along_z << 2), along_z | (along_x << 2))
    here = (within >> 1 == core) & (
        jnp.arange(slots, dtype=jnp.int32)[None, :] < counts[:, :1]
    )
    kind = jnp.where(here, entry >> 3, 2)
    words = (
        (entry & 7)
        | (stream << 3)
        | (lefts << LEFT)
        | (rights << RIGHT)
        | (targets << TARGET)
        | (kind << KIND)
    )
    lists, totals = pl.pallas_call(
        place_kernel,
        out_shape=(
            jax.ShapeDtypeStruct((1, 4 * LIST + 1), jnp.int32),
            jax.ShapeDtypeStruct((1, 4), jnp.int32),
        ),
        in_specs=[smem, smem],
        out_specs=(smem, smem),
        name="place",
        cost_estimate=pl.CostEstimate(flops=10**9, bytes_accessed=10**4, transcendentals=0),
    )(words, counts)
    pinned = [
        pltpu.with_memory_space_constraint(x, pltpu.VMEM)
        for x in (left_ops, left_other, right_ops, right_other)
    ]
    acc_shape = (own_blocks + 1, left_width, right_width)
    begun = pl.pallas_call(
        early_kernel,
        out_shape=jax.ShapeDtypeStruct(acc_shape, F32),
        in_specs=[smem, smem] + [vmem] * 4 + [anywhere] * 2,
        out_specs=vmem,
        scratch_shapes=[
            pltpu.VMEM((2,) + first.shape, BF16),
            pltpu.SemaphoreType.DMA((2,)),
        ],
        compiler_params=pltpu.CompilerParams(vmem_limit_bytes=20 * 2**20),
        name="early",
        cost_estimate=pl.CostEstimate(flops=8 * 10**9, bytes_accessed=10**6, transcendentals=0),
    )(lists, totals, *pinned, first, second)
    rows = own_blocks * share
    outgoing = pl.pallas_call(
        late_kernel,
        out_shape=jax.ShapeDtypeStruct((groups, rows + 16, right_width), BF16),
        in_specs=[smem, smem] + [vmem] * 4 + [anywhere] * 2 + [vmem] * 2,
        out_specs=vmem,
        scratch_shapes=[
            pltpu.VMEM((2,) + first.shape, BF16),
            pltpu.VMEM(acc_shape, F32),
            pltpu.SemaphoreType.DMA((2,)),
        ],
        compiler_params=pltpu.CompilerParams(vmem_limit_bytes=20 * 2**20),
        name="late",
        cost_estimate=pl.CostEstimate(flops=5 * 10**9, bytes_accessed=10**6, transcendentals=0),
    )(lists, totals, *pinned, first_new, second_new, begun, wavefunction)
    arrived = lax.all_to_all(outgoing, "ops", 0, 0)
    shard = jax.ShapeDtypeStruct((own_blocks, share, right_width), F32)
    sigma_vector, notes = pl.pallas_call(
        sum_kernel,
        out_shape=(shard, jax.ShapeDtypeStruct((8, 128), F32)),
        in_specs=[smem, smem, smem, vmem, vmem],
        out_specs=(vmem, vmem),
        name="group_sum",
    )(rank, left_dims, right_dims, arrived, wavefunction)
    for steps in ((1, 3, 2), (4, 12, 8)):
        parts = [lax.ppermute(notes, "blk", [(i, i ^ d) for i in range(holders)]) for d in steps]
        notes = (notes + parts[0]) + (parts[1] + parts[2])
    scaled, sums = pl.pallas_call(
        scale_kernel,
        out_shape=(shard, jax.ShapeDtypeStruct((groups * holders, 128), F32)),
        in_specs=[smem, vmem, vmem, vmem, vmem],
        out_specs=(vmem, vmem),
        name="scale",
    )(rank, notes, sigma_vector, wavefunction, h_diagonal)
    all_sums = lax.all_to_all(sums, ("ops", "blk"), 0, 0, tiled=True)
    correction = pl.pallas_call(
        functools.partial(finish_kernel, left_dims.shape[0] * left_width * right_width),
        out_shape=shard,
        in_specs=[smem, vmem, vmem, vmem, vmem],
        out_specs=vmem,
        name="finish",
    )(rank, all_sums, notes, scaled, wavefunction)
    return (sigma_vector, correction)


def solution(mesh):
    in_specs = (
        P("blk", None, None),
        P(),
        P(),
        P("ops", "blk", None, None),
        P("ops", "blk", None, None),
        P("ops", "blk"),
        P("ops", "blk"),
        P("ops", "blk"),
        P("ops", "blk"),
        P("ops", "blk"),
        P("blk", "ops", None),
    )
    out_specs = (P("blk", "ops", None), P("blk", "ops", None))
    return jax.shard_map(body, mesh=mesh, in_specs=in_specs, out_specs=out_specs, check_vma=False)
```

```python
import functools

import jax
import jax.numpy as jnp
from jax import lax
from jax.experimental import pallas as pl
from jax.experimental.pallas import tpu as pltpu
from jax.sharding import PartitionSpec as P

UNROLL = 16
TAIL = 4
LIST = 528
SPARE = 4
LEFT, RIGHT, TARGET, KIND = 4, 10, 16, 19
STEPS = (
    ((1, 3), (4, 12)),
    ((3, 1), (12, 4)),
    ((4, 12), (1, 3)),
    ((12, 4), (3, 1)),
)
F32 = jnp.float32
BF16 = jnp.bfloat16


def place_kernel(
    words, counts, left0, left1, right0, right1, first, second,
    lists, totals, lefts, rights, blocks, sems,
):
    copies = [
        pltpu.make_async_copy(source, target, sems.at[i])
        for i, (source, target) in enumerate((
            (left0.at[0], lefts.at[0]),
            (left1.at[0], lefts.at[1]),
            (right0.at[0], rights.at[0]),
            (right1.at[0], rights.at[1]),
            (first, blocks.at[0]),
            (second, blocks.at[1]),
        ))
    ]
    for copy in copies:
        copy.start()
    early, late = jnp.int32(0), jnp.int32(0)
    for group in range(2):

        def place(i, filled, group=group):
            early, late = filled
            for u in range(8):
                word = words[group, i * 8 + u]
                kind = word >> KIND
                lists[0, jnp.where(kind == 0, early, jnp.where(kind == 1, LIST + late, 2 * LIST))] = word
                early += jnp.where(kind == 0, 1, 0)
                late += jnp.where(kind == 1, 1, 0)
            return early, late

        early, late = lax.fori_loop(0, (counts[group, 0] + 7) // 8, place, (early, late))
    for u in range(UNROLL):
        lists[0, early + u] = SPARE << TARGET
        lists[0, LIST + late + u] = SPARE << TARGET
    totals[0, 0] = early
    totals[0, 1] = late
    for copy in copies:
        copy.wait()


def run_slots(lists, totals, which, lefts, rights, blocks, acc):
    def many(i, carry, width, offset):
        for u in range(width):
            word = lists[0, offset + i * width + u]
            left, right = (word >> LEFT) & 63, (word >> RIGHT) & 63
            psi = blocks[(word >> 3) & 1, word & 7]
            product = jnp.dot(
                lefts[left >> 5, left & 31], psi, preferred_element_type=F32
            ).astype(BF16)
            acc[(word >> TARGET) & 7] += lax.dot_general(
                product, rights[right >> 5, right & 31], (((1,), (1,)), ((), ())),
                preferred_element_type=F32,
            )
        return carry

    live, base = totals[0, which], which * LIST
    turns = (live + UNROLL - 1 - 2 * TAIL) // UNROLL
    lax.fori_loop(0, turns, functools.partial(many, width=UNROLL, offset=base), 0)
    rest = jnp.maximum(live - turns * UNROLL, 0)
    lax.fori_loop(
        0,
        (rest + TAIL - 1) // TAIL,
        functools.partial(many, width=TAIL, offset=base + turns * UNROLL),
        0,
    )


def early_kernel(lists, totals, lefts, rights, blocks, acc):
    acc[...] = jnp.zeros_like(acc)
    run_slots(lists, totals, 0, lefts, rights, blocks, acc)


def late_kernel(lists, totals, lefts, rights, first, second, begun, out, acc, blocks, sems):
    copies = [
        pltpu.make_async_copy(first, blocks.at[0], sems.at[0]),
        pltpu.make_async_copy(second, blocks.at[1], sems.at[1]),
    ]
    for copy in copies:
        copy.start()
    acc[...] = begun[...]
    for copy in copies:
        copy.wait()
    run_slots(lists, totals, 1, lefts, rights, blocks, acc)
    groups, rows = out.shape[0], out.shape[1]
    share = rows // SPARE
    for b in range(SPARE):
        for g in range(groups):
            out[g, b * share:(b + 1) * share, :] = acc[b, g * share:(g + 1) * share].astype(BF16)


def energy_kernel(groups, acc, own, sums):
    energy = jnp.zeros((1, 1), F32)
    norm = jnp.zeros((1, 1), F32)
    for b in range(SPARE):
        wide = own[b].astype(F32)
        energy += jnp.sum(acc[b] * wide, keepdims=True)
        norm += jnp.sum(wide * wide, keepdims=True)
    row = lax.broadcasted_iota(jnp.int32, sums.shape, 0)
    sums[...] = jnp.where(row == 0, energy, jnp.where(row == 1, norm / groups, 0.0))


def combine_kernel(
    rank, left_dims, right_dims, arrived, totals, own, diagonal, sigma, scaled, sums
):
    groups = arrived.shape[0]
    blocks, share, width = sigma.shape
    rayleigh = totals[0:1, 0:1] / totals[1:2, 0:1]
    row = lax.broadcasted_iota(jnp.int32, (share, width), 0) + rank[0] * share
    column = lax.broadcasted_iota(jnp.int32, (share, width), 1)
    start = pl.multiple_of(rank[0] * share, share)
    along = jnp.zeros((1, 1), F32)
    square = jnp.zeros((1, 1), F32)
    for b in range(blocks):
        total = arrived[0, b * share:(b + 1) * share, :].astype(F32)
        for g in range(1, groups):
            total += arrived[g, b * share:(b + 1) * share, :].astype(F32)
        ident = rank[1] * blocks + b
        inside = (row < left_dims[ident]) & (column < right_dims[ident])
        total = jnp.where(inside, total, 0.0)
        sigma[b] = total
        state = own[b, pl.ds(start, share), :].astype(F32)
        value = (total - rayleigh * state) / jnp.maximum(jnp.abs(diagonal[b] - rayleigh), 1.0)
        scaled[b] = value
        along += jnp.sum(state * value, keepdims=True)
        square += jnp.sum(value * value, keepdims=True)
    lane = lax.broadcasted_iota(jnp.int32, sums.shape, 1)
    sums[...] = jnp.where(lane == 0, along, jnp.where(lane == 1, square, 0.0))


def finish_kernel(slots_total, rank, arrived, totals, scaled, own, correction):
    blocks, share, width = scaled.shape
    sums = jnp.sum(arrived[...], axis=0, keepdims=True)
    along, square = sums[0:1, 0:1], sums[0:1, 1:2]
    ratio = along / totals[1:2, 0:1]
    length_sq = jnp.maximum(square - along * ratio, 0.0)
    factor = jnp.sqrt(length_sq / slots_total + 1e-06)
    start = pl.multiple_of(rank[0] * share, share)
    for b in range(blocks):
        state = own[b, pl.ds(start, share), :].astype(F32)
        correction[b] = (scaled[b] - ratio * state) / factor


def body(
    wavefunction,
    left_dims,
    right_dims,
    left_ops,
    right_ops,
    source_block,
    target_slot,
    left_index,
    right_index,
    pair_count,
    h_diagonal,
):
    groups = lax.axis_size("ops")
    holders = lax.axis_size("blk")
    group_rank = lax.axis_index("ops")
    rank = jnp.stack([group_rank, lax.axis_index("blk")]).astype(jnp.int32)
    own_blocks, left_width, right_width = wavefunction.shape
    share = left_width // groups
    per_core = own_blocks // 2
    smem = pl.BlockSpec(memory_space=pltpu.SMEM)
    vmem = pl.BlockSpec(memory_space=pltpu.VMEM)
    anywhere = pl.BlockSpec(memory_space=pl.ANY)

    core = lax.rem(group_rank, 2)
    holder = lax.axis_index("blk")
    pairs = [(i, i ^ 1) for i in range(groups)]
    half = lax.dynamic_slice_in_dim(wavefunction, core * per_core, per_core, 0)
    left_other = lax.ppermute(left_ops, "ops", pairs)
    right_other = lax.ppermute(right_ops, "ops", pairs)
    tables = jnp.stack([source_block, target_slot, left_index, right_index], axis=1)
    counts = jnp.broadcast_to(pair_count, (1, 128))
    tables_other = lax.ppermute(tables, "ops", pairs)
    counts_other = lax.ppermute(counts, "ops", pairs)

    def exchange(x, masks):
        return lax.ppermute(
            x,
            ("ops", "blk"),
            [
                (g * holders + h, g * holders + (h ^ masks[g % 2]))
                for g in range(groups)
                for h in range(holders)
            ],
        )

    first, second = half[:1], half[1:]
    for step, (one, two) in enumerate(STEPS):
        if step:
            first = jnp.concatenate([first, first_new])
            second = jnp.concatenate([second, second_new])
        first_new = exchange(first, one)
        second_new = exchange(second, two)

    tables = jnp.concatenate([tables, tables_other])
    counts = jnp.concatenate([counts, counts_other])
    sources, targets, lefts, rights = (tables[:, i] for i in range(4))
    slots = sources.shape[1]
    away = (sources // own_blocks) ^ holder

    def code(bits):
        gray = bits ^ (bits >> 1)
        return jnp.where(core == 0, gray, ((gray & 1) << 1) | (gray >> 1))

    along_x, along_z = code(away & 3), code(away >> 2)
    within = lax.rem(sources, own_blocks)
    stream = within & 1
    entry = jnp.where(stream == 0, along_x | (along_z << 2), along_z | (along_x << 2))
    here = (within >> 1 == core) & (
        jnp.arange(slots, dtype=jnp.int32)[None, :] < counts[:, :1]
    )
    kind = jnp.where(here, entry >> 3, 2)
    store = jnp.arange(2, dtype=jnp.int32)[:, None] * left_ops.shape[1]
    words = (
        (entry & 7)
        | (stream << 3)
        | ((lefts + store) << LEFT)
        | ((rights + store) << RIGHT)
        | (targets << TARGET)
        | (kind << KIND)
    )
    both = pltpu.VMEM((2,) + left_ops.shape[1:], BF16)
    lists, totals, left_all, right_all, blocks = pl.pallas_call(
        place_kernel,
        out_shape=(
            jax.ShapeDtypeStruct((1, 2 * LIST + 1), jnp.int32),
            jax.ShapeDtypeStruct((1, 2), jnp.int32),
            both,
            both,
            pltpu.VMEM((2,) + first.shape, BF16),
        ),
        in_specs=[smem, smem] + [anywhere] * 6,
        out_specs=(smem, smem, vmem, vmem, vmem),
        scratch_shapes=[pltpu.SemaphoreType.DMA((6,))],
        compiler_params=pltpu.CompilerParams(vmem_limit_bytes=2**20),
        name="place",
        cost_estimate=pl.CostEstimate(flops=10**9, bytes_accessed=10**4, transcendentals=0),
    )(words, counts, left_ops, left_other, right_ops, right_other, first, second)
    left_all, right_all, blocks = (
        pltpu.with_memory_space_constraint(x, pltpu.VMEM) for x in (left_all, right_all, blocks)
    )
    acc_shape = (own_blocks + 1, left_width, right_width)
    begun = pl.pallas_call(
        early_kernel,
        out_shape=jax.ShapeDtypeStruct(acc_shape, F32),
        in_specs=[smem, smem] + [vmem] * 3,
        out_specs=vmem,
        compiler_params=pltpu.CompilerParams(vmem_limit_bytes=2 * 2**20),
        name="early",
        cost_estimate=pl.CostEstimate(flops=8 * 10**9, bytes_accessed=10**6, transcendentals=0),
    )(lists, totals, left_all, right_all, blocks)
    devices = groups * holders
    row_sums = jax.ShapeDtypeStruct((devices, 128), F32)
    outgoing, partial = pl.pallas_call(
        late_kernel,
        out_shape=(
            jax.ShapeDtypeStruct((groups, own_blocks * share, right_width), BF16),
            jax.ShapeDtypeStruct(acc_shape, F32),
        ),
        in_specs=[smem, smem] + [vmem] * 2 + [anywhere] * 2 + [vmem],
        out_specs=(vmem, vmem),
        scratch_shapes=[
            pltpu.VMEM((2,) + first.shape, BF16),
            pltpu.SemaphoreType.DMA((2,)),
        ],
        compiler_params=pltpu.CompilerParams(vmem_limit_bytes=8 * 2**20),
        name="late",
        cost_estimate=pl.CostEstimate(flops=5 * 10**9, bytes_accessed=10**6, transcendentals=0),
    )(lists, totals, left_all, right_all, first_new, second_new, begun)
    first_sums = pl.pallas_call(
        functools.partial(energy_kernel, groups),
        out_shape=jax.ShapeDtypeStruct((8, 128), F32),
        in_specs=[vmem, vmem],
        out_specs=vmem,
        compiler_params=pltpu.CompilerParams(vmem_limit_bytes=4 * 2**20),
        name="energy",
        cost_estimate=pl.CostEstimate(flops=10**9, bytes_accessed=10**6, transcendentals=0),
    )(partial, wavefunction)
    arrived = lax.all_to_all(outgoing, "ops", 0, 0)
    for axis, size, masks in (
        ("ops", groups, (1,)),
        ("ops", groups, (2, 6, 4)),
        ("blk", holders, (1, 3, 2)),
        ("blk", holders, (4, 12, 8)),
    ):
        parts = [
            lax.ppermute(first_sums, axis, [(i, i ^ mask) for i in range(size)]) for mask in masks
        ]
        first_sums = first_sums + parts[0]
        if len(parts) > 1:
            first_sums = first_sums + (parts[1] + parts[2])
    shard = jax.ShapeDtypeStruct((own_blocks, share, right_width), F32)
    sigma_vector, scaled, second_sums = pl.pallas_call(
        combine_kernel,
        out_shape=(shard, shard, row_sums),
        in_specs=[smem, smem, smem, vmem, vmem, vmem, vmem],
        out_specs=(vmem, vmem, vmem),
        compiler_params=pltpu.CompilerParams(vmem_limit_bytes=4 * 2**20),
        name="combine",
    )(rank, left_dims, right_dims, arrived, first_sums, wavefunction, h_diagonal)
    second_sums = lax.all_to_all(second_sums, ("ops", "blk"), 0, 0, tiled=True)
    correction = pl.pallas_call(
        functools.partial(finish_kernel, left_dims.shape[0] * left_width * right_width),
        out_shape=shard,
        in_specs=[smem, vmem, vmem, vmem, vmem],
        out_specs=vmem,
        compiler_params=pltpu.CompilerParams(vmem_limit_bytes=4 * 2**20),
        name="finish",
    )(rank, second_sums, first_sums, scaled, wavefunction)
    return (sigma_vector, correction)


def solution(mesh):
    in_specs = (
        P("blk", None, None),
        P(),
        P(),
        P("ops", "blk", None, None),
        P("ops", "blk", None, None),
        P("ops", "blk"),
        P("ops", "blk"),
        P("ops", "blk"),
        P("ops", "blk"),
        P("ops", "blk"),
        P("blk", "ops", None),
    )
    out_specs = (P("blk", "ops", None), P("blk", "ops", None))
    return jax.shard_map(body, mesh=mesh, in_specs=in_specs, out_specs=out_specs, check_vma=False)
```

```python
import functools

import jax
import jax.numpy as jnp
from jax import lax
from jax.experimental import pallas as pl
from jax.experimental.pallas import tpu as pltpu
from jax.sharding import PartitionSpec as P

UNROLL = 16
TAIL = 4
LIST = 272
SPARE = 4
LEFT, RIGHT, TARGET, KIND = 4, 9, 14, 17
MASKS = (((1, 3), (3, 1), (4, 12), (12, 4)), ((4, 12), (12, 4), (1, 3), (3, 1)))
F32 = jnp.float32
BF16 = jnp.bfloat16


def pick_kernel(own, first, second, sems):
    core = lax.rem(lax.axis_index("ops"), 2)
    copies = [
        pltpu.make_async_copy(own.at[pl.ds(2 * core + i, 1)], target, sems.at[i])
        for i, target in enumerate((first, second))
    ]
    for copy in copies:
        copy.start()
    for copy in copies:
        copy.wait()


def place_kernel(source, target, left, right, count, other, other_count, lists, totals, codes):
    core = lax.rem(lax.axis_index("ops"), 2)
    holder = lax.axis_index("blk")

    def code(bits):
        gray = bits ^ (bits >> 1)
        return jnp.where(core == 0, gray, ((gray & 1) << 1) | (gray >> 1))

    def fill(block, carry):
        away, within = (block // 4) ^ holder, lax.rem(block, 4)
        along_x, along_z = code(away & 3), code(away >> 2)
        stream = within & 1
        entry = jnp.where(stream == 0, along_x | (along_z << 2), along_z | (along_x << 2))
        kind = jnp.where(entry < 4, 0, jnp.where(entry < 12, 1, 2))
        slab = jnp.where(kind == 1, 2 * stream + (entry >> 3), stream)
        kind = jnp.where(within >> 1 == core, kind, 3)
        codes[0, block] = (entry & 3) | (slab << 2) | (kind << KIND)
        return carry

    lax.fori_loop(0, codes.shape[1], fill, 0)
    tables = (
        (lambda k: source[0, k], lambda k: target[0, k], lambda k: left[0, k], lambda k: right[0, k]),
        tuple((lambda k, i=i: other[0, i, k]) for i in range(4)),
    )
    for group, live in enumerate((count[0, 0], other_count[0, 0])):
        read_source, read_target, read_left, read_right = tables[group]

        def place(k, filled, group=group):
            word = codes[0, read_source(k)]
            kind = word >> KIND
            word |= (read_left(k) << LEFT) | (read_right(k) << RIGHT) | (read_target(k) << TARGET)
            where = jnp.int32(6 * LIST)
            for i, length in enumerate(filled):
                where = jnp.where(kind == i, (2 * i + group) * LIST + length, where)
            lists[0, where] = word
            return tuple(n + jnp.where(kind == i, 1, 0) for i, n in enumerate(filled))

        def places(i, filled, place=place):
            for u in range(4):
                filled = place(4 * i + u, filled)
            return filled

        none = (jnp.int32(0),) * 3
        quads = live // 4
        filled = lax.fori_loop(0, quads, places, none)
        filled = lax.fori_loop(4 * quads, live, place, filled)
        for i, length in enumerate(filled):
            for u in range(UNROLL):
                lists[0, (2 * i + group) * LIST + length + u] = SPARE << TARGET
            totals[0, 2 * i + group] = length


def run_slots(lists, totals, which, lefts, rights, blocks, acc):
    for group in range(2):
        lstore, rstore = lefts[group], rights[group]

        def many(i, carry, width, offset, lstore=lstore, rstore=rstore):
            for u in range(width):
                word = lists[0, offset + i * width + u]
                psi = blocks[(word >> 2) & 3, word & 3]
                product = jnp.dot(
                    lstore[0, (word >> LEFT) & 31], psi, preferred_element_type=F32
                ).astype(BF16)
                acc[(word >> TARGET) & 7] += lax.dot_general(
                    product, rstore[0, (word >> RIGHT) & 31], (((1,), (1,)), ((), ())),
                    preferred_element_type=F32,
                )
            return carry

        live, base = totals[0, 2 * which + group], (2 * which + group) * LIST
        turns = (live + UNROLL - 1 - 2 * TAIL) // UNROLL
        lax.fori_loop(0, turns, functools.partial(many, width=UNROLL, offset=base), 0)
        rest = jnp.maximum(live - turns * UNROLL, 0)
        lax.fori_loop(
            0,
            (rest + TAIL - 1) // TAIL,
            functools.partial(many, width=TAIL, offset=base + turns * UNROLL),
            0,
        )


def slots_kernel(which, slabs, lists, totals, left0, left1, right0, right1, *rest):
    gathered, rest = rest[:slabs], rest[slabs:]
    if which:
        begun, rest = rest[0], rest[1:]
    acc, rest = rest[0], rest[1:]
    if which == 2:
        out, rest = rest[0], rest[1:]
    blocks, sems = rest
    copies = [
        pltpu.make_async_copy(piece, blocks.at[i], sems.at[i]) for i, piece in enumerate(gathered)
    ]
    for copy in copies:
        copy.start()
    acc[...] = begun[...] if which else jnp.zeros_like(acc)
    for copy in copies:
        copy.wait()
    run_slots(lists, totals, which, (left0, left1), (right0, right1), blocks, acc)
    if which == 2:
        groups, rows = out.shape[0], out.shape[1]
        share = rows // SPARE
        for b in range(SPARE):
            for g in range(groups):
                out[g, b * share:(b + 1) * share, :] = acc[b, g * share:(g + 1) * share].astype(BF16)


def energy_kernel(groups, acc, own, sums):
    energy = jnp.zeros((1, 1), F32)
    norm = jnp.zeros((1, 1), F32)
    for b in range(SPARE):
        wide = own[b].astype(F32)
        energy += jnp.sum(acc[b] * wide, keepdims=True)
        norm += jnp.sum(wide * wide, keepdims=True)
    row = lax.broadcasted_iota(jnp.int32, sums.shape, 0)
    sums[...] = jnp.where(row == 0, energy, jnp.where(row == 1, norm / groups, 0.0))


def combine_kernel(left_dims, right_dims, arrived, totals, own, diagonal, sigma, scaled, sums):
    group_rank, holder = lax.axis_index("ops"), lax.axis_index("blk")
    groups = arrived.shape[0]
    blocks, share, width = sigma.shape
    rayleigh = totals[0:1, 0:1] / totals[1:2, 0:1]
    row = lax.broadcasted_iota(jnp.int32, (share, width), 0) + group_rank * share
    column = lax.broadcasted_iota(jnp.int32, (share, width), 1)
    start = pl.multiple_of(lax.axis_index("ops") * share, share)
    along = jnp.zeros((1, 1), F32)
    square = jnp.zeros((1, 1), F32)
    for b in range(blocks):
        total = arrived[0, b * share:(b + 1) * share, :].astype(F32)
        for g in range(1, groups):
            total += arrived[g, b * share:(b + 1) * share, :].astype(F32)
        ident = holder * blocks + b
        inside = (row < left_dims[ident]) & (column < right_dims[ident])
        total = jnp.where(inside, total, 0.0)
        sigma[b] = total
        state = own[b, pl.ds(start, share), :].astype(F32)
        value = (total - rayleigh * state) / jnp.maximum(jnp.abs(diagonal[b] - rayleigh), 1.0)
        scaled[b] = value
        along += jnp.sum(state * value, keepdims=True)
        square += jnp.sum(value * value, keepdims=True)
    lane = lax.broadcasted_iota(jnp.int32, sums.shape, 1)
    sums[...] = jnp.where(lane == 0, along, jnp.where(lane == 1, square, 0.0))


def finish_kernel(slots_total, arrived, totals, scaled, own, correction):
    blocks, share, width = scaled.shape
    sums = jnp.sum(arrived[...], axis=0, keepdims=True)
    along, square = sums[0:1, 0:1], sums[0:1, 1:2]
    ratio = along / totals[1:2, 0:1]
    length_sq = jnp.maximum(square - along * ratio, 0.0)
    factor = jnp.sqrt(length_sq / slots_total + 1e-06)
    start = pl.multiple_of(lax.axis_index("ops") * share, share)
    for b in range(blocks):
        state = own[b, pl.ds(start, share), :].astype(F32)
        correction[b] = (scaled[b] - ratio * state) / factor


def body(
    wavefunction,
    left_dims,
    right_dims,
    left_ops,
    right_ops,
    source_block,
    target_slot,
    left_index,
    right_index,
    pair_count,
    h_diagonal,
):
    groups = lax.axis_size("ops")
    holders = lax.axis_size("blk")
    own_blocks, left_width, right_width = wavefunction.shape
    share = left_width // groups
    smem = pl.BlockSpec(memory_space=pltpu.SMEM)
    vmem = pl.BlockSpec(memory_space=pltpu.VMEM)
    anywhere = pl.BlockSpec(memory_space=pl.ANY)

    def in_vmem(x):
        return pltpu.with_memory_space_constraint(x, pltpu.VMEM)

    pairs = [(i, i ^ 1) for i in range(groups)]
    left_other = lax.ppermute(left_ops, "ops", pairs)
    right_other = lax.ppermute(right_ops, "ops", pairs)
    tables_other = lax.ppermute(
        jnp.stack([source_block, target_slot, left_index, right_index], axis=1), "ops", pairs
    )
    count_other = lax.ppermute(pair_count, "ops", pairs)

    def exchange(x, *masks):
        partner = [0, 0]
        for mask in masks:
            partner = [partner[core] ^ mask[core] for core in range(2)]
        return lax.ppermute(
            x,
            ("ops", "blk"),
            [
                (g * holders + h, g * holders + (h ^ partner[g % 2]))
                for g in range(groups)
                for h in range(holders)
            ],
        )

    block = jax.ShapeDtypeStruct((1, left_width, right_width), BF16)
    streams = pl.pallas_call(
        pick_kernel,
        out_shape=(block, block),
        in_specs=[anywhere],
        out_specs=(vmem, vmem),
        scratch_shapes=[pltpu.SemaphoreType.DMA((2,))],
        compiler_params=pltpu.CompilerParams(vmem_limit_bytes=2**20),
        name="pick",
    )(wavefunction)
    near = [
        [exchange(x, one), exchange(x, two), exchange(x, one, two)]
        for x, (one, two, _, _) in zip(streams, MASKS)
    ]
    near = [jnp.concatenate([x] + parts) for x, parts in zip(streams, near)]
    third = [exchange(x, masks[2]) for x, masks in zip(near, MASKS)]
    fourth = [exchange(x, masks[3]) for x, masks in zip(near, MASKS)]
    last = [exchange(x, masks[3]) for x, masks in zip(third, MASKS)]

    lists, totals = pl.pallas_call(
        place_kernel,
        out_shape=(
            jax.ShapeDtypeStruct((1, 6 * LIST + 1), jnp.int32),
            jax.ShapeDtypeStruct((1, 6), jnp.int32),
        ),
        in_specs=[smem] * 7,
        out_specs=(smem, smem),
        scratch_shapes=[pltpu.SMEM((1, left_dims.shape[0]), jnp.int32)],
        compiler_params=pltpu.CompilerParams(vmem_limit_bytes=2**20),
        name="place",
        cost_estimate=pl.CostEstimate(flops=10**9, bytes_accessed=10**4, transcendentals=0),
    )(source_block, target_slot, left_index, right_index, pair_count, tables_other, count_other)

    stores = [in_vmem(x) for x in (left_ops, left_other, right_ops, right_other)]
    partial_shape = jax.ShapeDtypeStruct((own_blocks + 1, left_width, right_width), F32)
    outgoing_shape = jax.ShapeDtypeStruct((groups, own_blocks * share, right_width), BF16)

    def slots_call(which, gathered, begun, flops):
        outs = (partial_shape,) if which < 2 else (partial_shape, outgoing_shape)
        return pl.pallas_call(
            functools.partial(slots_kernel, which, len(gathered)),
            out_shape=outs,
            in_specs=[smem, smem] + [vmem] * 4 + [anywhere] * len(gathered) + [vmem] * len(begun),
            out_specs=(vmem,) * len(outs),
            scratch_shapes=[
                pltpu.VMEM((len(gathered),) + gathered[0].shape, BF16),
                pltpu.SemaphoreType.DMA((len(gathered),)),
            ],
            compiler_params=pltpu.CompilerParams(vmem_limit_bytes=6 * 2**20),
            name=("near", "middle", "last")[which],
            cost_estimate=pl.CostEstimate(flops=flops, bytes_accessed=10**6, transcendentals=0),
        )(lists, totals, *stores, *gathered, *begun)

    begun = slots_call(0, near, (), 5 * 10**9)
    begun = slots_call(1, [third[0], fourth[0], third[1], fourth[1]], begun, 4 * 10**9)
    partial, outgoing = slots_call(2, last, begun, 2 * 10**9)
    devices = groups * holders
    row_sums = jax.ShapeDtypeStruct((devices, 128), F32)
    first_sums = pl.pallas_call(
        functools.partial(energy_kernel, groups),
        out_shape=jax.ShapeDtypeStruct((8, 128), F32),
        in_specs=[vmem, vmem],
        out_specs=vmem,
        compiler_params=pltpu.CompilerParams(vmem_limit_bytes=4 * 2**20),
        name="energy",
        cost_estimate=pl.CostEstimate(flops=10**9, bytes_accessed=10**6, transcendentals=0),
    )(partial, wavefunction)
    arrived = lax.all_to_all(outgoing, "ops", 0, 0)
    for axis, size, masks in (
        ("ops", groups, (1,)),
        ("ops", groups, (2, 6, 4)),
        ("blk", holders, (1, 3, 2)),
        ("blk", holders, (4, 12, 8)),
    ):
        parts = [
            lax.ppermute(first_sums, axis, [(i, i ^ mask) for i in range(size)]) for mask in masks
        ]
        first_sums = first_sums + parts[0]
        if len(parts) > 1:
            first_sums = first_sums + (parts[1] + parts[2])
    shard = jax.ShapeDtypeStruct((own_blocks, share, right_width), F32)
    sigma_vector, scaled, second_sums = pl.pallas_call(
        combine_kernel,
        out_shape=(shard, shard, row_sums),
        in_specs=[smem, smem, vmem, vmem, vmem, vmem],
        out_specs=(vmem, vmem, vmem),
        compiler_params=pltpu.CompilerParams(vmem_limit_bytes=4 * 2**20),
        name="combine",
    )(left_dims, right_dims, arrived, first_sums, wavefunction, h_diagonal)
    second_sums = lax.all_to_all(second_sums, ("ops", "blk"), 0, 0, tiled=True)
    correction = pl.pallas_call(
        functools.partial(finish_kernel, left_dims.shape[0] * left_width * right_width),
        out_shape=shard,
        in_specs=[vmem, vmem, vmem, vmem],
        out_specs=vmem,
        compiler_params=pltpu.CompilerParams(vmem_limit_bytes=4 * 2**20),
        name="finish",
    )(second_sums, first_sums, scaled, wavefunction)
    return (sigma_vector, correction)


def solution(mesh):
    in_specs = (
        P("blk", None, None),
        P(),
        P(),
        P("ops", "blk", None, None),
        P("ops", "blk", None, None),
        P("ops", "blk"),
        P("ops", "blk"),
        P("ops", "blk"),
        P("ops", "blk"),
        P("ops", "blk"),
        P("blk", "ops", None),
    )
    out_specs = (P("blk", "ops", None), P("blk", "ops", None))
    return jax.shard_map(body, mesh=mesh, in_specs=in_specs, out_specs=out_specs, check_vma=False)
```

```python
import functools

import jax
import jax.numpy as jnp
from jax import lax
from jax.experimental import pallas as pl
from jax.experimental.pallas import tpu as pltpu
from jax.sharding import PartitionSpec as P

UNROLL = 16
TAIL = 4
LIST = 272
SPARE = 4
LEFT, RIGHT, TARGET, KIND = 4, 9, 14, 17
MASKS = (((1, 3), (3, 1), (4, 12), (12, 4)), ((4, 12), (12, 4), (1, 3), (3, 1)))
F32 = jnp.float32
BF16 = jnp.bfloat16


def run_copies(copies):
    for copy in copies:
        copy.start()
    for copy in copies:
        copy.wait()


def pick_kernel(own, first, second, sems):
    core = lax.rem(lax.axis_index("ops"), 2)
    run_copies([
        pltpu.make_async_copy(own.at[pl.ds(2 * core + i, 1)], target, sems.at[i])
        for i, target in enumerate((first, second))
    ])


def place_kernel(tables, other, lists, totals, words, scalars, sems):
    core = lax.rem(lax.axis_index("ops"), 2)
    holder = lax.axis_index("blk")

    def code(bits):
        gray = bits ^ (bits >> 1)
        return jnp.where(core == 0, gray, ((gray & 1) << 1) | (gray >> 1))

    lives = []
    for group, table in enumerate((tables, other)):
        block = table[0, 0:1, :]
        away, within = (block >> 2) ^ holder, block & 3
        along_x, along_z = code(away & 3), code(away >> 2)
        stream = within & 1
        entry = jnp.where(stream == 0, along_x | (along_z << 2), along_z | (along_x << 2))
        kind = jnp.where((within >> 1) == core, entry >> 3, 2)
        words[group] = (
            (entry & 7)
            | (stream << 3)
            | (table[0, 2:3, :] << LEFT)
            | (table[0, 3:4, :] << RIGHT)
            | (table[0, 1:2, :] << TARGET)
            | (kind << KIND)
        )
        lives.append(jnp.sum(jnp.where(table[0, 1:2, :] < SPARE, 1, 0)))
    run_copies([pltpu.make_async_copy(words, scalars, sems.at[0])])
    for group in range(2):
        first, second = group * LIST, (2 + group) * LIST

        def place(k, filled, group=group, first=first, second=second):
            early, late = filled
            word = scalars[group, 0, k]
            kind = word >> KIND
            lists[0, jnp.where(kind == 0, first + early, jnp.where(kind == 1, second + late, 4 * LIST))] = word
            return early + jnp.where(kind == 0, 1, 0), late + jnp.where(kind == 1, 1, 0)

        def places(i, filled, place=place):
            for u in range(8):
                filled = place(8 * i + u, filled)
            return filled

        turns = lives[group] // 8
        filled = lax.fori_loop(0, turns, places, (jnp.int32(0), jnp.int32(0)))
        early, late = lax.fori_loop(8 * turns, lives[group], place, filled)
        for u in range(UNROLL):
            lists[0, first + early + u] = SPARE << TARGET
            lists[0, second + late + u] = SPARE << TARGET
        totals[0, group] = early
        totals[0, 2 + group] = late


def run_slots(lists, totals, which, lefts, rights, blocks, acc):
    for group in range(2):
        lstore, rstore = lefts[group], rights[group]

        def many(i, carry, width, offset, lstore=lstore, rstore=rstore):
            for u in range(width):
                word = lists[0, offset + i * width + u]
                psi = blocks[(word >> 3) & 1, word & 7]
                product = jnp.dot(
                    lstore[0, (word >> LEFT) & 31], psi, preferred_element_type=F32
                ).astype(BF16)
                acc[(word >> TARGET) & 7] += lax.dot_general(
                    product, rstore[0, (word >> RIGHT) & 31], (((1,), (1,)), ((), ())),
                    preferred_element_type=F32,
                )
            return carry

        live, base = totals[0, 2 * which + group], (2 * which + group) * LIST
        turns = (live + UNROLL - 1 - 2 * TAIL) // UNROLL
        lax.fori_loop(0, turns, functools.partial(many, width=UNROLL, offset=base), 0)
        rest = jnp.maximum(live - turns * UNROLL, 0)
        lax.fori_loop(
            0,
            (rest + TAIL - 1) // TAIL,
            functools.partial(many, width=TAIL, offset=base + turns * UNROLL),
            0,
        )


def early_kernel(lists, totals, left0, left1, right0, right1, first, second, acc, blocks, sems):
    run_copies([
        pltpu.make_async_copy(piece, blocks.at[i], sems.at[i])
        for i, piece in enumerate((first, second))
    ])
    acc[...] = jnp.zeros_like(acc)
    run_slots(lists, totals, 0, (left0, left1), (right0, right1), blocks, acc)


def late_kernel(
    groups, lists, totals, left0, left1, right0, right1, first, second, begun, own,
    keep, give, sums, acc, blocks, sems,
):
    run_copies([
        pltpu.make_async_copy(piece, blocks.at[i], sems.at[i])
        for i, piece in enumerate((first, second))
    ])
    acc[...] = begun[...]
    run_slots(lists, totals, 1, (left0, left1), (right0, right1), blocks, acc)
    core = lax.rem(lax.axis_index("ops"), 2)
    chips, _, share, _ = keep.shape
    energy = jnp.zeros((1, 1), F32)
    norm = jnp.zeros((1, 1), F32)
    for b in range(SPARE):
        wide = own[b].astype(F32)
        energy += jnp.sum(acc[b] * wide, keepdims=True)
        norm += jnp.sum(wide * wide, keepdims=True)
        for y in range(chips):
            for out, place in ((keep, core), (give, 1 - core)):
                start = pl.multiple_of((2 * y + place) * share, share)
                out[y, b] = acc[b, pl.ds(start, share), :]
    lane = lax.broadcasted_iota(jnp.int32, sums.shape, 1)
    sums[...] = jnp.where(lane == 0, energy, jnp.where(lane == 1, norm / groups, 0.0))


def chip_kernel(masks, keep, got, mine, *outs):
    chip = lax.axis_index("ops") // 2
    for mask, out in zip((0,) + masks, (mine,) + outs):
        for b in range(out.shape[0]):
            out[b] = keep[chip ^ mask, b] + got[chip ^ mask, b]


def combine_kernel(
    left_dims, right_dims, mine, near, far, across, totals, own, diagonal, sigma, scaled, sums
):
    group_rank, holder = lax.axis_index("ops"), lax.axis_index("blk")
    blocks, share, width = sigma.shape
    whole = jnp.sum(totals[...], axis=0, keepdims=True)
    rayleigh = whole[0:1, 0:1] / whole[0:1, 1:2]
    row = lax.broadcasted_iota(jnp.int32, (share, width), 0) + group_rank * share
    column = lax.broadcasted_iota(jnp.int32, (share, width), 1)
    start = pl.multiple_of(group_rank * share, share)
    along = jnp.zeros((1, 1), F32)
    square = jnp.zeros((1, 1), F32)
    for b in range(blocks):
        ident = holder * blocks + b
        inside = (row < left_dims[ident]) & (column < right_dims[ident])
        total = jnp.where(inside, (mine[b] + near[b]) + (far[b] + across[b]), 0.0)
        sigma[b] = total
        state = own[b, pl.ds(start, share), :].astype(F32)
        value = (total - rayleigh * state) / jnp.maximum(jnp.abs(diagonal[b] - rayleigh), 1.0)
        scaled[b] = value
        along += jnp.sum(state * value, keepdims=True)
        square += jnp.sum(value * value, keepdims=True)
    lane = lax.broadcasted_iota(jnp.int32, sums.shape, 1)
    sums[...] = jnp.where(lane == 0, along, jnp.where(lane == 1, square, 0.0))


def finish_kernel(slots_total, arrived, totals, scaled, own, correction):
    blocks, share, width = scaled.shape
    sums = jnp.sum(arrived[...], axis=0, keepdims=True)
    along, square = sums[0:1, 0:1], sums[0:1, 1:2]
    ratio = along / jnp.sum(totals[...], axis=0, keepdims=True)[0:1, 1:2]
    length_sq = jnp.maximum(square - along * ratio, 0.0)
    factor = jnp.sqrt(length_sq / slots_total + 1e-06)
    start = pl.multiple_of(lax.axis_index("ops") * share, share)
    for b in range(blocks):
        state = own[b, pl.ds(start, share), :].astype(F32)
        correction[b] = (scaled[b] - ratio * state) / factor


def body(
    wavefunction,
    left_dims,
    right_dims,
    left_ops,
    right_ops,
    source_block,
    target_slot,
    left_index,
    right_index,
    pair_count,
    h_diagonal,
):
    groups = lax.axis_size("ops")
    holders = lax.axis_size("blk")
    own_blocks, left_width, right_width = wavefunction.shape
    share = left_width // groups
    smem = pl.BlockSpec(memory_space=pltpu.SMEM)
    vmem = pl.BlockSpec(memory_space=pltpu.VMEM)
    anywhere = pl.BlockSpec(memory_space=pl.ANY)

    def in_vmem(x):
        return pltpu.with_memory_space_constraint(x, pltpu.VMEM)

    pairs = [(i, i ^ 1) for i in range(groups)]
    left_other = lax.ppermute(left_ops, "ops", pairs)
    right_other = lax.ppermute(right_ops, "ops", pairs)
    alive = lax.broadcasted_iota(jnp.int32, target_slot.shape, 1) < pair_count
    tables = jnp.stack(
        [source_block, jnp.where(alive, target_slot, SPARE), left_index, right_index], axis=1
    )
    tables_other = lax.ppermute(tables, "ops", pairs)

    def exchange(x, mask):
        return lax.ppermute(
            x,
            ("ops", "blk"),
            [
                (g * holders + h, g * holders + (h ^ mask[g % 2]))
                for g in range(groups)
                for h in range(holders)
            ],
        )

    block = jax.ShapeDtypeStruct((1, left_width, right_width), BF16)
    first, second = pl.pallas_call(
        pick_kernel,
        out_shape=(block, block),
        in_specs=[pl.BlockSpec(memory_space=pltpu.HBM)],
        out_specs=(vmem, vmem),
        scratch_shapes=[pltpu.SemaphoreType.DMA((2,))],
        compiler_params=pltpu.CompilerParams(vmem_limit_bytes=2**20),
        name="pick",
    )(wavefunction)
    for step, (one, two) in enumerate(zip(*MASKS)):
        first_new, second_new = exchange(first, one), exchange(second, two)
        if step == 0:
            first_new, tables_other = lax.optimization_barrier((first_new, tables_other))
            lists, totals = pl.pallas_call(
                place_kernel,
                out_shape=(
                    jax.ShapeDtypeStruct((1, 4 * LIST + 1), jnp.int32),
                    jax.ShapeDtypeStruct((1, 4), jnp.int32),
                ),
                in_specs=[vmem, vmem],
                out_specs=(smem, smem),
                scratch_shapes=[
                    pltpu.VMEM((2, 1, tables.shape[2]), jnp.int32),
                    pltpu.SMEM((2, 1, tables.shape[2]), jnp.int32),
                    pltpu.SemaphoreType.DMA((1,)),
                ],
                compiler_params=pltpu.CompilerParams(vmem_limit_bytes=2**20),
                name="place",
                cost_estimate=pl.CostEstimate(
                    flops=10**9, bytes_accessed=10**4, transcendentals=0
                ),
            )(tables, tables_other)
        if step == 2:
            first_new, lists, totals = lax.optimization_barrier((first_new, lists, totals))
        if step < 3:
            first = jnp.concatenate([first, first_new])
            second = jnp.concatenate([second, second_new])

    stores = [in_vmem(x) for x in (left_ops, left_other, right_ops, right_other)]
    partial_shape = (own_blocks + 1, left_width, right_width)
    half_blocks = pltpu.VMEM((2,) + first.shape, BF16)
    begun = pl.pallas_call(
        early_kernel,
        out_shape=jax.ShapeDtypeStruct(partial_shape, F32),
        in_specs=[smem, smem] + [vmem] * 4 + [anywhere] * 2,
        out_specs=vmem,
        scratch_shapes=[half_blocks, pltpu.SemaphoreType.DMA((2,))],
        compiler_params=pltpu.CompilerParams(vmem_limit_bytes=6 * 2**20),
        name="early",
        cost_estimate=pl.CostEstimate(flops=8 * 10**9, bytes_accessed=10**6, transcendentals=0),
    )(lists, totals, *stores, first, second)
    chips = groups // 2
    devices = groups * holders
    row_sums = jax.ShapeDtypeStruct((devices, 128), F32)
    halves = jax.ShapeDtypeStruct((chips, own_blocks, share, right_width), F32)
    keep, give, first_sums = pl.pallas_call(
        functools.partial(late_kernel, groups),
        out_shape=(halves, halves, row_sums),
        in_specs=[smem, smem] + [vmem] * 4 + [anywhere] * 2 + [vmem] * 2,
        out_specs=(vmem,) * 3,
        scratch_shapes=[
            pltpu.VMEM(partial_shape, F32), half_blocks, pltpu.SemaphoreType.DMA((2,)),
        ],
        compiler_params=pltpu.CompilerParams(vmem_limit_bytes=8 * 2**20),
        name="late",
        cost_estimate=pl.CostEstimate(flops=5 * 10**9, bytes_accessed=10**6, transcendentals=0),
    )(lists, totals, *stores, first_new, second_new, begun, wavefunction)
    got = lax.ppermute(give, "ops", pairs)
    chip_masks = (1, 3, 2)
    shard_sum = jax.ShapeDtypeStruct((own_blocks, share, right_width), F32)
    mine, *outgoing = pl.pallas_call(
        functools.partial(chip_kernel, chip_masks),
        out_shape=(shard_sum,) * 4,
        in_specs=[vmem, vmem],
        out_specs=(vmem,) * 4,
        compiler_params=pltpu.CompilerParams(vmem_limit_bytes=4 * 2**20),
        name="chip_sum",
    )(keep, got)
    arrived = [
        lax.ppermute(x, "ops", [(i, i ^ (2 * mask)) for i in range(groups)])
        for x, mask in zip(outgoing, chip_masks)
    ]
    first_sums = lax.all_to_all(first_sums, ("ops", "blk"), 0, 0, tiled=True)
    shard = jax.ShapeDtypeStruct((own_blocks, share, right_width), F32)
    sigma_vector, scaled, second_sums = pl.pallas_call(
        combine_kernel,
        out_shape=(shard, shard, row_sums),
        in_specs=[smem, smem] + [vmem] * 7,
        out_specs=(vmem, vmem, vmem),
        compiler_params=pltpu.CompilerParams(vmem_limit_bytes=4 * 2**20),
        name="combine",
    )(left_dims, right_dims, mine, *arrived, first_sums, wavefunction, h_diagonal)
    second_sums = lax.all_to_all(second_sums, ("ops", "blk"), 0, 0, tiled=True)
    correction = pl.pallas_call(
        functools.partial(finish_kernel, left_dims.shape[0] * left_width * right_width),
        out_shape=shard,
        in_specs=[vmem, vmem, vmem, vmem],
        out_specs=vmem,
        compiler_params=pltpu.CompilerParams(vmem_limit_bytes=4 * 2**20),
        name="finish",
    )(second_sums, first_sums, scaled, wavefunction)
    return (sigma_vector, correction)


def solution(mesh):
    in_specs = (
        P("blk", None, None),
        P(),
        P(),
        P("ops", "blk", None, None),
        P("ops", "blk", None, None),
        P("ops", "blk"),
        P("ops", "blk"),
        P("ops", "blk"),
        P("ops", "blk"),
        P("ops", "blk"),
        P("blk", "ops", None),
    )
    out_specs = (P("blk", "ops", None), P("blk", "ops", None))
    return jax.shard_map(body, mesh=mesh, in_specs=in_specs, out_specs=out_specs, check_vma=False)
```

```python
import functools

import jax
import jax.numpy as jnp
from jax import lax
from jax.experimental import pallas as pl
from jax.experimental.pallas import tpu as pltpu
from jax.sharding import PartitionSpec as P

UNROLL = 16
TAIL = 4
LIST = 272
SPARE = 4
KINDS = 3
NOTE = 8
LEFT, RIGHT, TARGET, KIND = 4, 9, 14, 17
MASKS = (((1, 3), (3, 1), (4, 12), (12, 4)), ((4, 12), (12, 4), (1, 3), (3, 1)))
F32 = jnp.float32
BF16 = jnp.bfloat16


def run_copies(copies):
    for copy in copies:
        copy.start()
    for copy in copies:
        copy.wait()


def pick_kernel(own, first, second, sems):
    core = lax.rem(lax.axis_index("ops"), 2)
    run_copies([
        pltpu.make_async_copy(own.at[pl.ds(2 * core + i, 1)], target, sems.at[i])
        for i, target in enumerate((first, second))
    ])


def place_kernel(tables, other, lists, totals, words, scalars, sems):
    core = lax.rem(lax.axis_index("ops"), 2)
    holder = lax.axis_index("blk")

    def code(bits):
        gray = bits ^ (bits >> 1)
        return jnp.where(core == 0, gray, ((gray & 1) << 1) | (gray >> 1))

    lives = []
    for group, table in enumerate((tables, other)):
        block = table[0, 0:1, :]
        away, within = (block >> 2) ^ holder, block & 3
        along_x, along_z = code(away & 3), code(away >> 2)
        stream = within & 1
        entry = jnp.where(stream == 0, along_x | (along_z << 2), along_z | (along_x << 2))
        kind = jnp.where((within >> 1) == core, jnp.where(entry < 8, 0, 1 + stream), 3)
        words[group] = (
            (entry & 7)
            | (stream << 3)
            | (table[0, 2:3, :] << LEFT)
            | (table[0, 3:4, :] << RIGHT)
            | (table[0, 1:2, :] << TARGET)
            | (kind << KIND)
        )
        lives.append(jnp.sum(jnp.where(table[0, 1:2, :] < SPARE, 1, 0)))
    run_copies([pltpu.make_async_copy(words, scalars, sems.at[0])])
    for group in range(2):

        def place(k, filled, group=group):
            word = scalars[group, 0, k]
            kind = word >> KIND
            where = jnp.int32(2 * KINDS * LIST)
            for i, length in enumerate(filled):
                where = jnp.where(kind == i, (2 * i + group) * LIST + length, where)
            lists[0, where] = word
            return tuple(length + jnp.where(kind == i, 1, 0) for i, length in enumerate(filled))

        def places(i, filled, place=place):
            for u in range(8):
                filled = place(8 * i + u, filled)
            return filled

        turns = lives[group] // 8
        filled = lax.fori_loop(0, turns, places, (jnp.int32(0),) * KINDS)
        filled = lax.fori_loop(8 * turns, lives[group], place, filled)
        for i, length in enumerate(filled):
            for u in range(UNROLL):
                lists[0, (2 * i + group) * LIST + length + u] = SPARE << TARGET
            totals[0, 2 * i + group] = length


def run_slots(lists, totals, which, lefts, rights, blocks, acc):
    for group in range(2):
        lstore, rstore = lefts[group], rights[group]

        def many(i, carry, width, offset, lstore=lstore, rstore=rstore):
            for u in range(width):
                word = lists[0, offset + i * width + u]
                psi = blocks[(word >> 3) & 1, word & 7] if which == 0 else blocks[word & 7]
                product = jnp.dot(
                    lstore[0, (word >> LEFT) & 31], psi, preferred_element_type=F32
                ).astype(BF16)
                acc[(word >> TARGET) & 7] += lax.dot_general(
                    product, rstore[0, (word >> RIGHT) & 31], (((1,), (1,)), ((), ())),
                    preferred_element_type=F32,
                )
            return carry

        live, base = totals[0, 2 * which + group], (2 * which + group) * LIST
        turns = (live + UNROLL - 1 - 2 * TAIL) // UNROLL
        lax.fori_loop(0, turns, functools.partial(many, width=UNROLL, offset=base), 0)
        rest = jnp.maximum(live - turns * UNROLL, 0)
        lax.fori_loop(
            0,
            (rest + TAIL - 1) // TAIL,
            functools.partial(many, width=TAIL, offset=base + turns * UNROLL),
            0,
        )


def early_kernel(lists, totals, left0, left1, right0, right1, first, second, acc, blocks, sems):
    run_copies([
        pltpu.make_async_copy(piece, blocks.at[i], sems.at[i])
        for i, piece in enumerate((first, second))
    ])
    acc[...] = jnp.zeros_like(acc)
    run_slots(lists, totals, 0, (left0, left1), (right0, right1), blocks, acc)


def late_kernel(lists, totals, left0, left1, right0, right1, first, begun, acc):
    acc[...] = begun[...]
    run_slots(lists, totals, 1, (left0, left1), (right0, right1), first, acc)


def last_kernel(
    groups, lists, totals, left0, left1, right0, right1, second, begun, own, keep, give, acc
):
    acc[...] = begun[...]
    run_slots(lists, totals, 2, (left0, left1), (right0, right1), second, acc)
    core = lax.rem(lax.axis_index("ops"), 2)
    chips, width = keep.shape[0], keep.shape[2]
    share = (keep.shape[1] - NOTE) // SPARE
    energy = jnp.zeros((1, 1), F32)
    norm = jnp.zeros((1, 1), F32)
    for b in range(SPARE):
        wide = own[b].astype(F32)
        energy += jnp.sum(acc[b] * wide, keepdims=True)
        norm += jnp.sum(wide * wide, keepdims=True)
        for y in range(chips):
            for out, place in ((keep, core), (give, 1 - core)):
                start = pl.multiple_of((2 * y + place) * share, share)
                out[y, b * share:(b + 1) * share] = acc[b, pl.ds(start, share), :]
    row = lax.broadcasted_iota(jnp.int32, (NOTE, width), 0)
    note = jnp.where(row == 0, energy, jnp.where(row == 1, norm / groups, 0.0))
    for y in range(chips):
        for out in (keep, give):
            out[y, SPARE * share:] = note


def chip_kernel(masks, keep, got, mine, *outs):
    chip = lax.axis_index("ops") // 2
    for mask, out in zip((0,) + masks, (mine,) + outs):
        out[...] = keep[chip ^ mask] + got[chip ^ mask]


def combine_kernel(
    left_dims, right_dims, mine, near, far, across, totals, own, diagonal, sigma, scaled, sums
):
    group_rank, holder = lax.axis_index("ops"), lax.axis_index("blk")
    blocks, share, width = sigma.shape
    rayleigh = totals[0:1, 0:1] / totals[1:2, 0:1]
    row = lax.broadcasted_iota(jnp.int32, (share, width), 0) + group_rank * share
    column = lax.broadcasted_iota(jnp.int32, (share, width), 1)
    start = pl.multiple_of(group_rank * share, share)
    along = jnp.zeros((1, 1), F32)
    square = jnp.zeros((1, 1), F32)
    for b in range(blocks):
        ident = holder * blocks + b
        inside = (row < left_dims[ident]) & (column < right_dims[ident])
        rows = slice(b * share, (b + 1) * share)
        total = (mine[rows] + near[rows]) + (far[rows] + across[rows])
        total = jnp.where(inside, total, 0.0)
        sigma[b] = total
        state = own[b, pl.ds(start, share), :].astype(F32)
        value = (total - rayleigh * state) / jnp.maximum(jnp.abs(diagonal[b] - rayleigh), 1.0)
        scaled[b] = value
        along += jnp.sum(state * value, keepdims=True)
        square += jnp.sum(value * value, keepdims=True)
    lane = lax.broadcasted_iota(jnp.int32, sums.shape, 1)
    sums[...] = jnp.where(lane == 0, along, jnp.where(lane == 1, square, 0.0))


def finish_kernel(slots_total, arrived, totals, scaled, own, correction):
    blocks, share, width = scaled.shape
    sums = jnp.sum(arrived[...], axis=0, keepdims=True)
    along, square = sums[0:1, 0:1], sums[0:1, 1:2]
    ratio = along / totals[1:2, 0:1]
    length_sq = jnp.maximum(square - along * ratio, 0.0)
    factor = jnp.sqrt(length_sq / slots_total + 1e-06)
    start = pl.multiple_of(lax.axis_index("ops") * share, share)
    for b in range(blocks):
        state = own[b, pl.ds(start, share), :].astype(F32)
        correction[b] = (scaled[b] - ratio * state) / factor


def body(
    wavefunction,
    left_dims,
    right_dims,
    left_ops,
    right_ops,
    source_block,
    target_slot,
    left_index,
    right_index,
    pair_count,
    h_diagonal,
):
    groups = lax.axis_size("ops")
    holders = lax.axis_size("blk")
    own_blocks, left_width, right_width = wavefunction.shape
    share = left_width // groups
    smem = pl.BlockSpec(memory_space=pltpu.SMEM)
    vmem = pl.BlockSpec(memory_space=pltpu.VMEM)
    anywhere = pl.BlockSpec(memory_space=pl.ANY)

    def in_vmem(x):
        return pltpu.with_memory_space_constraint(x, pltpu.VMEM)

    pairs = [(i, i ^ 1) for i in range(groups)]
    left_other = lax.ppermute(left_ops, "ops", pairs)
    right_other = lax.ppermute(right_ops, "ops", pairs)
    alive = lax.broadcasted_iota(jnp.int32, target_slot.shape, 1) < pair_count
    tables = jnp.stack(
        [source_block, jnp.where(alive, target_slot, SPARE), left_index, right_index], axis=1
    )
    tables_other = lax.ppermute(tables, "ops", pairs)

    def exchange(x, mask):
        return lax.ppermute(
            x,
            ("ops", "blk"),
            [
                (g * holders + h, g * holders + (h ^ mask[g % 2]))
                for g in range(groups)
                for h in range(holders)
            ],
        )

    block = jax.ShapeDtypeStruct((1, left_width, right_width), BF16)
    first, second = pl.pallas_call(
        pick_kernel,
        out_shape=(block, block),
        in_specs=[pl.BlockSpec(memory_space=pltpu.HBM)],
        out_specs=(vmem, vmem),
        scratch_shapes=[pltpu.SemaphoreType.DMA((2,))],
        compiler_params=pltpu.CompilerParams(vmem_limit_bytes=2**20),
        name="pick",
    )(pltpu.with_memory_space_constraint(wavefunction, pltpu.HBM))
    for step, (one, two) in enumerate(zip(*MASKS)):
        first_new, second_new = exchange(first, one), exchange(second, two)
        if step == 0:
            lists, totals = pl.pallas_call(
                place_kernel,
                out_shape=(
                    jax.ShapeDtypeStruct((1, 2 * KINDS * LIST + 1), jnp.int32),
                    jax.ShapeDtypeStruct((1, 2 * KINDS), jnp.int32),
                ),
                in_specs=[vmem, vmem],
                out_specs=(smem, smem),
                scratch_shapes=[
                    pltpu.VMEM((2, 1, tables.shape[2]), jnp.int32),
                    pltpu.SMEM((2, 1, tables.shape[2]), jnp.int32),
                    pltpu.SemaphoreType.DMA((1,)),
                ],
                compiler_params=pltpu.CompilerParams(vmem_limit_bytes=2**20),
                name="place",
                cost_estimate=pl.CostEstimate(
                    flops=10**9, bytes_accessed=10**4, transcendentals=0
                ),
            )(tables, tables_other)
        if step == 2:
            first_new, lists, totals = lax.optimization_barrier((first_new, lists, totals))
        if step < 3:
            first = jnp.concatenate([first, first_new])
            second = jnp.concatenate([second, second_new])

    stores = [in_vmem(x) for x in (left_ops, left_other, right_ops, right_other)]
    partial_shape = (own_blocks + 1, left_width, right_width)
    half_blocks = pltpu.VMEM((2,) + first.shape, BF16)
    begun = pl.pallas_call(
        early_kernel,
        out_shape=jax.ShapeDtypeStruct(partial_shape, F32),
        in_specs=[smem, smem] + [vmem] * 4 + [anywhere] * 2,
        out_specs=vmem,
        scratch_shapes=[half_blocks, pltpu.SemaphoreType.DMA((2,))],
        compiler_params=pltpu.CompilerParams(vmem_limit_bytes=6 * 2**20),
        name="early",
        cost_estimate=pl.CostEstimate(flops=8 * 10**9, bytes_accessed=10**6, transcendentals=0),
    )(lists, totals, *stores, first, second)
    chips = groups // 2
    begun = pl.pallas_call(
        late_kernel,
        out_shape=jax.ShapeDtypeStruct(partial_shape, F32),
        in_specs=[smem, smem] + [vmem] * 6,
        out_specs=vmem,
        compiler_params=pltpu.CompilerParams(vmem_limit_bytes=6 * 2**20),
        name="late",
        cost_estimate=pl.CostEstimate(flops=2 * 10**9, bytes_accessed=10**6, transcendentals=0),
    )(lists, totals, *stores, first_new, begun)
    halves = jax.ShapeDtypeStruct((chips, own_blocks * share + NOTE, right_width), F32)
    keep, give = pl.pallas_call(
        functools.partial(last_kernel, groups),
        out_shape=(halves, halves),
        in_specs=[smem, smem] + [vmem] * 7,
        out_specs=(vmem, vmem),
        scratch_shapes=[pltpu.VMEM(partial_shape, F32)],
        compiler_params=pltpu.CompilerParams(vmem_limit_bytes=6 * 2**20),
        name="last",
        cost_estimate=pl.CostEstimate(flops=2 * 10**9, bytes_accessed=10**6, transcendentals=0),
    )(lists, totals, *stores, second_new, begun, wavefunction)
    got = lax.ppermute(give, "ops", pairs)
    chip_masks = (1, 3, 2)
    chip_sum = jax.ShapeDtypeStruct(halves.shape[1:], F32)
    mine, *outgoing = pl.pallas_call(
        functools.partial(chip_kernel, chip_masks),
        out_shape=(chip_sum,) * 4,
        in_specs=[vmem, vmem],
        out_specs=(vmem,) * 4,
        compiler_params=pltpu.CompilerParams(vmem_limit_bytes=4 * 2**20),
        name="chip_sum",
    )(keep, got)
    arrived = [
        lax.ppermute(x, "ops", [(i, i ^ (2 * mask)) for i in range(groups)])
        for x, mask in zip(outgoing, chip_masks)
    ]
    notes = [x[own_blocks * share:, :128] for x in (mine, *arrived)]
    first_sums = (notes[0] + notes[1]) + (notes[2] + notes[3])
    for masks in ((1, 3, 2), (4, 12, 8)):
        notes = [first_sums] + [
            lax.ppermute(first_sums, "blk", [(i, i ^ mask) for i in range(holders)])
            for mask in masks
        ]
        first_sums = (notes[0] + notes[1]) + (notes[2] + notes[3])
    devices = groups * holders
    row_sums = jax.ShapeDtypeStruct((devices, 128), F32)
    shard = jax.ShapeDtypeStruct((own_blocks, share, right_width), F32)
    sigma_vector, scaled, second_sums = pl.pallas_call(
        combine_kernel,
        out_shape=(shard, shard, row_sums),
        in_specs=[smem, smem] + [vmem] * 7,
        out_specs=(vmem, vmem, vmem),
        compiler_params=pltpu.CompilerParams(vmem_limit_bytes=4 * 2**20),
        name="combine",
    )(left_dims, right_dims, mine, *arrived, first_sums, wavefunction, h_diagonal)
    second_sums = lax.all_to_all(second_sums, ("ops", "blk"), 0, 0, tiled=True)
    correction = pl.pallas_call(
        functools.partial(finish_kernel, left_dims.shape[0] * left_width * right_width),
        out_shape=shard,
        in_specs=[vmem, vmem, vmem, vmem],
        out_specs=vmem,
        compiler_params=pltpu.CompilerParams(vmem_limit_bytes=4 * 2**20),
        name="finish",
    )(second_sums, first_sums, scaled, wavefunction)
    return (sigma_vector, correction)


def solution(mesh):
    in_specs = (
        P("blk", None, None),
        P(),
        P(),
        P("ops", "blk", None, None),
        P("ops", "blk", None, None),
        P("ops", "blk"),
        P("ops", "blk"),
        P("ops", "blk"),
        P("ops", "blk"),
        P("ops", "blk"),
        P("blk", "ops", None),
    )
    out_specs = (P("blk", "ops", None), P("blk", "ops", None))
    return jax.shard_map(body, mesh=mesh, in_specs=in_specs, out_specs=out_specs, check_vma=False)
```

```python
import functools

import jax
import jax.numpy as jnp
from jax import lax
from jax.experimental import pallas as pl
from jax.experimental.pallas import tpu as pltpu
from jax.sharding import PartitionSpec as P

UNROLL = 16
TAIL = 4
LIST = 272
SPARE = 4
KINDS = 3
NOTE = 8
LEFT, RIGHT, TARGET, KIND = 4, 9, 14, 17
MASKS = (((1, 3), (3, 1), (4, 12), (12, 4)), ((4, 12), (12, 4), (1, 3), (3, 1)))
F32 = jnp.float32
BF16 = jnp.bfloat16


def run_copies(copies):
    for copy in copies:
        copy.start()
    for copy in copies:
        copy.wait()


def pick_kernel(own, first, second, sems):
    core = lax.rem(lax.axis_index("ops"), 2)
    run_copies([
        pltpu.make_async_copy(own.at[pl.ds(2 * core + i, 1)], target, sems.at[i])
        for i, target in enumerate((first, second))
    ])


def place_kernel(tables, other, lists, totals, words, scalars, sems):
    core = lax.rem(lax.axis_index("ops"), 2)
    holder = lax.axis_index("blk")

    def code(bits):
        gray = bits ^ (bits >> 1)
        return jnp.where(core == 0, gray, ((gray & 1) << 1) | (gray >> 1))

    lives = []
    for group, table in enumerate((tables, other)):
        block = table[0, 0:1, :]
        away, within = (block >> 2) ^ holder, block & 3
        along_x, along_z = code(away & 3), code(away >> 2)
        stream = within & 1
        entry = jnp.where(stream == 0, along_x | (along_z << 2), along_z | (along_x << 2))
        kind = jnp.where((within >> 1) == core, jnp.where(entry < 8, 0, 1 + stream), 3)
        words[group] = (
            (entry & 7)
            | (stream << 3)
            | (table[0, 2:3, :] << LEFT)
            | (table[0, 3:4, :] << RIGHT)
            | (table[0, 1:2, :] << TARGET)
            | (kind << KIND)
        )
        lives.append(jnp.sum(jnp.where(table[0, 1:2, :] < SPARE, 1, 0)))
    run_copies([pltpu.make_async_copy(words, scalars, sems.at[0])])
    for group in range(2):

        def place(k, filled, group=group):
            word = scalars[group, 0, k]
            kind = word >> KIND
            where = jnp.int32(2 * KINDS * LIST)
            for i, length in enumerate(filled):
                where = jnp.where(kind == i, (2 * i + group) * LIST + length, where)
            lists[0, where] = word
            return tuple(length + jnp.where(kind == i, 1, 0) for i, length in enumerate(filled))

        def places(i, filled, place=place):
            for u in range(8):
                filled = place(8 * i + u, filled)
            return filled

        turns = lives[group] // 8
        filled = lax.fori_loop(0, turns, places, (jnp.int32(0),) * KINDS)
        filled = lax.fori_loop(8 * turns, lives[group], place, filled)
        for i, length in enumerate(filled):
            for u in range(UNROLL):
                lists[0, (2 * i + group) * LIST + length + u] = SPARE << TARGET
            totals[0, 2 * i + group] = length


def run_slots(lists, totals, which, lefts, rights, blocks, acc):
    for group in range(2):
        lstore, rstore = lefts[group], rights[group]

        def many(i, carry, width, offset, lstore=lstore, rstore=rstore):
            for u in range(width):
                word = lists[0, offset + i * width + u]
                psi = blocks[(word >> 3) & 1, word & 7] if which == 0 else blocks[word & 7]
                product = jnp.dot(
                    lstore[0, (word >> LEFT) & 31], psi, preferred_element_type=F32
                ).astype(BF16)
                acc[(word >> TARGET) & 7] += lax.dot_general(
                    product, rstore[0, (word >> RIGHT) & 31], (((1,), (1,)), ((), ())),
                    preferred_element_type=F32,
                )
            return carry

        live, base = totals[0, 2 * which + group], (2 * which + group) * LIST
        turns = (live + UNROLL - 1 - 2 * TAIL) // UNROLL
        lax.fori_loop(0, turns, functools.partial(many, width=UNROLL, offset=base), 0)
        rest = jnp.maximum(live - turns * UNROLL, 0)
        lax.fori_loop(
            0,
            (rest + TAIL - 1) // TAIL,
            functools.partial(many, width=TAIL, offset=base + turns * UNROLL),
            0,
        )


def early_kernel(lists, totals, left0, left1, right0, right1, first, second, acc, blocks, sems):
    run_copies([
        pltpu.make_async_copy(piece, blocks.at[i], sems.at[i])
        for i, piece in enumerate((first, second))
    ])
    acc[...] = jnp.zeros_like(acc)
    run_slots(lists, totals, 0, (left0, left1), (right0, right1), blocks, acc)


def late_kernel(lists, totals, left0, left1, right0, right1, first, begun, acc):
    acc[...] = begun[...]
    run_slots(lists, totals, 1, (left0, left1), (right0, right1), first, acc)


def last_kernel(
    groups, lists, totals, left0, left1, right0, right1, second, begun, own, keep, give, acc
):
    acc[...] = begun[...]
    run_slots(lists, totals, 2, (left0, left1), (right0, right1), second, acc)
    core = lax.rem(lax.axis_index("ops"), 2)
    chips, width = keep.shape[0], keep.shape[2]
    share = (keep.shape[1] - NOTE) // SPARE
    energy = jnp.zeros((1, 1), F32)
    norm = jnp.zeros((1, 1), F32)
    for b in range(SPARE):
        wide = own[b].astype(F32)
        energy += jnp.sum(acc[b] * wide, keepdims=True)
        norm += jnp.sum(wide * wide, keepdims=True)
        for y in range(chips):
            for out, place in ((keep, core), (give, 1 - core)):
                start = pl.multiple_of((2 * y + place) * share, share)
                out[y, b * share:(b + 1) * share] = acc[b, pl.ds(start, share), :]
    lane = lax.broadcasted_iota(jnp.int32, (NOTE, width), 1)
    note = jnp.where(lane == 0, energy, jnp.where(lane == 1, norm / groups, 0.0))
    for y in range(chips):
        for out in (keep, give):
            out[y, SPARE * share:] = note


def chip_kernel(masks, keep, got, note, mine, *outs):
    chip = lax.axis_index("ops") // 2
    rows = mine.shape[0]
    total = keep[0, rows:, :128] + got[0, rows:, :128]
    for i in range(note.shape[0] // NOTE):
        note[i * NOTE:(i + 1) * NOTE] = total
    for mask, out in zip((0,) + masks, (mine,) + outs):
        out[...] = keep[chip ^ mask, :rows] + got[chip ^ mask, :rows]


def combine_kernel(
    left_dims, right_dims, mine, near, far, across, totals, own, diagonal, sigma, scaled, sums
):
    group_rank, holder = lax.axis_index("ops"), lax.axis_index("blk")
    blocks, share, width = sigma.shape
    whole = jnp.sum(totals[...], axis=0, keepdims=True)
    rayleigh = whole[0:1, 0:1] / whole[0:1, 1:2]
    row = lax.broadcasted_iota(jnp.int32, (share, width), 0) + group_rank * share
    column = lax.broadcasted_iota(jnp.int32, (share, width), 1)
    start = pl.multiple_of(group_rank * share, share)
    along = jnp.zeros((1, 1), F32)
    square = jnp.zeros((1, 1), F32)
    for b in range(blocks):
        ident = holder * blocks + b
        inside = (row < left_dims[ident]) & (column < right_dims[ident])
        rows = slice(b * share, (b + 1) * share)
        total = (mine[rows] + near[rows]) + (far[rows] + across[rows])
        total = jnp.where(inside, total, 0.0)
        sigma[b] = total
        state = own[b, pl.ds(start, share), :].astype(F32)
        value = (total - rayleigh * state) / jnp.maximum(jnp.abs(diagonal[b] - rayleigh), 1.0)
        scaled[b] = value
        along += jnp.sum(state * value, keepdims=True)
        square += jnp.sum(value * value, keepdims=True)
    lane = lax.broadcasted_iota(jnp.int32, sums.shape, 1)
    sums[...] = jnp.where(lane == 0, along, jnp.where(lane == 1, square, 0.0))


def finish_kernel(slots_total, arrived, totals, scaled, own, correction):
    blocks, share, width = scaled.shape
    sums = jnp.sum(arrived[...], axis=0, keepdims=True)
    along, square = sums[0:1, 0:1], sums[0:1, 1:2]
    ratio = along / jnp.sum(totals[...], axis=0, keepdims=True)[0:1, 1:2]
    length_sq = jnp.maximum(square - along * ratio, 0.0)
    factor = jnp.sqrt(length_sq / slots_total + 1e-06)
    start = pl.multiple_of(lax.axis_index("ops") * share, share)
    for b in range(blocks):
        state = own[b, pl.ds(start, share), :].astype(F32)
        correction[b] = (scaled[b] - ratio * state) / factor


def body(
    wavefunction,
    left_dims,
    right_dims,
    left_ops,
    right_ops,
    source_block,
    target_slot,
    left_index,
    right_index,
    pair_count,
    h_diagonal,
):
    groups = lax.axis_size("ops")
    holders = lax.axis_size("blk")
    own_blocks, left_width, right_width = wavefunction.shape
    share = left_width // groups
    smem = pl.BlockSpec(memory_space=pltpu.SMEM)
    vmem = pl.BlockSpec(memory_space=pltpu.VMEM)
    anywhere = pl.BlockSpec(memory_space=pl.ANY)

    def in_vmem(x):
        return pltpu.with_memory_space_constraint(x, pltpu.VMEM)

    pairs = [(i, i ^ 1) for i in range(groups)]
    left_other = lax.ppermute(left_ops, "ops", pairs)
    right_other = lax.ppermute(right_ops, "ops", pairs)
    alive = lax.broadcasted_iota(jnp.int32, target_slot.shape, 1) < pair_count
    tables = jnp.stack(
        [source_block, jnp.where(alive, target_slot, SPARE), left_index, right_index], axis=1
    )
    tables_other = lax.ppermute(tables, "ops", pairs)

    def exchange(x, mask):
        return lax.ppermute(
            x,
            ("ops", "blk"),
            [
                (g * holders + h, g * holders + (h ^ mask[g % 2]))
                for g in range(groups)
                for h in range(holders)
            ],
        )

    block = jax.ShapeDtypeStruct((1, left_width, right_width), BF16)
    first, second = pl.pallas_call(
        pick_kernel,
        out_shape=(block, block),
        in_specs=[pl.BlockSpec(memory_space=pltpu.HBM)],
        out_specs=(vmem, vmem),
        scratch_shapes=[pltpu.SemaphoreType.DMA((2,))],
        compiler_params=pltpu.CompilerParams(vmem_limit_bytes=2**20),
        name="pick",
    )(pltpu.with_memory_space_constraint(wavefunction, pltpu.HBM))
    for step, (one, two) in enumerate(zip(*MASKS)):
        first_new, second_new = exchange(first, one), exchange(second, two)
        if step == 0:
            lists, totals = pl.pallas_call(
                place_kernel,
                out_shape=(
                    jax.ShapeDtypeStruct((1, 2 * KINDS * LIST + 1), jnp.int32),
                    jax.ShapeDtypeStruct((1, 2 * KINDS), jnp.int32),
                ),
                in_specs=[vmem, vmem],
                out_specs=(smem, smem),
                scratch_shapes=[
                    pltpu.VMEM((2, 1, tables.shape[2]), jnp.int32),
                    pltpu.SMEM((2, 1, tables.shape[2]), jnp.int32),
                    pltpu.SemaphoreType.DMA((1,)),
                ],
                compiler_params=pltpu.CompilerParams(vmem_limit_bytes=2**20),
                name="place",
                cost_estimate=pl.CostEstimate(
                    flops=10**9, bytes_accessed=10**4, transcendentals=0
                ),
            )(tables, tables_other)
        if step == 2:
            first_new, lists, totals = lax.optimization_barrier((first_new, lists, totals))
        if step < 3:
            first = jnp.concatenate([first, first_new])
            second = jnp.concatenate([second, second_new])

    stores = [in_vmem(x) for x in (left_ops, left_other, right_ops, right_other)]
    partial_shape = (own_blocks + 1, left_width, right_width)
    half_blocks = pltpu.VMEM((2,) + first.shape, BF16)
    begun = pl.pallas_call(
        early_kernel,
        out_shape=jax.ShapeDtypeStruct(partial_shape, F32),
        in_specs=[smem, smem] + [vmem] * 4 + [anywhere] * 2,
        out_specs=vmem,
        scratch_shapes=[half_blocks, pltpu.SemaphoreType.DMA((2,))],
        compiler_params=pltpu.CompilerParams(vmem_limit_bytes=6 * 2**20),
        name="early",
        cost_estimate=pl.CostEstimate(flops=8 * 10**9, bytes_accessed=10**6, transcendentals=0),
    )(lists, totals, *stores, first, second)
    chips = groups // 2
    begun = pl.pallas_call(
        late_kernel,
        out_shape=jax.ShapeDtypeStruct(partial_shape, F32),
        in_specs=[smem, smem] + [vmem] * 6,
        out_specs=vmem,
        compiler_params=pltpu.CompilerParams(vmem_limit_bytes=6 * 2**20),
        name="late",
        cost_estimate=pl.CostEstimate(flops=2 * 10**9, bytes_accessed=10**6, transcendentals=0),
    )(lists, totals, *stores, first_new, begun)
    halves = jax.ShapeDtypeStruct((chips, own_blocks * share + NOTE, right_width), F32)
    keep, give = pl.pallas_call(
        functools.partial(last_kernel, groups),
        out_shape=(halves, halves),
        in_specs=[smem, smem] + [vmem] * 7,
        out_specs=(vmem, vmem),
        scratch_shapes=[pltpu.VMEM(partial_shape, F32)],
        compiler_params=pltpu.CompilerParams(vmem_limit_bytes=6 * 2**20),
        name="last",
        cost_estimate=pl.CostEstimate(flops=2 * 10**9, bytes_accessed=10**6, transcendentals=0),
    )(lists, totals, *stores, second_new, begun, wavefunction)
    got = lax.ppermute(give, "ops", pairs)
    chip_masks = (1, 3, 2)
    chip_sum = jax.ShapeDtypeStruct((own_blocks * share, right_width), F32)
    note, mine, *outgoing = pl.pallas_call(
        functools.partial(chip_kernel, chip_masks),
        out_shape=(jax.ShapeDtypeStruct((holders, 128), F32),) + (chip_sum,) * 4,
        in_specs=[vmem, vmem],
        out_specs=(vmem,) * 5,
        compiler_params=pltpu.CompilerParams(vmem_limit_bytes=4 * 2**20),
        name="chip_sum",
    )(keep, got)

    def along_y(x, mask):
        return lax.ppermute(x, "ops", [(i, i ^ (2 * mask)) for i in range(groups)])

    notes = [note] + [along_y(note, mask) for mask in chip_masks]
    arrived = [along_y(x, mask) for x, mask in zip(outgoing, chip_masks)]
    first_sums = lax.all_to_all(
        (notes[0] + notes[1]) + (notes[2] + notes[3]), "blk", 0, 0, tiled=True
    )
    devices = groups * holders
    row_sums = jax.ShapeDtypeStruct((devices, 128), F32)
    shard = jax.ShapeDtypeStruct((own_blocks, share, right_width), F32)
    sigma_vector, scaled, second_sums = pl.pallas_call(
        combine_kernel,
        out_shape=(shard, shard, row_sums),
        in_specs=[smem, smem] + [vmem] * 7,
        out_specs=(vmem, vmem, vmem),
        compiler_params=pltpu.CompilerParams(vmem_limit_bytes=4 * 2**20),
        name="combine",
    )(left_dims, right_dims, mine, *arrived, first_sums, wavefunction, h_diagonal)
    second_sums = lax.all_to_all(second_sums, ("ops", "blk"), 0, 0, tiled=True)
    correction = pl.pallas_call(
        functools.partial(finish_kernel, left_dims.shape[0] * left_width * right_width),
        out_shape=shard,
        in_specs=[vmem, vmem, vmem, vmem],
        out_specs=vmem,
        compiler_params=pltpu.CompilerParams(vmem_limit_bytes=4 * 2**20),
        name="finish",
    )(second_sums, first_sums, scaled, wavefunction)
    return (sigma_vector, correction)


def solution(mesh):
    in_specs = (
        P("blk", None, None),
        P(),
        P(),
        P("ops", "blk", None, None),
        P("ops", "blk", None, None),
        P("ops", "blk"),
        P("ops", "blk"),
        P("ops", "blk"),
        P("ops", "blk"),
        P("ops", "blk"),
        P("blk", "ops", None),
    )
    out_specs = (P("blk", "ops", None), P("blk", "ops", None))
    return jax.shard_map(body, mesh=mesh, in_specs=in_specs, out_specs=out_specs, check_vma=False)
```

```python
import functools

import jax
import jax.numpy as jnp
from jax import lax
from jax.experimental import pallas as pl
from jax.experimental.pallas import tpu as pltpu
from jax.sharding import PartitionSpec as P

UNROLL = 16
TAIL = 4
LIST = 272
SPARE = 4
KINDS = 3
NOTE = 8
LEFT, RIGHT, TARGET, KIND = 4, 9, 14, 17
MASKS = (((1, 3), (3, 1), (4, 12), (12, 4)), ((4, 12), (12, 4), (1, 3), (3, 1)))
F32 = jnp.float32
BF16 = jnp.bfloat16


def run_copies(copies):
    for copy in copies:
        copy.start()
    for copy in copies:
        copy.wait()


def pick_kernel(own, first, second, sems):
    core = lax.rem(lax.axis_index("ops"), 2)
    run_copies([
        pltpu.make_async_copy(own.at[pl.ds(2 * core + i, 1)], target, sems.at[i])
        for i, target in enumerate((first, second))
    ])


def place_kernel(tables, other, lists, totals, words, scalars, sems):
    core = lax.rem(lax.axis_index("ops"), 2)
    holder = lax.axis_index("blk")

    def code(bits):
        gray = bits ^ (bits >> 1)
        return jnp.where(core == 0, gray, ((gray & 1) << 1) | (gray >> 1))

    lives = []
    for group, table in enumerate((tables, other)):
        block = table[0, 0:1, :]
        away, within = (block >> 2) ^ holder, block & 3
        along_x, along_z = code(away & 3), code(away >> 2)
        stream = within & 1
        entry = jnp.where(stream == 0, along_x | (along_z << 2), along_z | (along_x << 2))
        kind = jnp.where((within >> 1) == core, jnp.where(entry < 8, 0, 1 + stream), 3)
        words[group] = (
            (entry & 7)
            | (stream << 3)
            | (table[0, 2:3, :] << LEFT)
            | (table[0, 3:4, :] << RIGHT)
            | (table[0, 1:2, :] << TARGET)
            | (kind << KIND)
        )
        lives.append(jnp.sum(jnp.where(table[0, 1:2, :] < SPARE, 1, 0)))
    run_copies([pltpu.make_async_copy(words, scalars, sems.at[0])])
    for group in range(2):

        def place(k, filled, group=group):
            word = scalars[group, 0, k]
            kind = word >> KIND
            where = jnp.int32(2 * KINDS * LIST)
            for i, length in enumerate(filled):
                where = jnp.where(kind == i, (2 * i + group) * LIST + length, where)
            lists[0, where] = word
            return tuple(length + jnp.where(kind == i, 1, 0) for i, length in enumerate(filled))

        def places(i, filled, place=place):
            for u in range(8):
                filled = place(8 * i + u, filled)
            return filled

        turns = lives[group] // 8
        filled = lax.fori_loop(0, turns, places, (jnp.int32(0),) * KINDS)
        filled = lax.fori_loop(8 * turns, lives[group], place, filled)
        for i, length in enumerate(filled):
            for u in range(UNROLL):
                lists[0, (2 * i + group) * LIST + length + u] = SPARE << TARGET
            totals[0, 2 * i + group] = length


def run_slots(lists, totals, which, lefts, rights, blocks, acc):
    for group in range(2):
        lstore, rstore = lefts[group], rights[group]

        def many(i, carry, width, offset, lstore=lstore, rstore=rstore):
            for u in range(width):
                word = lists[0, offset + i * width + u]
                psi = blocks[(word >> 3) & 1, word & 7] if which == 0 else blocks[word & 7]
                product = jnp.dot(
                    lstore[0, (word >> LEFT) & 31], psi, preferred_element_type=F32
                ).astype(BF16)
                acc[(word >> TARGET) & 7] += lax.dot_general(
                    product, rstore[0, (word >> RIGHT) & 31], (((1,), (1,)), ((), ())),
                    preferred_element_type=F32,
                )
            return carry

        live, base = totals[0, 2 * which + group], (2 * which + group) * LIST
        turns = (live + UNROLL - 1 - 2 * TAIL) // UNROLL
        lax.fori_loop(0, turns, functools.partial(many, width=UNROLL, offset=base), 0)
        rest = jnp.maximum(live - turns * UNROLL, 0)
        lax.fori_loop(
            0,
            (rest + TAIL - 1) // TAIL,
            functools.partial(many, width=TAIL, offset=base + turns * UNROLL),
            0,
        )


def early_kernel(lists, totals, left0, left1, right0, right1, first, second, acc, blocks, sems):
    run_copies([
        pltpu.make_async_copy(piece, blocks.at[i], sems.at[i])
        for i, piece in enumerate((first, second))
    ])
    acc[...] = jnp.zeros_like(acc)
    run_slots(lists, totals, 0, (left0, left1), (right0, right1), blocks, acc)


def late_kernel(lists, totals, left0, left1, right0, right1, first, begun, acc):
    del begun
    run_slots(lists, totals, 1, (left0, left1), (right0, right1), first, acc)


def last_kernel(
    groups, lists, totals, left0, left1, right0, right1, second, begun, own, acc, keep, give
):
    del begun
    run_slots(lists, totals, 2, (left0, left1), (right0, right1), second, acc)
    core = lax.rem(lax.axis_index("ops"), 2)
    chips, width = keep.shape[0], keep.shape[2]
    share = (keep.shape[1] - NOTE) // SPARE
    energy = jnp.zeros((1, 1), F32)
    norm = jnp.zeros((1, 1), F32)
    for b in range(SPARE):
        wide = own[b].astype(F32)
        energy += jnp.sum(acc[b] * wide, keepdims=True)
        norm += jnp.sum(wide * wide, keepdims=True)
        for y in range(chips):
            for out, place in ((keep, core), (give, 1 - core)):
                start = pl.multiple_of((2 * y + place) * share, share)
                out[y, b * share:(b + 1) * share] = acc[b, pl.ds(start, share), :]
    lane = lax.broadcasted_iota(jnp.int32, (NOTE, width), 1)
    note = jnp.where(lane == 0, energy, jnp.where(lane == 1, norm / groups, 0.0))
    for y in range(chips):
        for out in (keep, give):
            out[y, SPARE * share:] = note


def chip_kernel(masks, keep, got, note, mine, *outs):
    chip = lax.axis_index("ops") // 2
    rows = mine.shape[0]
    total = keep[0, rows:, :128] + got[0, rows:, :128]
    for i in range(note.shape[0] // NOTE):
        note[i * NOTE:(i + 1) * NOTE] = total
    for mask, out in zip((0,) + masks, (mine,) + outs):
        out[...] = keep[chip ^ mask, :rows] + got[chip ^ mask, :rows]


def combine_kernel(
    left_dims, right_dims, mine, near, far, across, totals, own, diagonal, sigma, scaled, sums
):
    group_rank, holder = lax.axis_index("ops"), lax.axis_index("blk")
    blocks, share, width = sigma.shape
    whole = jnp.sum(totals[...], axis=0, keepdims=True)
    rayleigh = whole[0:1, 0:1] / whole[0:1, 1:2]
    row = lax.broadcasted_iota(jnp.int32, (share, width), 0) + group_rank * share
    column = lax.broadcasted_iota(jnp.int32, (share, width), 1)
    start = pl.multiple_of(group_rank * share, share)
    along = jnp.zeros((1, 1), F32)
    square = jnp.zeros((1, 1), F32)
    for b in range(blocks):
        ident = holder * blocks + b
        inside = (row < left_dims[ident]) & (column < right_dims[ident])
        rows = slice(b * share, (b + 1) * share)
        total = (mine[rows] + near[rows]) + (far[rows] + across[rows])
        total = jnp.where(inside, total, 0.0)
        sigma[b] = total
        state = own[b, pl.ds(start, share), :].astype(F32)
        value = (total - rayleigh * state) / jnp.maximum(jnp.abs(diagonal[b] - rayleigh), 1.0)
        scaled[b] = value
        along += jnp.sum(state * value, keepdims=True)
        square += jnp.sum(value * value, keepdims=True)
    lane = lax.broadcasted_iota(jnp.int32, sums.shape, 1)
    sums[...] = jnp.where(lane == 0, along, jnp.where(lane == 1, square, 0.0))


def finish_kernel(slots_total, arrived, totals, scaled, own, correction):
    blocks, share, width = scaled.shape
    sums = jnp.sum(arrived[...], axis=0, keepdims=True)
    along, square = sums[0:1, 0:1], sums[0:1, 1:2]
    ratio = along / jnp.sum(totals[...], axis=0, keepdims=True)[0:1, 1:2]
    length_sq = jnp.maximum(square - along * ratio, 0.0)
    factor = jnp.sqrt(length_sq / slots_total + 1e-06)
    start = pl.multiple_of(lax.axis_index("ops") * share, share)
    for b in range(blocks):
        state = own[b, pl.ds(start, share), :].astype(F32)
        correction[b] = (scaled[b] - ratio * state) / factor


def body(
    wavefunction,
    left_dims,
    right_dims,
    left_ops,
    right_ops,
    source_block,
    target_slot,
    left_index,
    right_index,
    pair_count,
    h_diagonal,
):
    groups = lax.axis_size("ops")
    holders = lax.axis_size("blk")
    own_blocks, left_width, right_width = wavefunction.shape
    share = left_width // groups
    smem = pl.BlockSpec(memory_space=pltpu.SMEM)
    vmem = pl.BlockSpec(memory_space=pltpu.VMEM)
    anywhere = pl.BlockSpec(memory_space=pl.ANY)

    def in_vmem(x):
        return pltpu.with_memory_space_constraint(x, pltpu.VMEM)

    pairs = [(i, i ^ 1) for i in range(groups)]
    alive = lax.broadcasted_iota(jnp.int32, target_slot.shape, 1) < pair_count
    tables = jnp.stack(
        [source_block, jnp.where(alive, target_slot, SPARE), left_index, right_index], axis=1
    )
    tables_other = lax.ppermute(tables, "ops", pairs)

    def exchange(x, mask):
        return lax.ppermute(
            x,
            ("ops", "blk"),
            [
                (g * holders + h, g * holders + (h ^ mask[g % 2]))
                for g in range(groups)
                for h in range(holders)
            ],
        )

    block = jax.ShapeDtypeStruct((1, left_width, right_width), BF16)
    first, second = pl.pallas_call(
        pick_kernel,
        out_shape=(block, block),
        in_specs=[pl.BlockSpec(memory_space=pltpu.HBM)],
        out_specs=(vmem, vmem),
        scratch_shapes=[pltpu.SemaphoreType.DMA((2,))],
        compiler_params=pltpu.CompilerParams(vmem_limit_bytes=2**20),
        name="pick",
    )(pltpu.with_memory_space_constraint(wavefunction, pltpu.HBM))
    first, left_here, right_here = lax.optimization_barrier((first, left_ops, right_ops))
    left_other = lax.ppermute(left_here, "ops", pairs)
    right_other = lax.ppermute(right_here, "ops", pairs)
    for step, (one, two) in enumerate(zip(*MASKS)):
        first_new, second_new = exchange(first, one), exchange(second, two)
        if step == 1:
            second_new, tables_other = lax.optimization_barrier((second_new, tables_other))
            lists, totals = pl.pallas_call(
                place_kernel,
                out_shape=(
                    jax.ShapeDtypeStruct((1, 2 * KINDS * LIST + 1), jnp.int32),
                    jax.ShapeDtypeStruct((1, 2 * KINDS), jnp.int32),
                ),
                in_specs=[vmem, vmem],
                out_specs=(smem, smem),
                scratch_shapes=[
                    pltpu.VMEM((2, 1, tables.shape[2]), jnp.int32),
                    pltpu.SMEM((2, 1, tables.shape[2]), jnp.int32),
                    pltpu.SemaphoreType.DMA((1,)),
                ],
                compiler_params=pltpu.CompilerParams(vmem_limit_bytes=2**20),
                name="place",
                cost_estimate=pl.CostEstimate(
                    flops=10**9, bytes_accessed=10**4, transcendentals=0
                ),
            )(tables, tables_other)
        if step == 2:
            first_new, lists, totals = lax.optimization_barrier((first_new, lists, totals))
        if step < 3:
            first = jnp.concatenate([first, first_new])
            second = jnp.concatenate([second, second_new])

    stores = [in_vmem(x) for x in (left_ops, left_other, right_ops, right_other)]
    partial_shape = (own_blocks + 1, left_width, right_width)
    half_blocks = pltpu.VMEM((2,) + first.shape, BF16)
    begun = pl.pallas_call(
        early_kernel,
        out_shape=jax.ShapeDtypeStruct(partial_shape, F32),
        in_specs=[smem, smem] + [vmem] * 4 + [anywhere] * 2,
        out_specs=vmem,
        scratch_shapes=[half_blocks, pltpu.SemaphoreType.DMA((2,))],
        compiler_params=pltpu.CompilerParams(vmem_limit_bytes=6 * 2**20),
        name="early",
        cost_estimate=pl.CostEstimate(flops=8 * 10**9, bytes_accessed=10**6, transcendentals=0),
    )(lists, totals, *stores, first, second)
    chips = groups // 2
    begun = pl.pallas_call(
        late_kernel,
        out_shape=jax.ShapeDtypeStruct(partial_shape, F32),
        in_specs=[smem, smem] + [vmem] * 6,
        out_specs=vmem,
        input_output_aliases={7: 0},
        compiler_params=pltpu.CompilerParams(vmem_limit_bytes=6 * 2**20),
        name="late",
        cost_estimate=pl.CostEstimate(flops=2 * 10**9, bytes_accessed=10**6, transcendentals=0),
    )(lists, totals, *stores, first_new, begun)
    halves = jax.ShapeDtypeStruct((chips, own_blocks * share + NOTE, right_width), F32)
    _, keep, give = pl.pallas_call(
        functools.partial(last_kernel, groups),
        out_shape=(jax.ShapeDtypeStruct(partial_shape, F32), halves, halves),
        in_specs=[smem, smem] + [vmem] * 7,
        out_specs=(vmem,) * 3,
        input_output_aliases={7: 0},
        compiler_params=pltpu.CompilerParams(vmem_limit_bytes=6 * 2**20),
        name="last",
        cost_estimate=pl.CostEstimate(flops=2 * 10**9, bytes_accessed=10**6, transcendentals=0),
    )(lists, totals, *stores, second_new, begun, wavefunction)
    got = lax.ppermute(give, "ops", pairs)
    chip_masks = (1, 3, 2)
    chip_sum = jax.ShapeDtypeStruct((own_blocks * share, right_width), F32)
    note, mine, *outgoing = pl.pallas_call(
        functools.partial(chip_kernel, chip_masks),
        out_shape=(jax.ShapeDtypeStruct((holders, 128), F32),) + (chip_sum,) * 4,
        in_specs=[vmem, vmem],
        out_specs=(vmem,) * 5,
        compiler_params=pltpu.CompilerParams(vmem_limit_bytes=4 * 2**20),
        name="chip_sum",
    )(keep, got)

    def along_y(x, mask):
        return lax.ppermute(x, "ops", [(i, i ^ (2 * mask)) for i in range(groups)])

    notes = [note] + [along_y(note, mask) for mask in chip_masks]
    arrived = [along_y(x, mask) for x, mask in zip(outgoing, chip_masks)]
    first_sums = lax.all_to_all(
        (notes[0] + notes[1]) + (notes[2] + notes[3]), "blk", 0, 0, tiled=True
    )
    devices = groups * holders
    row_sums = jax.ShapeDtypeStruct((devices, 128), F32)
    shard = jax.ShapeDtypeStruct((own_blocks, share, right_width), F32)
    sigma_vector, scaled, second_sums = pl.pallas_call(
        combine_kernel,
        out_shape=(shard, shard, row_sums),
        in_specs=[smem, smem] + [vmem] * 7,
        out_specs=(vmem, vmem, vmem),
        compiler_params=pltpu.CompilerParams(vmem_limit_bytes=4 * 2**20),
        name="combine",
    )(left_dims, right_dims, mine, *arrived, first_sums, wavefunction, h_diagonal)
    second_sums = lax.all_to_all(second_sums, ("ops", "blk"), 0, 0, tiled=True)
    correction = pl.pallas_call(
        functools.partial(finish_kernel, left_dims.shape[0] * left_width * right_width),
        out_shape=shard,
        in_specs=[vmem, vmem, vmem, vmem],
        out_specs=vmem,
        compiler_params=pltpu.CompilerParams(vmem_limit_bytes=4 * 2**20),
        name="finish",
    )(second_sums, first_sums, scaled, wavefunction)
    return (sigma_vector, correction)


def solution(mesh):
    in_specs = (
        P("blk", None, None),
        P(),
        P(),
        P("ops", "blk", None, None),
        P("ops", "blk", None, None),
        P("ops", "blk"),
        P("ops", "blk"),
        P("ops", "blk"),
        P("ops", "blk"),
        P("ops", "blk"),
        P("blk", "ops", None),
    )
    out_specs = (P("blk", "ops", None), P("blk", "ops", None))
    return jax.shard_map(body, mesh=mesh, in_specs=in_specs, out_specs=out_specs, check_vma=False)
```

```python
import functools

import jax
import jax.numpy as jnp
from jax import lax
from jax.experimental import pallas as pl
from jax.experimental.pallas import tpu as pltpu
from jax.sharding import PartitionSpec as P

UNROLL = 16
TAIL = 4
LIST = 272
SPARE = 4
KINDS = 3
NOTE = 8
LEFT, RIGHT, TARGET = 4, 9, 14
MASKS = (((1, 3), (3, 1), (4, 12), (12, 4)), ((4, 12), (12, 4), (1, 3), (3, 1)))
F32 = jnp.float32
BF16 = jnp.bfloat16


def run_copies(copies):
    for copy in copies:
        copy.start()
    for copy in copies:
        copy.wait()


def pick_kernel(own, first, second, sems):
    core = lax.rem(lax.axis_index("ops"), 2)
    run_copies([
        pltpu.make_async_copy(own.at[pl.ds(2 * core + i, 1)], target, sems.at[i])
        for i, target in enumerate((first, second))
    ])


def place_kernel(tables, other, lists, totals, staged, scalars, sems):
    core = lax.rem(lax.axis_index("ops"), 2)
    holder = lax.axis_index("blk")
    slots = tables.shape[2]

    def code(bits):
        gray = bits ^ (bits >> 1)
        return jnp.where(core == 0, gray, ((gray & 1) << 1) | (gray >> 1))

    row = lax.broadcasted_iota(jnp.int32, (8, slots), 0)
    earlier = lax.broadcasted_iota(jnp.int32, (slots, slots), 0)
    later = lax.broadcasted_iota(jnp.int32, (slots, slots), 1)
    ahead = jnp.where(earlier <= later, 1.0, 0.0).astype(BF16)
    lives = []
    for group, table in enumerate((tables, other)):
        block, target = table[0, 0:1, :], table[0, 1:2, :]
        away, within = (block >> 2) ^ holder, block & 3
        along_x, along_z = code(away & 3), code(away >> 2)
        stream = within & 1
        entry = jnp.where(stream == 0, along_x | (along_z << 2), along_z | (along_x << 2))
        kind = jnp.where(entry == 0, 0, jnp.where(entry < 8, 1, 2))
        kind = jnp.where(((within >> 1) == core) & (target < SPARE), kind, KINDS)
        word = (
            (entry & 7)
            | (stream << 3)
            | (table[0, 2:3, :] << LEFT)
            | (table[0, 3:4, :] << RIGHT)
            | (target << TARGET)
        )
        chosen = row == kind
        counts = jnp.dot(
            jnp.where(chosen, 1.0, 0.0).astype(BF16), ahead, preferred_element_type=F32
        ).astype(jnp.int32)
        where = jnp.where(chosen, counts - 1 + (2 * row + group) * LIST, 0)
        where = jnp.where(kind < KINDS, jnp.sum(where[:KINDS], axis=0, keepdims=True), 2 * KINDS * LIST)
        staged[group] = jnp.where(row < KINDS, counts, jnp.where(row == KINDS, word, where))
        lives.append(jnp.sum(jnp.where(target < SPARE, 1, 0)))
    run_copies([pltpu.make_async_copy(staged, scalars, sems.at[0])])
    for group in range(2):

        def places(i, carry, group=group):
            for u in range(16):
                lists[0, scalars[group, KINDS + 1, 16 * i + u]] = scalars[group, KINDS, 16 * i + u]
            return carry

        lax.fori_loop(0, (lives[group] + 15) // 16, places, 0)
        for i in range(KINDS):
            length = scalars[group, i, slots - 1]
            totals[0, 2 * i + group] = length
            for u in range(UNROLL):
                lists[0, (2 * i + group) * LIST + length + u] = SPARE << TARGET


def run_slots(lists, totals, which, lefts, rights, blocks, acc):
    for group in range(2):
        lstore, rstore = lefts[group], rights[group]

        def many(i, carry, width, offset, lstore=lstore, rstore=rstore):
            for u in range(width):
                word = lists[0, offset + i * width + u]
                psi = blocks[(word >> 3) & 1, word & 7]
                product = jnp.dot(
                    lstore[0, (word >> LEFT) & 31], psi, preferred_element_type=F32
                ).astype(BF16)
                acc[(word >> TARGET) & 7] += lax.dot_general(
                    product, rstore[0, (word >> RIGHT) & 31], (((1,), (1,)), ((), ())),
                    preferred_element_type=F32,
                )
            return carry

        live, base = totals[0, 2 * which + group], (2 * which + group) * LIST
        turns = (live + UNROLL - 1 - 2 * TAIL) // UNROLL
        lax.fori_loop(0, turns, functools.partial(many, width=UNROLL, offset=base), 0)
        rest = jnp.maximum(live - turns * UNROLL, 0)
        lax.fori_loop(
            0,
            (rest + TAIL - 1) // TAIL,
            functools.partial(many, width=TAIL, offset=base + turns * UNROLL),
            0,
        )


def slots_kernel(
    which, lists, totals, left0, left1, right0, right1, first, second, *rest
):
    acc, blocks, sems = rest[-3:]
    copies = [
        pltpu.make_async_copy(piece, blocks.at[i], sems.at[i])
        for i, piece in enumerate((first, second))
    ]
    for copy in copies:
        copy.start()
    if which == 0:
        acc[...] = jnp.zeros_like(acc)
    for copy in copies:
        copy.wait()
    run_slots(lists, totals, which, (left0, left1), (right0, right1), blocks, acc)


def late_kernel(
    groups, lists, totals, left0, left1, right0, right1, first, second, begun, own,
    acc, keep, give, blocks, sems,
):
    slots_kernel(
        2, lists, totals, left0, left1, right0, right1, first, second, begun, acc, blocks, sems
    )
    core = lax.rem(lax.axis_index("ops"), 2)
    chips, width = keep.shape[0], keep.shape[2]
    share = (keep.shape[1] - NOTE) // SPARE
    energy = jnp.zeros((1, 1), F32)
    norm = jnp.zeros((1, 1), F32)
    for b in range(SPARE):
        wide = own[b].astype(F32)
        energy += jnp.sum(acc[b] * wide, keepdims=True)
        norm += jnp.sum(wide * wide, keepdims=True)
        for y in range(chips):
            for out, place in ((keep, core), (give, 1 - core)):
                start = pl.multiple_of((2 * y + place) * share, share)
                out[y, b * share:(b + 1) * share] = acc[b, pl.ds(start, share), :]
    lane = lax.broadcasted_iota(jnp.int32, (NOTE, width), 1)
    note = jnp.where(lane == 0, energy, jnp.where(lane == 1, norm / groups, 0.0))
    for y in range(chips):
        for out in (keep, give):
            out[y, SPARE * share:] = note


def chip_kernel(masks, keep, got, note, mine, *outs):
    chip = lax.axis_index("ops") // 2
    rows = mine.shape[0]
    total = keep[0, rows:, :128] + got[0, rows:, :128]
    for i in range(note.shape[0] // NOTE):
        note[i * NOTE:(i + 1) * NOTE] = total
    for mask, out in zip((0,) + masks, (mine,) + outs):
        out[...] = keep[chip ^ mask, :rows] + got[chip ^ mask, :rows]


def combine_kernel(
    left_dims, right_dims, mine, near, far, across, totals, own, diagonal, sigma, scaled, sums
):
    group_rank, holder = lax.axis_index("ops"), lax.axis_index("blk")
    blocks, share, width = sigma.shape
    whole = jnp.sum(totals[...], axis=0, keepdims=True)
    rayleigh = whole[0:1, 0:1] / whole[0:1, 1:2]
    row = lax.broadcasted_iota(jnp.int32, (share, width), 0) + group_rank * share
    column = lax.broadcasted_iota(jnp.int32, (share, width), 1)
    start = pl.multiple_of(group_rank * share, share)
    along = jnp.zeros((1, 1), F32)
    square = jnp.zeros((1, 1), F32)
    for b in range(blocks):
        ident = holder * blocks + b
        inside = (row < left_dims[ident]) & (column < right_dims[ident])
        rows = slice(b * share, (b + 1) * share)
        total = (mine[rows] + near[rows]) + (far[rows] + across[rows])
        total = jnp.where(inside, total, 0.0)
        sigma[b] = total
        state = own[b, pl.ds(start, share), :].astype(F32)
        value = (total - rayleigh * state) / jnp.maximum(jnp.abs(diagonal[b] - rayleigh), 1.0)
        scaled[b] = value
        along += jnp.sum(state * value, keepdims=True)
        square += jnp.sum(value * value, keepdims=True)
    lane = lax.broadcasted_iota(jnp.int32, sums.shape, 1)
    sums[...] = jnp.where(lane == 0, along, jnp.where(lane == 1, square, 0.0))


def finish_kernel(slots_total, arrived, totals, scaled, own, correction):
    blocks, share, width = scaled.shape
    sums = jnp.sum(arrived[...], axis=0, keepdims=True)
    along, square = sums[0:1, 0:1], sums[0:1, 1:2]
    ratio = along / jnp.sum(totals[...], axis=0, keepdims=True)[0:1, 1:2]
    length_sq = jnp.maximum(square - along * ratio, 0.0)
    factor = jnp.sqrt(length_sq / slots_total + 1e-06)
    start = pl.multiple_of(lax.axis_index("ops") * share, share)
    for b in range(blocks):
        state = own[b, pl.ds(start, share), :].astype(F32)
        correction[b] = (scaled[b] - ratio * state) / factor


def body(
    wavefunction,
    left_dims,
    right_dims,
    left_ops,
    right_ops,
    source_block,
    target_slot,
    left_index,
    right_index,
    pair_count,
    h_diagonal,
):
    groups = lax.axis_size("ops")
    holders = lax.axis_size("blk")
    own_blocks, left_width, right_width = wavefunction.shape
    share = left_width // groups
    smem = pl.BlockSpec(memory_space=pltpu.SMEM)
    vmem = pl.BlockSpec(memory_space=pltpu.VMEM)
    anywhere = pl.BlockSpec(memory_space=pl.ANY)

    def in_vmem(x):
        return pltpu.with_memory_space_constraint(x, pltpu.VMEM)

    pairs = [(i, i ^ 1) for i in range(groups)]
    alive = lax.broadcasted_iota(jnp.int32, target_slot.shape, 1) < pair_count
    tables = jnp.stack(
        [source_block, jnp.where(alive, target_slot, SPARE), left_index, right_index], axis=1
    )
    tables_other = lax.ppermute(tables, "ops", pairs)

    def exchange(x, mask):
        return lax.ppermute(
            x,
            ("ops", "blk"),
            [
                (g * holders + h, g * holders + (h ^ mask[g % 2]))
                for g in range(groups)
                for h in range(holders)
            ],
        )

    block = jax.ShapeDtypeStruct((1, left_width, right_width), BF16)
    first, second = pl.pallas_call(
        pick_kernel,
        out_shape=(block, block),
        in_specs=[pl.BlockSpec(memory_space=pltpu.HBM)],
        out_specs=(vmem, vmem),
        scratch_shapes=[pltpu.SemaphoreType.DMA((2,))],
        compiler_params=pltpu.CompilerParams(vmem_limit_bytes=2**20),
        name="pick",
    )(pltpu.with_memory_space_constraint(wavefunction, pltpu.HBM))
    first, left_here, right_here = lax.optimization_barrier((first, left_ops, right_ops))
    left_other = lax.ppermute(left_here, "ops", pairs)
    right_other = lax.ppermute(right_here, "ops", pairs)
    stores = [in_vmem(x) for x in (left_ops, left_other, right_ops, right_other)]
    partial_shape = (own_blocks + 1, left_width, right_width)

    def slots_call(which, lists, totals, gathered, begun, flops):
        return pl.pallas_call(
            functools.partial(slots_kernel, which),
            out_shape=jax.ShapeDtypeStruct(partial_shape, F32),
            in_specs=[smem, smem] + [vmem] * 4 + [anywhere] * 2 + [vmem] * len(begun),
            out_specs=vmem,
            input_output_aliases={8: 0} if begun else {},
            scratch_shapes=[
                pltpu.VMEM((2,) + gathered[0].shape, BF16), pltpu.SemaphoreType.DMA((2,)),
            ],
            compiler_params=pltpu.CompilerParams(vmem_limit_bytes=6 * 2**20),
            name=("near", "early")[which],
            cost_estimate=pl.CostEstimate(flops=flops, bytes_accessed=10**6, transcendentals=0),
        )(lists, totals, *stores, *gathered, *begun)

    for step, (one, two) in enumerate(zip(*MASKS)):
        first_new, second_new = exchange(first, one), exchange(second, two)
        if step == 0:
            first_new, tables_other = lax.optimization_barrier((first_new, tables_other))
            lists, totals = pl.pallas_call(
                place_kernel,
                out_shape=(
                    jax.ShapeDtypeStruct((1, 2 * KINDS * LIST + 1), jnp.int32),
                    jax.ShapeDtypeStruct((1, 2 * KINDS), jnp.int32),
                ),
                in_specs=[vmem, vmem],
                out_specs=(smem, smem),
                scratch_shapes=[
                    pltpu.VMEM((2, 8, tables.shape[2]), jnp.int32),
                    pltpu.SMEM((2, 8, tables.shape[2]), jnp.int32),
                    pltpu.SemaphoreType.DMA((1,)),
                ],
                compiler_params=pltpu.CompilerParams(vmem_limit_bytes=2 * 2**20),
                name="place",
                cost_estimate=pl.CostEstimate(
                    flops=10**9, bytes_accessed=10**4, transcendentals=0
                ),
            )(tables, tables_other)
            near = (first, second)
        if step == 1:
            second_new, lists, totals = lax.optimization_barrier((second_new, lists, totals))
        if step == 2:
            begun = slots_call(0, lists, totals, near, (), 3 * 10**9)
            first_new, second_new, begun = lax.optimization_barrier(
                (first_new, second_new, begun)
            )
        if step < 3:
            first = jnp.concatenate([first, first_new])
            second = jnp.concatenate([second, second_new])

    begun = slots_call(1, lists, totals, (first, second), (begun,), 6 * 10**9)
    chips = groups // 2
    halves = jax.ShapeDtypeStruct((chips, own_blocks * share + NOTE, right_width), F32)
    _, keep, give = pl.pallas_call(
        functools.partial(late_kernel, groups),
        out_shape=(jax.ShapeDtypeStruct(partial_shape, F32), halves, halves),
        in_specs=[smem, smem] + [vmem] * 4 + [anywhere] * 2 + [vmem] * 2,
        out_specs=(vmem,) * 3,
        input_output_aliases={8: 0},
        scratch_shapes=[
            pltpu.VMEM((2,) + first.shape, BF16), pltpu.SemaphoreType.DMA((2,)),
        ],
        compiler_params=pltpu.CompilerParams(vmem_limit_bytes=6 * 2**20),
        name="late",
        cost_estimate=pl.CostEstimate(flops=4 * 10**9, bytes_accessed=10**6, transcendentals=0),
    )(lists, totals, *stores, first_new, second_new, begun, wavefunction)
    got = lax.ppermute(give, "ops", pairs)
    chip_masks = (1, 3, 2)
    chip_sum = jax.ShapeDtypeStruct((own_blocks * share, right_width), F32)
    note, mine, *outgoing = pl.pallas_call(
        functools.partial(chip_kernel, chip_masks),
        out_shape=(jax.ShapeDtypeStruct((holders, 128), F32),) + (chip_sum,) * 4,
        in_specs=[vmem, vmem],
        out_specs=(vmem,) * 5,
        compiler_params=pltpu.CompilerParams(vmem_limit_bytes=4 * 2**20),
        name="chip_sum",
    )(keep, got)

    def along_y(x, mask):
        return lax.ppermute(x, "ops", [(i, i ^ (2 * mask)) for i in range(groups)])

    notes = [note] + [along_y(note, mask) for mask in chip_masks]
    arrived = [along_y(x, mask) for x, mask in zip(outgoing, chip_masks)]
    first_sums = lax.all_to_all(
        (notes[0] + notes[1]) + (notes[2] + notes[3]), "blk", 0, 0, tiled=True
    )
    devices = groups * holders
    row_sums = jax.ShapeDtypeStruct((devices, 128), F32)
    shard = jax.ShapeDtypeStruct((own_blocks, share, right_width), F32)
    sigma_vector, scaled, second_sums = pl.pallas_call(
        combine_kernel,
        out_shape=(shard, shard, row_sums),
        in_specs=[smem, smem] + [vmem] * 7,
        out_specs=(vmem, vmem, vmem),
        compiler_params=pltpu.CompilerParams(vmem_limit_bytes=4 * 2**20),
        name="combine",
    )(left_dims, right_dims, mine, *arrived, first_sums, wavefunction, h_diagonal)
    second_sums = lax.all_to_all(second_sums, ("ops", "blk"), 0, 0, tiled=True)
    correction = pl.pallas_call(
        functools.partial(finish_kernel, left_dims.shape[0] * left_width * right_width),
        out_shape=shard,
        in_specs=[vmem, vmem, vmem, vmem],
        out_specs=vmem,
        compiler_params=pltpu.CompilerParams(vmem_limit_bytes=4 * 2**20),
        name="finish",
    )(second_sums, first_sums, scaled, wavefunction)
    return (sigma_vector, correction)


def solution(mesh):
    in_specs = (
        P("blk", None, None),
        P(),
        P(),
        P("ops", "blk", None, None),
        P("ops", "blk", None, None),
        P("ops", "blk"),
        P("ops", "blk"),
        P("ops", "blk"),
        P("ops", "blk"),
        P("ops", "blk"),
        P("blk", "ops", None),
    )
    out_specs = (P("blk", "ops", None), P("blk", "ops", None))
    return jax.shard_map(body, mesh=mesh, in_specs=in_specs, out_specs=out_specs, check_vma=False)
```

```python
import functools

import jax
import jax.numpy as jnp
from jax import lax
from jax.experimental import pallas as pl
from jax.experimental.pallas import tpu as pltpu
from jax.sharding import PartitionSpec as P

UNROLL = 16
TAIL = 4
LIST = 528
SPARE = 4
KINDS = 3
NOTE = 8
LEFT, RIGHT, TARGET, GROUP = 4, 9, 14, 17
MASKS = (((1, 3), (3, 1), (4, 12), (12, 4)), ((4, 12), (12, 4), (1, 3), (3, 1)))
F32 = jnp.float32
BF16 = jnp.bfloat16


def run_copies(copies):
    for copy in copies:
        copy.start()
    for copy in copies:
        copy.wait()


def pick_kernel(own, first, second, sems):
    core = lax.rem(lax.axis_index("ops"), 2)
    run_copies([
        pltpu.make_async_copy(own.at[pl.ds(2 * core + i, 1)], target, sems.at[i])
        for i, target in enumerate((first, second))
    ])


def place_kernel(tables, other, lists, totals, staged, scalars, sems):
    core = lax.rem(lax.axis_index("ops"), 2)
    holder = lax.axis_index("blk")
    slots = tables.shape[2]

    def code(bits):
        gray = bits ^ (bits >> 1)
        return jnp.where(core == 0, gray, ((gray & 1) << 1) | (gray >> 1))

    row = lax.broadcasted_iota(jnp.int32, (8, slots), 0)
    earlier = lax.broadcasted_iota(jnp.int32, (slots, slots), 0)
    later = lax.broadcasted_iota(jnp.int32, (slots, slots), 1)
    ahead = jnp.where(earlier <= later, 1.0, 0.0).astype(BF16)
    before = jnp.zeros((8, 1), jnp.int32)
    lives = []
    for group, table in enumerate((tables, other)):
        block, target = table[0, 0:1, :], table[0, 1:2, :]
        away, within = (block >> 2) ^ holder, block & 3
        along_x, along_z = code(away & 3), code(away >> 2)
        stream = within & 1
        entry = jnp.where(stream == 0, along_x | (along_z << 2), along_z | (along_x << 2))
        kind = jnp.where(entry < 8, 0, 1 + stream)
        kind = jnp.where(((within >> 1) == core) & (target < SPARE), kind, KINDS)
        word = (
            (entry & 7)
            | (stream << 3)
            | (table[0, 2:3, :] << LEFT)
            | (table[0, 3:4, :] << RIGHT)
            | (target << TARGET)
            | (group << GROUP)
        )
        chosen = row == kind
        counts = jnp.dot(
            jnp.where(chosen, 1.0, 0.0).astype(BF16), ahead, preferred_element_type=F32
        ).astype(jnp.int32)
        where = jnp.where(chosen, counts - 1 + row * LIST + before, 0)
        where = jnp.where(kind < KINDS, jnp.sum(where[:KINDS], axis=0, keepdims=True), KINDS * LIST)
        before = counts[:, slots - 1:]
        staged[group] = jnp.where(row < KINDS, counts, jnp.where(row == KINDS, word, where))
        lives.append(jnp.sum(jnp.where(target < SPARE, 1, 0)))
    run_copies([pltpu.make_async_copy(staged, scalars, sems.at[0])])
    for group in range(2):

        def places(i, carry, group=group):
            for u in range(16):
                lists[0, scalars[group, KINDS + 1, 16 * i + u]] = scalars[group, KINDS, 16 * i + u]
            return carry

        lax.fori_loop(0, (lives[group] + 15) // 16, places, 0)
    for i in range(KINDS):
        length = scalars[0, i, slots - 1] + scalars[1, i, slots - 1]
        totals[0, i] = length
        for u in range(UNROLL):
            lists[0, i * LIST + length + u] = SPARE << TARGET


def run_slots(lists, totals, which, lefts, rights, blocks, acc):
    def many(i, carry, width, offset):
        for u in range(width):
            word = lists[0, offset + i * width + u]
            own = (word >> GROUP) == 0
            left, right = (word >> LEFT) & 31, (word >> RIGHT) & 31
            psi = blocks[(word >> 3) & 1, word & 7] if which == 0 else blocks[word & 7]
            product = jnp.dot(
                jnp.where(own, lefts[0][0, left], lefts[1][0, left]), psi,
                preferred_element_type=F32,
            ).astype(BF16)
            acc[(word >> TARGET) & 7] += lax.dot_general(
                product, jnp.where(own, rights[0][0, right], rights[1][0, right]),
                (((1,), (1,)), ((), ())), preferred_element_type=F32,
            )
        return carry

    live, base = totals[0, which], which * LIST
    turns = (live + UNROLL - 1 - 2 * TAIL) // UNROLL
    lax.fori_loop(0, turns, functools.partial(many, width=UNROLL, offset=base), 0)
    rest = jnp.maximum(live - turns * UNROLL, 0)
    lax.fori_loop(
        0,
        (rest + TAIL - 1) // TAIL,
        functools.partial(many, width=TAIL, offset=base + turns * UNROLL),
        0,
    )


def early_kernel(lists, totals, left0, left1, right0, right1, first, second, acc, blocks, sems):
    run_copies([
        pltpu.make_async_copy(piece, blocks.at[i], sems.at[i])
        for i, piece in enumerate((first, second))
    ])
    acc[...] = jnp.zeros_like(acc)
    run_slots(lists, totals, 0, (left0, left1), (right0, right1), blocks, acc)


def late_kernel(lists, totals, left0, left1, right0, right1, first, begun, acc):
    del begun
    run_slots(lists, totals, 1, (left0, left1), (right0, right1), first, acc)


def last_kernel(
    groups, lists, totals, left0, left1, right0, right1, second, begun, own, acc, keep, give
):
    del begun
    run_slots(lists, totals, 2, (left0, left1), (right0, right1), second, acc)
    core = lax.rem(lax.axis_index("ops"), 2)
    chips, width = keep.shape[0], keep.shape[2]
    share = (keep.shape[1] - NOTE) // SPARE
    energy = jnp.zeros((1, 1), F32)
    norm = jnp.zeros((1, 1), F32)
    for b in range(SPARE):
        wide = own[b].astype(F32)
        energy += jnp.sum(acc[b] * wide, keepdims=True)
        norm += jnp.sum(wide * wide, keepdims=True)
        for y in range(chips):
            for out, place in ((keep, core), (give, 1 - core)):
                start = pl.multiple_of((2 * y + place) * share, share)
                out[y, b * share:(b + 1) * share] = acc[b, pl.ds(start, share), :]
    lane = lax.broadcasted_iota(jnp.int32, (NOTE, width), 1)
    note = jnp.where(lane == 0, energy, jnp.where(lane == 1, norm / groups, 0.0))
    for y in range(chips):
        for out in (keep, give):
            out[y, SPARE * share:] = note


def chip_kernel(masks, keep, got, note, mine, *outs):
    chip = lax.axis_index("ops") // 2
    rows = mine.shape[0]
    total = keep[0, rows:, :128] + got[0, rows:, :128]
    for i in range(note.shape[0] // NOTE):
        note[i * NOTE:(i + 1) * NOTE] = total
    for mask, out in zip((0,) + masks, (mine,) + outs):
        out[...] = keep[chip ^ mask, :rows] + got[chip ^ mask, :rows]


def combine_kernel(
    left_dims, right_dims, mine, near, far, across, totals, own, diagonal, sigma, scaled, sums
):
    group_rank, holder = lax.axis_index("ops"), lax.axis_index("blk")
    blocks, share, width = sigma.shape
    whole = jnp.sum(totals[...], axis=0, keepdims=True)
    rayleigh = whole[0:1, 0:1] / whole[0:1, 1:2]
    row = lax.broadcasted_iota(jnp.int32, (share, width), 0) + group_rank * share
    column = lax.broadcasted_iota(jnp.int32, (share, width), 1)
    start = pl.multiple_of(group_rank * share, share)
    along = jnp.zeros((1, 1), F32)
    square = jnp.zeros((1, 1), F32)
    for b in range(blocks):
        ident = holder * blocks + b
        inside = (row < left_dims[ident]) & (column < right_dims[ident])
        rows = slice(b * share, (b + 1) * share)
        total = (mine[rows] + near[rows]) + (far[rows] + across[rows])
        total = jnp.where(inside, total, 0.0)
        sigma[b] = total
        state = own[b, pl.ds(start, share), :].astype(F32)
        value = (total - rayleigh * state) / jnp.maximum(jnp.abs(diagonal[b] - rayleigh), 1.0)
        scaled[b] = value
        along += jnp.sum(state * value, keepdims=True)
        square += jnp.sum(value * value, keepdims=True)
    lane = lax.broadcasted_iota(jnp.int32, sums.shape, 1)
    sums[...] = jnp.where(lane == 0, along, jnp.where(lane == 1, square, 0.0))


def finish_kernel(slots_total, arrived, totals, scaled, own, correction):
    blocks, share, width = scaled.shape
    sums = jnp.sum(arrived[...], axis=0, keepdims=True)
    along, square = sums[0:1, 0:1], sums[0:1, 1:2]
    ratio = along / jnp.sum(totals[...], axis=0, keepdims=True)[0:1, 1:2]
    length_sq = jnp.maximum(square - along * ratio, 0.0)
    factor = jnp.sqrt(length_sq / slots_total + 1e-06)
    start = pl.multiple_of(lax.axis_index("ops") * share, share)
    for b in range(blocks):
        state = own[b, pl.ds(start, share), :].astype(F32)
        correction[b] = (scaled[b] - ratio * state) / factor


def body(
    wavefunction,
    left_dims,
    right_dims,
    left_ops,
    right_ops,
    source_block,
    target_slot,
    left_index,
    right_index,
    pair_count,
    h_diagonal,
):
    groups = lax.axis_size("ops")
    holders = lax.axis_size("blk")
    own_blocks, left_width, right_width = wavefunction.shape
    share = left_width // groups
    smem = pl.BlockSpec(memory_space=pltpu.SMEM)
    vmem = pl.BlockSpec(memory_space=pltpu.VMEM)
    anywhere = pl.BlockSpec(memory_space=pl.ANY)

    def in_vmem(x):
        return pltpu.with_memory_space_constraint(x, pltpu.VMEM)

    pairs = [(i, i ^ 1) for i in range(groups)]
    alive = lax.broadcasted_iota(jnp.int32, target_slot.shape, 1) < pair_count
    tables = jnp.stack(
        [source_block, jnp.where(alive, target_slot, SPARE), left_index, right_index], axis=1
    )
    tables_other = lax.ppermute(tables, "ops", pairs)

    def exchange(x, mask):
        return lax.ppermute(
            x,
            ("ops", "blk"),
            [
                (g * holders + h, g * holders + (h ^ mask[g % 2]))
                for g in range(groups)
                for h in range(holders)
            ],
        )

    block = jax.ShapeDtypeStruct((1, left_width, right_width), BF16)
    first, second = pl.pallas_call(
        pick_kernel,
        out_shape=(block, block),
        in_specs=[pl.BlockSpec(memory_space=pltpu.HBM)],
        out_specs=(vmem, vmem),
        scratch_shapes=[pltpu.SemaphoreType.DMA((2,))],
        compiler_params=pltpu.CompilerParams(vmem_limit_bytes=2**20),
        name="pick",
    )(pltpu.with_memory_space_constraint(wavefunction, pltpu.HBM))
    first, left_here, right_here = lax.optimization_barrier((first, left_ops, right_ops))
    left_other = lax.ppermute(left_here, "ops", pairs)
    right_other = lax.ppermute(right_here, "ops", pairs)
    for step, (one, two) in enumerate(zip(*MASKS)):
        first_new, second_new = exchange(first, one), exchange(second, two)
        if step == 1:
            second_new, tables_other = lax.optimization_barrier((second_new, tables_other))
            lists, totals = pl.pallas_call(
                place_kernel,
                out_shape=(
                    jax.ShapeDtypeStruct((1, KINDS * LIST + 1), jnp.int32),
                    jax.ShapeDtypeStruct((1, KINDS), jnp.int32),
                ),
                in_specs=[vmem, vmem],
                out_specs=(smem, smem),
                scratch_shapes=[
                    pltpu.VMEM((2, 8, tables.shape[2]), jnp.int32),
                    pltpu.SMEM((2, 8, tables.shape[2]), jnp.int32),
                    pltpu.SemaphoreType.DMA((1,)),
                ],
                compiler_params=pltpu.CompilerParams(vmem_limit_bytes=2 * 2**20),
                name="place",
                cost_estimate=pl.CostEstimate(
                    flops=10**9, bytes_accessed=10**4, transcendentals=0
                ),
            )(tables, tables_other)
        if step == 2:
            first_new, lists, totals = lax.optimization_barrier((first_new, lists, totals))
        if step < 3:
            first = jnp.concatenate([first, first_new])
            second = jnp.concatenate([second, second_new])

    stores = [in_vmem(x) for x in (left_ops, left_other, right_ops, right_other)]
    partial_shape = (own_blocks + 1, left_width, right_width)
    half_blocks = pltpu.VMEM((2,) + first.shape, BF16)
    begun = pl.pallas_call(
        early_kernel,
        out_shape=jax.ShapeDtypeStruct(partial_shape, F32),
        in_specs=[smem, smem] + [vmem] * 4 + [anywhere] * 2,
        out_specs=vmem,
        scratch_shapes=[half_blocks, pltpu.SemaphoreType.DMA((2,))],
        compiler_params=pltpu.CompilerParams(vmem_limit_bytes=6 * 2**20),
        name="early",
        cost_estimate=pl.CostEstimate(flops=8 * 10**9, bytes_accessed=10**6, transcendentals=0),
    )(lists, totals, *stores, first, second)
    chips = groups // 2
    begun = pl.pallas_call(
        late_kernel,
        out_shape=jax.ShapeDtypeStruct(partial_shape, F32),
        in_specs=[smem, smem] + [vmem] * 6,
        out_specs=vmem,
        input_output_aliases={7: 0},
        compiler_params=pltpu.CompilerParams(vmem_limit_bytes=6 * 2**20),
        name="late",
        cost_estimate=pl.CostEstimate(flops=2 * 10**9, bytes_accessed=10**6, transcendentals=0),
    )(lists, totals, *stores, first_new, begun)
    halves = jax.ShapeDtypeStruct((chips, own_blocks * share + NOTE, right_width), F32)
    _, keep, give = pl.pallas_call(
        functools.partial(last_kernel, groups),
        out_shape=(jax.ShapeDtypeStruct(partial_shape, F32), halves, halves),
        in_specs=[smem, smem] + [vmem] * 7,
        out_specs=(vmem,) * 3,
        input_output_aliases={7: 0},
        compiler_params=pltpu.CompilerParams(vmem_limit_bytes=6 * 2**20),
        name="last",
        cost_estimate=pl.CostEstimate(flops=2 * 10**9, bytes_accessed=10**6, transcendentals=0),
    )(lists, totals, *stores, second_new, begun, wavefunction)
    got = lax.ppermute(give, "ops", pairs)
    chip_masks = (1, 3, 2)
    chip_sum = jax.ShapeDtypeStruct((own_blocks * share, right_width), F32)
    note, mine, *outgoing = pl.pallas_call(
        functools.partial(chip_kernel, chip_masks),
        out_shape=(jax.ShapeDtypeStruct((holders, 128), F32),) + (chip_sum,) * 4,
        in_specs=[vmem, vmem],
        out_specs=(vmem,) * 5,
        compiler_params=pltpu.CompilerParams(vmem_limit_bytes=4 * 2**20),
        name="chip_sum",
    )(keep, got)

    def along_y(x, mask):
        return lax.ppermute(x, "ops", [(i, i ^ (2 * mask)) for i in range(groups)])

    notes = [note] + [along_y(note, mask) for mask in chip_masks]
    arrived = [along_y(x, mask) for x, mask in zip(outgoing, chip_masks)]
    first_sums = lax.all_to_all(
        (notes[0] + notes[1]) + (notes[2] + notes[3]), "blk", 0, 0, tiled=True
    )
    devices = groups * holders
    row_sums = jax.ShapeDtypeStruct((devices, 128), F32)
    shard = jax.ShapeDtypeStruct((own_blocks, share, right_width), F32)
    sigma_vector, scaled, second_sums = pl.pallas_call(
        combine_kernel,
        out_shape=(shard, shard, row_sums),
        in_specs=[smem, smem] + [vmem] * 7,
        out_specs=(vmem, vmem, vmem),
        compiler_params=pltpu.CompilerParams(vmem_limit_bytes=4 * 2**20),
        name="combine",
    )(left_dims, right_dims, mine, *arrived, first_sums, wavefunction, h_diagonal)
    second_sums = lax.all_to_all(second_sums, ("ops", "blk"), 0, 0, tiled=True)
    correction = pl.pallas_call(
        functools.partial(finish_kernel, left_dims.shape[0] * left_width * right_width),
        out_shape=shard,
        in_specs=[vmem, vmem, vmem, vmem],
        out_specs=vmem,
        compiler_params=pltpu.CompilerParams(vmem_limit_bytes=4 * 2**20),
        name="finish",
    )(second_sums, first_sums, scaled, wavefunction)
    return (sigma_vector, correction)


def solution(mesh):
    in_specs = (
        P("blk", None, None),
        P(),
        P(),
        P("ops", "blk", None, None),
        P("ops", "blk", None, None),
        P("ops", "blk"),
        P("ops", "blk"),
        P("ops", "blk"),
        P("ops", "blk"),
        P("ops", "blk"),
        P("blk", "ops", None),
    )
    out_specs = (P("blk", "ops", None), P("blk", "ops", None))
    return jax.shard_map(body, mesh=mesh, in_specs=in_specs, out_specs=out_specs, check_vma=False)
```

```python
import functools

import jax
import jax.numpy as jnp
from jax import lax
from jax.experimental import pallas as pl
from jax.experimental.pallas import tpu as pltpu
from jax.sharding import PartitionSpec as P

UNROLL = 16
TAIL = 4
LIST = 528
SPARE = 4
KINDS = 4
NOTE = 8
LEFT, RIGHT, TARGET, GROUP = 4, 9, 14, 17
MASKS = (((1, 3), (3, 1), (4, 12), (12, 4)), ((4, 12), (12, 4), (1, 3), (3, 1)))
F32 = jnp.float32
BF16 = jnp.bfloat16


def run_copies(copies):
    for copy in copies:
        copy.start()
    for copy in copies:
        copy.wait()


def pick_kernel(own, first, second, sems):
    core = lax.rem(lax.axis_index("ops"), 2)
    run_copies([
        pltpu.make_async_copy(own.at[pl.ds(2 * core + i, 1)], target, sems.at[i])
        for i, target in enumerate((first, second))
    ])


def place_kernel(tables, other, lists, totals, staged, scalars, sems):
    core = lax.rem(lax.axis_index("ops"), 2)
    holder = lax.axis_index("blk")
    slots = tables.shape[2]

    def code(bits):
        gray = bits ^ (bits >> 1)
        return jnp.where(core == 0, gray, ((gray & 1) << 1) | (gray >> 1))

    row = lax.broadcasted_iota(jnp.int32, (8, slots), 0)
    earlier = lax.broadcasted_iota(jnp.int32, (slots, slots), 0)
    later = lax.broadcasted_iota(jnp.int32, (slots, slots), 1)
    ahead = jnp.where(earlier <= later, 1.0, 0.0).astype(BF16)
    before = jnp.zeros((8, 1), jnp.int32)
    lives = []
    for group, table in enumerate((tables, other)):
        block, target = table[0, 0:1, :], table[0, 1:2, :]
        away, within = (block >> 2) ^ holder, block & 3
        along_x, along_z = code(away & 3), code(away >> 2)
        stream = within & 1
        entry = jnp.where(stream == 0, along_x | (along_z << 2), along_z | (along_x << 2))
        kind = jnp.where(entry == 0, 0, jnp.where(entry < 8, 1, 2 + stream))
        kind = jnp.where(((within >> 1) == core) & (target < SPARE), kind, KINDS)
        word = (
            (entry & 7)
            | (stream << 3)
            | (table[0, 2:3, :] << LEFT)
            | (table[0, 3:4, :] << RIGHT)
            | (target << TARGET)
            | (group << GROUP)
        )
        chosen = row == kind
        counts = jnp.dot(
            jnp.where(chosen, 1.0, 0.0).astype(BF16), ahead, preferred_element_type=F32
        ).astype(jnp.int32)
        where = jnp.where(chosen, counts - 1 + row * LIST + before, 0)
        where = jnp.where(kind < KINDS, jnp.sum(where[:KINDS], axis=0, keepdims=True), KINDS * LIST)
        before = counts[:, slots - 1:]
        staged[group] = jnp.where(row < KINDS, counts, jnp.where(row == KINDS, word, where))
        lives.append(jnp.sum(jnp.where(target < SPARE, 1, 0)))
    run_copies([pltpu.make_async_copy(staged, scalars, sems.at[0])])
    for group in range(2):

        def places(i, carry, group=group):
            for u in range(16):
                lists[0, scalars[group, KINDS + 1, 16 * i + u]] = scalars[group, KINDS, 16 * i + u]
            return carry

        lax.fori_loop(0, (lives[group] + 15) // 16, places, 0)
    for i in range(KINDS):
        length = scalars[0, i, slots - 1] + scalars[1, i, slots - 1]
        totals[0, i] = length
        for u in range(UNROLL):
            lists[0, i * LIST + length + u] = SPARE << TARGET


def run_slots(lists, totals, which, lefts, rights, blocks, acc):
    def many(i, carry, width, offset):
        for u in range(width):
            word = lists[0, offset + i * width + u]
            own = (word >> GROUP) == 0
            left, right = (word >> LEFT) & 31, (word >> RIGHT) & 31
            psi = blocks[(word >> 3) & 1, word & 7] if which < 2 else blocks[word & 7]
            product = jnp.dot(
                jnp.where(own, lefts[0][0, left], lefts[1][0, left]), psi,
                preferred_element_type=F32,
            ).astype(BF16)
            acc[(word >> TARGET) & 7] += lax.dot_general(
                product, jnp.where(own, rights[0][0, right], rights[1][0, right]),
                (((1,), (1,)), ((), ())), preferred_element_type=F32,
            )
        return carry

    live, base = totals[0, which], which * LIST
    turns = (live + UNROLL - 1 - 2 * TAIL) // UNROLL
    lax.fori_loop(0, turns, functools.partial(many, width=UNROLL, offset=base), 0)
    rest = jnp.maximum(live - turns * UNROLL, 0)
    lax.fori_loop(
        0,
        (rest + TAIL - 1) // TAIL,
        functools.partial(many, width=TAIL, offset=base + turns * UNROLL),
        0,
    )


def slots_kernel(which, lists, totals, left0, left1, right0, right1, first, second, *rest):
    acc, blocks, sems = rest[-3:]
    copies = [
        pltpu.make_async_copy(piece, blocks.at[i], sems.at[i])
        for i, piece in enumerate((first, second))
    ]
    for copy in copies:
        copy.start()
    if which == 0:
        acc[...] = jnp.zeros_like(acc)
    for copy in copies:
        copy.wait()
    run_slots(lists, totals, which, (left0, left1), (right0, right1), blocks, acc)


def late_kernel(lists, totals, left0, left1, right0, right1, first, begun, acc):
    del begun
    run_slots(lists, totals, 2, (left0, left1), (right0, right1), first, acc)


def last_kernel(
    groups, lists, totals, left0, left1, right0, right1, second, begun, own, acc, keep, give
):
    del begun
    run_slots(lists, totals, 3, (left0, left1), (right0, right1), second, acc)
    core = lax.rem(lax.axis_index("ops"), 2)
    chips, width = keep.shape[0], keep.shape[2]
    share = (keep.shape[1] - NOTE) // SPARE
    energy = jnp.zeros((1, 1), F32)
    norm = jnp.zeros((1, 1), F32)
    for b in range(SPARE):
        wide = own[b].astype(F32)
        energy += jnp.sum(acc[b] * wide, keepdims=True)
        norm += jnp.sum(wide * wide, keepdims=True)
        for y in range(chips):
            for out, place in ((keep, core), (give, 1 - core)):
                start = pl.multiple_of((2 * y + place) * share, share)
                out[y, b * share:(b + 1) * share] = acc[b, pl.ds(start, share), :]
    lane = lax.broadcasted_iota(jnp.int32, (NOTE, width), 1)
    note = jnp.where(lane == 0, energy, jnp.where(lane == 1, norm / groups, 0.0))
    for y in range(chips):
        for out in (keep, give):
            out[y, SPARE * share:] = note


def chip_kernel(masks, keep, got, note, mine, *outs):
    chip = lax.axis_index("ops") // 2
    rows = mine.shape[0]
    total = keep[0, rows:, :128] + got[0, rows:, :128]
    for i in range(note.shape[0] // NOTE):
        note[i * NOTE:(i + 1) * NOTE] = total
    for mask, out in zip((0,) + masks, (mine,) + outs):
        out[...] = keep[chip ^ mask, :rows] + got[chip ^ mask, :rows]


def combine_kernel(
    left_dims, right_dims, mine, near, far, across, totals, own, diagonal, sigma, scaled, sums
):
    group_rank, holder = lax.axis_index("ops"), lax.axis_index("blk")
    blocks, share, width = sigma.shape
    whole = jnp.sum(totals[...], axis=0, keepdims=True)
    rayleigh = whole[0:1, 0:1] / whole[0:1, 1:2]
    row = lax.broadcasted_iota(jnp.int32, (share, width), 0) + group_rank * share
    column = lax.broadcasted_iota(jnp.int32, (share, width), 1)
    start = pl.multiple_of(group_rank * share, share)
    along = jnp.zeros((1, 1), F32)
    square = jnp.zeros((1, 1), F32)
    for b in range(blocks):
        ident = holder * blocks + b
        inside = (row < left_dims[ident]) & (column < right_dims[ident])
        rows = slice(b * share, (b + 1) * share)
        total = (mine[rows] + near[rows]) + (far[rows] + across[rows])
        total = jnp.where(inside, total, 0.0)
        sigma[b] = total
        state = own[b, pl.ds(start, share), :].astype(F32)
        value = (total - rayleigh * state) / jnp.maximum(jnp.abs(diagonal[b] - rayleigh), 1.0)
        scaled[b] = value
        along += jnp.sum(state * value, keepdims=True)
        square += jnp.sum(value * value, keepdims=True)
    lane = lax.broadcasted_iota(jnp.int32, sums.shape, 1)
    sums[...] = jnp.where(lane == 0, along, jnp.where(lane == 1, square, 0.0))


def finish_kernel(slots_total, arrived, totals, scaled, own, correction):
    blocks, share, width = scaled.shape
    sums = jnp.sum(arrived[...], axis=0, keepdims=True)
    along, square = sums[0:1, 0:1], sums[0:1, 1:2]
    ratio = along / jnp.sum(totals[...], axis=0, keepdims=True)[0:1, 1:2]
    length_sq = jnp.maximum(square - along * ratio, 0.0)
    factor = jnp.sqrt(length_sq / slots_total + 1e-06)
    start = pl.multiple_of(lax.axis_index("ops") * share, share)
    for b in range(blocks):
        state = own[b, pl.ds(start, share), :].astype(F32)
        correction[b] = (scaled[b] - ratio * state) / factor


def body(
    wavefunction,
    left_dims,
    right_dims,
    left_ops,
    right_ops,
    source_block,
    target_slot,
    left_index,
    right_index,
    pair_count,
    h_diagonal,
):
    groups = lax.axis_size("ops")
    holders = lax.axis_size("blk")
    own_blocks, left_width, right_width = wavefunction.shape
    share = left_width // groups
    smem = pl.BlockSpec(memory_space=pltpu.SMEM)
    vmem = pl.BlockSpec(memory_space=pltpu.VMEM)
    anywhere = pl.BlockSpec(memory_space=pl.ANY)

    def in_vmem(x):
        return pltpu.with_memory_space_constraint(x, pltpu.VMEM)

    pairs = [(i, i ^ 1) for i in range(groups)]
    alive = lax.broadcasted_iota(jnp.int32, target_slot.shape, 1) < pair_count
    tables = jnp.stack(
        [source_block, jnp.where(alive, target_slot, SPARE), left_index, right_index], axis=1
    )

    def exchange(x, mask):
        return lax.ppermute(
            x,
            ("ops", "blk"),
            [
                (g * holders + h, g * holders + (h ^ mask[g % 2]))
                for g in range(groups)
                for h in range(holders)
            ],
        )

    block = jax.ShapeDtypeStruct((1, left_width, right_width), BF16)
    first, second = pl.pallas_call(
        pick_kernel,
        out_shape=(block, block),
        in_specs=[pl.BlockSpec(memory_space=pltpu.HBM)],
        out_specs=(vmem, vmem),
        scratch_shapes=[pltpu.SemaphoreType.DMA((2,))],
        compiler_params=pltpu.CompilerParams(vmem_limit_bytes=2**20),
        name="pick",
    )(pltpu.with_memory_space_constraint(wavefunction, pltpu.HBM))
    first, left_here, right_here = lax.optimization_barrier((first, left_ops, right_ops))
    left_other = lax.ppermute(left_here, "ops", pairs)
    right_other = lax.ppermute(right_here, "ops", pairs)
    stores = [in_vmem(x) for x in (left_ops, left_other, right_ops, right_other)]
    partial_shape = (own_blocks + 1, left_width, right_width)

    def slots_call(which, gathered, begun, flops):
        return pl.pallas_call(
            functools.partial(slots_kernel, which),
            out_shape=jax.ShapeDtypeStruct(partial_shape, F32),
            in_specs=[smem, smem] + [vmem] * 4 + [anywhere] * 2 + [vmem] * len(begun),
            out_specs=vmem,
            input_output_aliases={8: 0} if begun else {},
            scratch_shapes=[
                pltpu.VMEM((2,) + gathered[0].shape, BF16), pltpu.SemaphoreType.DMA((2,)),
            ],
            compiler_params=pltpu.CompilerParams(vmem_limit_bytes=6 * 2**20),
            name=("near", "early")[which],
            cost_estimate=pl.CostEstimate(flops=flops, bytes_accessed=10**6, transcendentals=0),
        )(lists, totals, *stores, *gathered, *begun)

    near = (first, second)
    for step, (one, two) in enumerate(zip(*MASKS)):
        first_new, second_new = exchange(first, one), exchange(second, two)
        if step == 0:
            tables_here, _, _ = lax.optimization_barrier((tables, first_new, second_new))
            tables_other = lax.ppermute(tables_here, "ops", pairs)
        if step == 1:
            tables_other, _ = lax.optimization_barrier((tables_other, second_new))
            lists, totals = pl.pallas_call(
                place_kernel,
                out_shape=(
                    jax.ShapeDtypeStruct((1, KINDS * LIST + 1), jnp.int32),
                    jax.ShapeDtypeStruct((1, KINDS), jnp.int32),
                ),
                in_specs=[vmem, vmem],
                out_specs=(smem, smem),
                scratch_shapes=[
                    pltpu.VMEM((2, 8, tables.shape[2]), jnp.int32),
                    pltpu.SMEM((2, 8, tables.shape[2]), jnp.int32),
                    pltpu.SemaphoreType.DMA((1,)),
                ],
                compiler_params=pltpu.CompilerParams(vmem_limit_bytes=2 * 2**20),
                name="place",
                cost_estimate=pl.CostEstimate(
                    flops=10**9, bytes_accessed=10**4, transcendentals=0
                ),
            )(tables, tables_other)
        if step == 2:
            near_sums = slots_call(0, near, (), 2 * 10**9)
            first_new, begun = lax.optimization_barrier((first_new, near_sums))
        if step < 3:
            first = jnp.concatenate([first, first_new])
            second = jnp.concatenate([second, second_new])

    begun = slots_call(1, (first, second), (begun,), 6 * 10**9)
    chips = groups // 2
    begun = pl.pallas_call(
        late_kernel,
        out_shape=jax.ShapeDtypeStruct(partial_shape, F32),
        in_specs=[smem, smem] + [vmem] * 6,
        out_specs=vmem,
        input_output_aliases={7: 0},
        compiler_params=pltpu.CompilerParams(vmem_limit_bytes=6 * 2**20),
        name="late",
        cost_estimate=pl.CostEstimate(flops=2 * 10**9, bytes_accessed=10**6, transcendentals=0),
    )(lists, totals, *stores, first_new, begun)
    halves = jax.ShapeDtypeStruct((chips, own_blocks * share + NOTE, right_width), F32)
    _, keep, give = pl.pallas_call(
        functools.partial(last_kernel, groups),
        out_shape=(jax.ShapeDtypeStruct(partial_shape, F32), halves, halves),
        in_specs=[smem, smem] + [vmem] * 7,
        out_specs=(vmem,) * 3,
        input_output_aliases={7: 0},
        compiler_params=pltpu.CompilerParams(vmem_limit_bytes=6 * 2**20),
        name="last",
        cost_estimate=pl.CostEstimate(flops=2 * 10**9, bytes_accessed=10**6, transcendentals=0),
    )(lists, totals, *stores, second_new, begun, wavefunction)
    got = lax.ppermute(give, "ops", pairs)
    chip_masks = (1, 3, 2)
    chip_sum = jax.ShapeDtypeStruct((own_blocks * share, right_width), F32)
    note, mine, *outgoing = pl.pallas_call(
        functools.partial(chip_kernel, chip_masks),
        out_shape=(jax.ShapeDtypeStruct((holders, 128), F32),) + (chip_sum,) * 4,
        in_specs=[vmem, vmem],
        out_specs=(vmem,) * 5,
        compiler_params=pltpu.CompilerParams(vmem_limit_bytes=4 * 2**20),
        name="chip_sum",
    )(keep, got)

    def along_y(x, mask):
        return lax.ppermute(x, "ops", [(i, i ^ (2 * mask)) for i in range(groups)])

    notes = [note] + [along_y(note, mask) for mask in chip_masks]
    arrived = [along_y(x, mask) for x, mask in zip(outgoing, chip_masks)]
    first_sums = lax.all_to_all(
        (notes[0] + notes[1]) + (notes[2] + notes[3]), "blk", 0, 0, tiled=True
    )
    devices = groups * holders
    row_sums = jax.ShapeDtypeStruct((devices, 128), F32)
    shard = jax.ShapeDtypeStruct((own_blocks, share, right_width), F32)
    sigma_vector, scaled, second_sums = pl.pallas_call(
        combine_kernel,
        out_shape=(shard, shard, row_sums),
        in_specs=[smem, smem] + [vmem] * 7,
        out_specs=(vmem, vmem, vmem),
        compiler_params=pltpu.CompilerParams(vmem_limit_bytes=4 * 2**20),
        name="combine",
    )(left_dims, right_dims, mine, *arrived, first_sums, wavefunction, h_diagonal)
    second_sums = lax.all_to_all(second_sums, ("ops", "blk"), 0, 0, tiled=True)
    correction = pl.pallas_call(
        functools.partial(finish_kernel, left_dims.shape[0] * left_width * right_width),
        out_shape=shard,
        in_specs=[vmem, vmem, vmem, vmem],
        out_specs=vmem,
        compiler_params=pltpu.CompilerParams(vmem_limit_bytes=4 * 2**20),
        name="finish",
    )(second_sums, first_sums, scaled, wavefunction)
    return (sigma_vector, correction)


def solution(mesh):
    in_specs = (
        P("blk", None, None),
        P(),
        P(),
        P("ops", "blk", None, None),
        P("ops", "blk", None, None),
        P("ops", "blk"),
        P("ops", "blk"),
        P("ops", "blk"),
        P("ops", "blk"),
        P("ops", "blk"),
        P("blk", "ops", None),
    )
    out_specs = (P("blk", "ops", None), P("blk", "ops", None))
    return jax.shard_map(body, mesh=mesh, in_specs=in_specs, out_specs=out_specs, check_vma=False)
```

```python
import functools

import jax
import jax.numpy as jnp
from jax import lax
from jax.experimental import pallas as pl
from jax.experimental.pallas import tpu as pltpu
from jax.sharding import PartitionSpec as P

UNROLL = 16
TAIL = 4
LIST = 528
SPARE = 4
KINDS = 3
NOTE = 8
LEFT, RIGHT, TARGET, GROUP = 4, 9, 14, 17
MASKS = (((1, 3), (3, 1), (4, 12), (12, 4)), ((4, 12), (12, 4), (1, 3), (3, 1)))
F32 = jnp.float32
BF16 = jnp.bfloat16


def run_copies(copies):
    for copy in copies:
        copy.start()
    for copy in copies:
        copy.wait()


def pick_kernel(own, first, second, sems):
    core = lax.rem(lax.axis_index("ops"), 2)
    run_copies([
        pltpu.make_async_copy(own.at[pl.ds(2 * core + i, 1)], target, sems.at[i])
        for i, target in enumerate((first, second))
    ])


def place_kernel(tables, other, lists, totals, staged, scalars, sems):
    core = lax.rem(lax.axis_index("ops"), 2)
    holder = lax.axis_index("blk")
    slots = tables.shape[2]

    def code(bits):
        gray = bits ^ (bits >> 1)
        return jnp.where(core == 0, gray, ((gray & 1) << 1) | (gray >> 1))

    row = lax.broadcasted_iota(jnp.int32, (8, slots), 0)
    earlier = lax.broadcasted_iota(jnp.int32, (slots, slots), 0)
    later = lax.broadcasted_iota(jnp.int32, (slots, slots), 1)
    ahead = jnp.where(earlier <= later, 1.0, 0.0).astype(BF16)
    before = jnp.zeros((8, 1), jnp.int32)
    lives = []
    for group, table in enumerate((tables, other)):
        block, target = table[0, 0:1, :], table[0, 1:2, :]
        away, within = (block >> 2) ^ holder, block & 3
        along_x, along_z = code(away & 3), code(away >> 2)
        stream = within & 1
        entry = jnp.where(stream == 0, along_x | (along_z << 2), along_z | (along_x << 2))
        kind = jnp.where(entry < 8, 0, 1 + stream)
        kind = jnp.where(((within >> 1) == core) & (target < SPARE), kind, KINDS)
        word = (
            (entry & 7)
            | (stream << 3)
            | (table[0, 2:3, :] << LEFT)
            | (table[0, 3:4, :] << RIGHT)
            | (target << TARGET)
            | (group << GROUP)
        )
        chosen = row == kind
        counts = jnp.dot(
            jnp.where(chosen, 1.0, 0.0).astype(BF16), ahead, preferred_element_type=F32
        ).astype(jnp.int32)
        where = jnp.where(chosen, counts - 1 + row * LIST + before, 0)
        where = jnp.where(kind < KINDS, jnp.sum(where[:KINDS], axis=0, keepdims=True), KINDS * LIST)
        before = counts[:, slots - 1:]
        staged[group] = jnp.where(row < KINDS, counts, jnp.where(row == KINDS, word, where))
        lives.append(jnp.sum(jnp.where(target < SPARE, 1, 0)))
    run_copies([pltpu.make_async_copy(staged, scalars, sems.at[0])])
    for group in range(2):

        def places(i, carry, group=group):
            for u in range(16):
                lists[0, scalars[group, KINDS + 1, 16 * i + u]] = scalars[group, KINDS, 16 * i + u]
            return carry

        lax.fori_loop(0, (lives[group] + 15) // 16, places, 0)
    for i in range(KINDS):
        length = scalars[0, i, slots - 1] + scalars[1, i, slots - 1]
        totals[0, i] = length
        for u in range(UNROLL):
            lists[0, i * LIST + length + u] = SPARE << TARGET


def run_slots(lists, totals, which, lefts, rights, blocks, acc):
    def many(i, carry, width, offset):
        for u in range(width):
            word = lists[0, offset + i * width + u]
            own = (word >> GROUP) == 0
            left, right = (word >> LEFT) & 31, (word >> RIGHT) & 31
            psi = blocks[(word >> 3) & 1, word & 7] if which == 0 else blocks[word & 7]
            product = jnp.dot(
                jnp.where(own, lefts[0][0, left], lefts[1][0, left]), psi,
                preferred_element_type=F32,
            ).astype(BF16)
            acc[(word >> TARGET) & 7] += lax.dot_general(
                product, jnp.where(own, rights[0][0, right], rights[1][0, right]),
                (((1,), (1,)), ((), ())), preferred_element_type=F32,
            )
        return carry

    done, left_over = which * LIST, totals[0, which]
    for width, slack in ((2 * UNROLL, 7), (UNROLL, 7), (TAIL, TAIL - 1)):
        turns = (left_over + slack) // width
        lax.fori_loop(0, turns, functools.partial(many, width=width, offset=done), 0)
        done += turns * width
        left_over = jnp.maximum(left_over - turns * width, 0)


def early_kernel(lists, totals, left0, left1, right0, right1, first, second, acc, blocks, sems):
    run_copies([
        pltpu.make_async_copy(piece, blocks.at[i], sems.at[i])
        for i, piece in enumerate((first, second))
    ])
    acc[...] = jnp.zeros_like(acc)
    run_slots(lists, totals, 0, (left0, left1), (right0, right1), blocks, acc)


def late_kernel(lists, totals, left0, left1, right0, right1, first, begun, acc):
    del begun
    run_slots(lists, totals, 1, (left0, left1), (right0, right1), first, acc)


def last_kernel(
    groups, lists, totals, left0, left1, right0, right1, second, begun, own, acc, keep, give
):
    del begun
    run_slots(lists, totals, 2, (left0, left1), (right0, right1), second, acc)
    core = lax.rem(lax.axis_index("ops"), 2)
    chips, width = keep.shape[0], keep.shape[2]
    share = (keep.shape[1] - NOTE) // SPARE
    energy = jnp.zeros((1, 1), F32)
    norm = jnp.zeros((1, 1), F32)
    for b in range(SPARE):
        wide = own[b].astype(F32)
        energy += jnp.sum(acc[b] * wide, keepdims=True)
        norm += jnp.sum(wide * wide, keepdims=True)
        for y in range(chips):
            for out, place in ((keep, core), (give, 1 - core)):
                start = pl.multiple_of((2 * y + place) * share, share)
                out[y, b * share:(b + 1) * share] = acc[b, pl.ds(start, share), :]
    lane = lax.broadcasted_iota(jnp.int32, (NOTE, width), 1)
    note = jnp.where(lane == 0, energy, jnp.where(lane == 1, norm / groups, 0.0))
    for y in range(chips):
        for out in (keep, give):
            out[y, SPARE * share:] = note


def chip_kernel(masks, keep, got, note, mine, *outs):
    chip = lax.axis_index("ops") // 2
    rows = mine.shape[0]
    total = keep[0, rows:, :128] + got[0, rows:, :128]
    for i in range(note.shape[0] // NOTE):
        note[i * NOTE:(i + 1) * NOTE] = total
    for mask, out in zip((0,) + masks, (mine,) + outs):
        out[...] = keep[chip ^ mask, :rows] + got[chip ^ mask, :rows]


def combine_kernel(
    left_dims, right_dims, mine, near, far, across, totals, own, diagonal, sigma, scaled, sums
):
    group_rank, holder = lax.axis_index("ops"), lax.axis_index("blk")
    blocks, share, width = sigma.shape
    whole = jnp.sum(totals[...], axis=0, keepdims=True)
    rayleigh = whole[0:1, 0:1] / whole[0:1, 1:2]
    row = lax.broadcasted_iota(jnp.int32, (share, width), 0) + group_rank * share
    column = lax.broadcasted_iota(jnp.int32, (share, width), 1)
    start = pl.multiple_of(group_rank * share, share)
    along = jnp.zeros((1, 1), F32)
    square = jnp.zeros((1, 1), F32)
    for b in range(blocks):
        ident = holder * blocks + b
        inside = (row < left_dims[ident]) & (column < right_dims[ident])
        rows = slice(b * share, (b + 1) * share)
        total = (mine[rows] + near[rows]) + (far[rows] + across[rows])
        total = jnp.where(inside, total, 0.0)
        sigma[b] = total
        state = own[b, pl.ds(start, share), :].astype(F32)
        value = (total - rayleigh * state) / jnp.maximum(jnp.abs(diagonal[b] - rayleigh), 1.0)
        scaled[b] = value
        along += jnp.sum(state * value, keepdims=True)
        square += jnp.sum(value * value, keepdims=True)
    lane = lax.broadcasted_iota(jnp.int32, sums.shape, 1)
    sums[...] = jnp.where(lane == 0, along, jnp.where(lane == 1, square, 0.0))


def finish_kernel(slots_total, arrived, totals, scaled, own, correction):
    blocks, share, width = scaled.shape
    sums = jnp.sum(arrived[...], axis=0, keepdims=True)
    along, square = sums[0:1, 0:1], sums[0:1, 1:2]
    ratio = along / jnp.sum(totals[...], axis=0, keepdims=True)[0:1, 1:2]
    length_sq = jnp.maximum(square - along * ratio, 0.0)
    factor = jnp.sqrt(length_sq / slots_total + 1e-06)
    start = pl.multiple_of(lax.axis_index("ops") * share, share)
    for b in range(blocks):
        state = own[b, pl.ds(start, share), :].astype(F32)
        correction[b] = (scaled[b] - ratio * state) / factor


def body(
    wavefunction,
    left_dims,
    right_dims,
    left_ops,
    right_ops,
    source_block,
    target_slot,
    left_index,
    right_index,
    pair_count,
    h_diagonal,
):
    groups = lax.axis_size("ops")
    holders = lax.axis_size("blk")
    own_blocks, left_width, right_width = wavefunction.shape
    share = left_width // groups
    smem = pl.BlockSpec(memory_space=pltpu.SMEM)
    vmem = pl.BlockSpec(memory_space=pltpu.VMEM)
    anywhere = pl.BlockSpec(memory_space=pl.ANY)

    def in_vmem(x):
        return pltpu.with_memory_space_constraint(x, pltpu.VMEM)

    pairs = [(i, i ^ 1) for i in range(groups)]
    alive = lax.broadcasted_iota(jnp.int32, target_slot.shape, 1) < pair_count
    tables = jnp.stack(
        [source_block, jnp.where(alive, target_slot, SPARE), left_index, right_index], axis=1
    )
    tables_other = lax.ppermute(tables, "ops", pairs)

    def exchange(x, mask):
        return lax.ppermute(
            x,
            ("ops", "blk"),
            [
                (g * holders + h, g * holders + (h ^ mask[g % 2]))
                for g in range(groups)
                for h in range(holders)
            ],
        )

    block = jax.ShapeDtypeStruct((1, left_width, right_width), BF16)
    first, second = pl.pallas_call(
        pick_kernel,
        out_shape=(block, block),
        in_specs=[pl.BlockSpec(memory_space=pltpu.HBM)],
        out_specs=(vmem, vmem),
        scratch_shapes=[pltpu.SemaphoreType.DMA((2,))],
        compiler_params=pltpu.CompilerParams(vmem_limit_bytes=2**20),
        name="pick",
    )(pltpu.with_memory_space_constraint(wavefunction, pltpu.HBM))
    first, left_here, right_here = lax.optimization_barrier((first, left_ops, right_ops))
    left_other = lax.ppermute(left_here, "ops", pairs)
    right_other = lax.ppermute(right_here, "ops", pairs)
    for step, (one, two) in enumerate(zip(*MASKS)):
        first_new, second_new = exchange(first, one), exchange(second, two)
        if step == 1:
            second_new, tables_other = lax.optimization_barrier((second_new, tables_other))
            lists, totals = pl.pallas_call(
                place_kernel,
                out_shape=(
                    jax.ShapeDtypeStruct((1, KINDS * LIST + 1), jnp.int32),
                    jax.ShapeDtypeStruct((1, KINDS), jnp.int32),
                ),
                in_specs=[vmem, vmem],
                out_specs=(smem, smem),
                scratch_shapes=[
                    pltpu.VMEM((2, 8, tables.shape[2]), jnp.int32),
                    pltpu.SMEM((2, 8, tables.shape[2]), jnp.int32),
                    pltpu.SemaphoreType.DMA((1,)),
                ],
                compiler_params=pltpu.CompilerParams(vmem_limit_bytes=2 * 2**20),
                name="place",
                cost_estimate=pl.CostEstimate(
                    flops=10**9, bytes_accessed=10**4, transcendentals=0
                ),
            )(tables, tables_other)
        if step == 2:
            first_new, lists, totals = lax.optimization_barrier((first_new, lists, totals))
        if step < 3:
            first = jnp.concatenate([first, first_new])
            second = jnp.concatenate([second, second_new])

    stores = [in_vmem(x) for x in (left_ops, left_other, right_ops, right_other)]
    partial_shape = (own_blocks + 1, left_width, right_width)
    half_blocks = pltpu.VMEM((2,) + first.shape, BF16)
    begun = pl.pallas_call(
        early_kernel,
        out_shape=jax.ShapeDtypeStruct(partial_shape, F32),
        in_specs=[smem, smem] + [vmem] * 4 + [anywhere] * 2,
        out_specs=vmem,
        scratch_shapes=[half_blocks, pltpu.SemaphoreType.DMA((2,))],
        compiler_params=pltpu.CompilerParams(vmem_limit_bytes=6 * 2**20),
        name="early",
        cost_estimate=pl.CostEstimate(flops=8 * 10**9, bytes_accessed=10**6, transcendentals=0),
    )(lists, totals, *stores, first, second)
    chips = groups // 2
    begun = pl.pallas_call(
        late_kernel,
        out_shape=jax.ShapeDtypeStruct(partial_shape, F32),
        in_specs=[smem, smem] + [vmem] * 6,
        out_specs=vmem,
        input_output_aliases={7: 0},
        compiler_params=pltpu.CompilerParams(vmem_limit_bytes=6 * 2**20),
        name="late",
        cost_estimate=pl.CostEstimate(flops=2 * 10**9, bytes_accessed=10**6, transcendentals=0),
    )(lists, totals, *stores, first_new, begun)
    halves = jax.ShapeDtypeStruct((chips, own_blocks * share + NOTE, right_width), F32)
    _, keep, give = pl.pallas_call(
        functools.partial(last_kernel, groups),
        out_shape=(jax.ShapeDtypeStruct(partial_shape, F32), halves, halves),
        in_specs=[smem, smem] + [vmem] * 7,
        out_specs=(vmem,) * 3,
        input_output_aliases={7: 0},
        compiler_params=pltpu.CompilerParams(vmem_limit_bytes=6 * 2**20),
        name="last",
        cost_estimate=pl.CostEstimate(flops=2 * 10**9, bytes_accessed=10**6, transcendentals=0),
    )(lists, totals, *stores, second_new, begun, wavefunction)
    got = lax.ppermute(give, "ops", pairs)
    chip_masks = (1, 3, 2)
    chip_sum = jax.ShapeDtypeStruct((own_blocks * share, right_width), F32)
    note, mine, *outgoing = pl.pallas_call(
        functools.partial(chip_kernel, chip_masks),
        out_shape=(jax.ShapeDtypeStruct((holders, 128), F32),) + (chip_sum,) * 4,
        in_specs=[vmem, vmem],
        out_specs=(vmem,) * 5,
        compiler_params=pltpu.CompilerParams(vmem_limit_bytes=4 * 2**20),
        name="chip_sum",
    )(keep, got)

    def along_y(x, mask):
        return lax.ppermute(x, "ops", [(i, i ^ (2 * mask)) for i in range(groups)])

    notes = [note] + [along_y(note, mask) for mask in chip_masks]
    arrived = [along_y(x, mask) for x, mask in zip(outgoing, chip_masks)]
    first_sums = lax.all_to_all(
        (notes[0] + notes[1]) + (notes[2] + notes[3]), "blk", 0, 0, tiled=True
    )
    devices = groups * holders
    row_sums = jax.ShapeDtypeStruct((devices, 128), F32)
    shard = jax.ShapeDtypeStruct((own_blocks, share, right_width), F32)
    sigma_vector, scaled, second_sums = pl.pallas_call(
        combine_kernel,
        out_shape=(shard, shard, row_sums),
        in_specs=[smem, smem] + [vmem] * 7,
        out_specs=(vmem, vmem, vmem),
        compiler_params=pltpu.CompilerParams(vmem_limit_bytes=4 * 2**20),
        name="combine",
    )(left_dims, right_dims, mine, *arrived, first_sums, wavefunction, h_diagonal)
    second_sums = lax.all_to_all(second_sums, ("ops", "blk"), 0, 0, tiled=True)
    correction = pl.pallas_call(
        functools.partial(finish_kernel, left_dims.shape[0] * left_width * right_width),
        out_shape=shard,
        in_specs=[vmem, vmem, vmem, vmem],
        out_specs=vmem,
        compiler_params=pltpu.CompilerParams(vmem_limit_bytes=4 * 2**20),
        name="finish",
    )(second_sums, first_sums, scaled, wavefunction)
    return (sigma_vector, correction)


def solution(mesh):
    in_specs = (
        P("blk", None, None),
        P(),
        P(),
        P("ops", "blk", None, None),
        P("ops", "blk", None, None),
        P("ops", "blk"),
        P("ops", "blk"),
        P("ops", "blk"),
        P("ops", "blk"),
        P("ops", "blk"),
        P("blk", "ops", None),
    )
    out_specs = (P("blk", "ops", None), P("blk", "ops", None))
    return jax.shard_map(body, mesh=mesh, in_specs=in_specs, out_specs=out_specs, check_vma=False)
```

```python
import functools

import jax
import jax.numpy as jnp
from jax import lax
from jax.experimental import pallas as pl
from jax.experimental.pallas import tpu as pltpu
from jax.sharding import PartitionSpec as P

UNROLL = 16
TAIL = 4
LIST = 528
SPARE = 4
KINDS = 3
NOTE = 8
LEFT, RIGHT, TARGET, GROUP = 4, 9, 14, 17
MASKS = (((1, 3), (3, 1), (4, 12), (12, 4)), ((4, 12), (12, 4), (1, 3), (3, 1)))
F32 = jnp.float32
BF16 = jnp.bfloat16


def run_copies(copies):
    for copy in copies:
        copy.start()
    for copy in copies:
        copy.wait()


def pick_kernel(own, first, second, sems):
    core = lax.rem(lax.axis_index("ops"), 2)
    run_copies([
        pltpu.make_async_copy(own.at[pl.ds(2 * core + i, 1)], target, sems.at[i])
        for i, target in enumerate((first, second))
    ])


def place_kernel(tables, other, lists, totals, staged, scalars, sems):
    core = lax.rem(lax.axis_index("ops"), 2)
    holder = lax.axis_index("blk")
    slots = tables.shape[2]

    def code(bits):
        gray = bits ^ (bits >> 1)
        return jnp.where(core == 0, gray, ((gray & 1) << 1) | (gray >> 1))

    row = lax.broadcasted_iota(jnp.int32, (8, slots), 0)
    earlier = lax.broadcasted_iota(jnp.int32, (slots, slots), 0)
    later = lax.broadcasted_iota(jnp.int32, (slots, slots), 1)
    ahead = jnp.where(earlier <= later, 1.0, 0.0).astype(BF16)
    before = jnp.zeros((8, 1), jnp.int32)
    lives = []
    for group, table in enumerate((tables, other)):
        block, target = table[0, 0:1, :], table[0, 1:2, :]
        away, within = (block >> 2) ^ holder, block & 3
        along_x, along_z = code(away & 3), code(away >> 2)
        stream = within & 1
        entry = jnp.where(stream == 0, along_x | (along_z << 2), along_z | (along_x << 2))
        kind = jnp.where(entry < 8, 0, 1 + stream)
        kind = jnp.where(((within >> 1) == core) & (target < SPARE), kind, KINDS)
        word = (
            (entry & 7)
            | (stream << 3)
            | (table[0, 2:3, :] << LEFT)
            | (table[0, 3:4, :] << RIGHT)
            | (target << TARGET)
            | (group << GROUP)
        )
        chosen = row == kind
        counts = jnp.dot(
            jnp.where(chosen, 1.0, 0.0).astype(BF16), ahead, preferred_element_type=F32
        ).astype(jnp.int32)
        where = jnp.where(chosen, counts - 1 + row * LIST + before, 0)
        where = jnp.where(kind < KINDS, jnp.sum(where[:KINDS], axis=0, keepdims=True), KINDS * LIST)
        before = counts[:, slots - 1:]
        staged[group] = jnp.where(row < KINDS, counts, jnp.where(row == KINDS, word, where))
        lives.append(jnp.sum(jnp.where(target < SPARE, 1, 0)))
    run_copies([pltpu.make_async_copy(staged, scalars, sems.at[0])])
    for group in range(2):

        def places(i, carry, group=group):
            for u in range(16):
                lists[0, scalars[group, KINDS + 1, 16 * i + u]] = scalars[group, KINDS, 16 * i + u]
            return carry

        lax.fori_loop(0, (lives[group] + 15) // 16, places, 0)
    for i in range(KINDS):
        length = scalars[0, i, slots - 1] + scalars[1, i, slots - 1]
        totals[0, i] = length
        for u in range(UNROLL):
            lists[0, i * LIST + length + u] = SPARE << TARGET


def run_slots(lists, totals, which, lefts, rights, blocks, acc):
    def many(i, carry, width, offset):
        for u in range(width):
            word = lists[0, offset + i * width + u]
            own = (word >> GROUP) == 0
            left, right = (word >> LEFT) & 31, (word >> RIGHT) & 31
            psi = blocks[0][word & 7]
            if len(blocks) == 2:
                psi = jnp.where(((word >> 3) & 1) == 0, psi, blocks[1][word & 7])
            product = jnp.dot(
                jnp.where(own, lefts[0][0, left], lefts[1][0, left]), psi,
                preferred_element_type=F32,
            ).astype(BF16)
            acc[(word >> TARGET) & 7] += lax.dot_general(
                product, jnp.where(own, rights[0][0, right], rights[1][0, right]),
                (((1,), (1,)), ((), ())), preferred_element_type=F32,
            )
        return carry

    live, base = totals[0, which], which * LIST
    turns = (live + UNROLL - 1 - 2 * TAIL) // UNROLL
    lax.fori_loop(0, turns, functools.partial(many, width=UNROLL, offset=base), 0)
    rest = jnp.maximum(live - turns * UNROLL, 0)
    lax.fori_loop(
        0,
        (rest + TAIL - 1) // TAIL,
        functools.partial(many, width=TAIL, offset=base + turns * UNROLL),
        0,
    )


def early_kernel(lists, totals, left0, left1, right0, right1, first, second, acc):
    acc[...] = jnp.zeros_like(acc)
    run_slots(lists, totals, 0, (left0, left1), (right0, right1), (first, second), acc)


def late_kernel(lists, totals, left0, left1, right0, right1, first, begun, acc):
    del begun
    run_slots(lists, totals, 1, (left0, left1), (right0, right1), (first,), acc)


def last_kernel(
    groups, lists, totals, left0, left1, right0, right1, second, begun, own, acc, keep, give
):
    del begun
    run_slots(lists, totals, 2, (left0, left1), (right0, right1), (second,), acc)
    core = lax.rem(lax.axis_index("ops"), 2)
    chips, width = keep.shape[0], keep.shape[2]
    share = (keep.shape[1] - NOTE) // SPARE
    energy = jnp.zeros((1, 1), F32)
    norm = jnp.zeros((1, 1), F32)
    for b in range(SPARE):
        wide = own[b].astype(F32)
        energy += jnp.sum(acc[b] * wide, keepdims=True)
        norm += jnp.sum(wide * wide, keepdims=True)
        for y in range(chips):
            for out, place in ((keep, core), (give, 1 - core)):
                start = pl.multiple_of((2 * y + place) * share, share)
                out[y, b * share:(b + 1) * share] = acc[b, pl.ds(start, share), :]
    lane = lax.broadcasted_iota(jnp.int32, (NOTE, width), 1)
    note = jnp.where(lane == 0, energy, jnp.where(lane == 1, norm / groups, 0.0))
    for y in range(chips):
        for out in (keep, give):
            out[y, SPARE * share:] = note


def chip_kernel(masks, keep, got, note, mine, *outs):
    chip = lax.axis_index("ops") // 2
    rows = mine.shape[0]
    total = keep[0, rows:, :128] + got[0, rows:, :128]
    for i in range(note.shape[0] // NOTE):
        note[i * NOTE:(i + 1) * NOTE] = total
    for mask, out in zip((0,) + masks, (mine,) + outs):
        out[...] = keep[chip ^ mask, :rows] + got[chip ^ mask, :rows]


def combine_kernel(
    left_dims, right_dims, mine, near, far, across, totals, own, diagonal, sigma, scaled, sums
):
    group_rank, holder = lax.axis_index("ops"), lax.axis_index("blk")
    blocks, share, width = sigma.shape
    whole = jnp.sum(totals[...], axis=0, keepdims=True)
    rayleigh = whole[0:1, 0:1] / whole[0:1, 1:2]
    row = lax.broadcasted_iota(jnp.int32, (share, width), 0) + group_rank * share
    column = lax.broadcasted_iota(jnp.int32, (share, width), 1)
    start = pl.multiple_of(group_rank * share, share)
    along = jnp.zeros((1, 1), F32)
    square = jnp.zeros((1, 1), F32)
    for b in range(blocks):
        ident = holder * blocks + b
        inside = (row < left_dims[ident]) & (column < right_dims[ident])
        rows = slice(b * share, (b + 1) * share)
        total = (mine[rows] + near[rows]) + (far[rows] + across[rows])
        total = jnp.where(inside, total, 0.0)
        sigma[b] = total
        state = own[b, pl.ds(start, share), :].astype(F32)
        value = (total - rayleigh * state) / jnp.maximum(jnp.abs(diagonal[b] - rayleigh), 1.0)
        scaled[b] = value
        along += jnp.sum(state * value, keepdims=True)
        square += jnp.sum(value * value, keepdims=True)
    lane = lax.broadcasted_iota(jnp.int32, sums.shape, 1)
    sums[...] = jnp.where(lane == 0, along, jnp.where(lane == 1, square, 0.0))


def finish_kernel(slots_total, arrived, totals, scaled, own, correction):
    blocks, share, width = scaled.shape
    sums = jnp.sum(arrived[...], axis=0, keepdims=True)
    along, square = sums[0:1, 0:1], sums[0:1, 1:2]
    ratio = along / jnp.sum(totals[...], axis=0, keepdims=True)[0:1, 1:2]
    length_sq = jnp.maximum(square - along * ratio, 0.0)
    factor = jnp.sqrt(length_sq / slots_total + 1e-06)
    start = pl.multiple_of(lax.axis_index("ops") * share, share)
    for b in range(blocks):
        state = own[b, pl.ds(start, share), :].astype(F32)
        correction[b] = (scaled[b] - ratio * state) / factor


def body(
    wavefunction,
    left_dims,
    right_dims,
    left_ops,
    right_ops,
    source_block,
    target_slot,
    left_index,
    right_index,
    pair_count,
    h_diagonal,
):
    groups = lax.axis_size("ops")
    holders = lax.axis_size("blk")
    own_blocks, left_width, right_width = wavefunction.shape
    share = left_width // groups
    smem = pl.BlockSpec(memory_space=pltpu.SMEM)
    vmem = pl.BlockSpec(memory_space=pltpu.VMEM)
    anywhere = pl.BlockSpec(memory_space=pl.ANY)

    def in_vmem(x):
        return pltpu.with_memory_space_constraint(x, pltpu.VMEM)

    pairs = [(i, i ^ 1) for i in range(groups)]
    alive = lax.broadcasted_iota(jnp.int32, target_slot.shape, 1) < pair_count
    tables = jnp.stack(
        [source_block, jnp.where(alive, target_slot, SPARE), left_index, right_index], axis=1
    )
    tables_other = lax.ppermute(tables, "ops", pairs)

    def exchange(x, mask):
        return lax.ppermute(
            x,
            ("ops", "blk"),
            [
                (g * holders + h, g * holders + (h ^ mask[g % 2]))
                for g in range(groups)
                for h in range(holders)
            ],
        )

    block = jax.ShapeDtypeStruct((1, left_width, right_width), BF16)
    first, second = pl.pallas_call(
        pick_kernel,
        out_shape=(block, block),
        in_specs=[pl.BlockSpec(memory_space=pltpu.HBM)],
        out_specs=(vmem, vmem),
        scratch_shapes=[pltpu.SemaphoreType.DMA((2,))],
        compiler_params=pltpu.CompilerParams(vmem_limit_bytes=2**20),
        name="pick",
    )(pltpu.with_memory_space_constraint(wavefunction, pltpu.HBM))
    first, left_here, right_here = lax.optimization_barrier((first, left_ops, right_ops))
    left_other = lax.ppermute(left_here, "ops", pairs)
    right_other = lax.ppermute(right_here, "ops", pairs)
    for step, (one, two) in enumerate(zip(*MASKS)):
        first_new, second_new = exchange(first, one), exchange(second, two)
        if step == 1:
            second_new, tables_other = lax.optimization_barrier((second_new, tables_other))
            lists, totals = pl.pallas_call(
                place_kernel,
                out_shape=(
                    jax.ShapeDtypeStruct((1, KINDS * LIST + 1), jnp.int32),
                    jax.ShapeDtypeStruct((1, KINDS), jnp.int32),
                ),
                in_specs=[vmem, vmem],
                out_specs=(smem, smem),
                scratch_shapes=[
                    pltpu.VMEM((2, 8, tables.shape[2]), jnp.int32),
                    pltpu.SMEM((2, 8, tables.shape[2]), jnp.int32),
                    pltpu.SemaphoreType.DMA((1,)),
                ],
                compiler_params=pltpu.CompilerParams(vmem_limit_bytes=2 * 2**20),
                name="place",
                cost_estimate=pl.CostEstimate(
                    flops=10**9, bytes_accessed=10**4, transcendentals=0
                ),
            )(tables, tables_other)
        if step == 2:
            first_new, lists, totals = lax.optimization_barrier((first_new, lists, totals))
        if step < 3:
            first = jnp.concatenate([first, first_new])
            second = jnp.concatenate([second, second_new])

    stores = [in_vmem(x) for x in (left_ops, left_other, right_ops, right_other)]
    partial_shape = (own_blocks + 1, left_width, right_width)
    begun = pl.pallas_call(
        early_kernel,
        out_shape=jax.ShapeDtypeStruct(partial_shape, F32),
        in_specs=[smem, smem] + [vmem] * 6,
        out_specs=vmem,
        compiler_params=pltpu.CompilerParams(vmem_limit_bytes=6 * 2**20),
        name="early",
        cost_estimate=pl.CostEstimate(flops=8 * 10**9, bytes_accessed=10**6, transcendentals=0),
    )(lists, totals, *stores, first, second)
    chips = groups // 2
    begun = pl.pallas_call(
        late_kernel,
        out_shape=jax.ShapeDtypeStruct(partial_shape, F32),
        in_specs=[smem, smem] + [vmem] * 6,
        out_specs=vmem,
        input_output_aliases={7: 0},
        compiler_params=pltpu.CompilerParams(vmem_limit_bytes=6 * 2**20),
        name="late",
        cost_estimate=pl.CostEstimate(flops=2 * 10**9, bytes_accessed=10**6, transcendentals=0),
    )(lists, totals, *stores, first_new, begun)
    halves = jax.ShapeDtypeStruct((chips, own_blocks * share + NOTE, right_width), F32)
    _, keep, give = pl.pallas_call(
        functools.partial(last_kernel, groups),
        out_shape=(jax.ShapeDtypeStruct(partial_shape, F32), halves, halves),
        in_specs=[smem, smem] + [vmem] * 7,
        out_specs=(vmem,) * 3,
        input_output_aliases={7: 0},
        compiler_params=pltpu.CompilerParams(vmem_limit_bytes=6 * 2**20),
        name="last",
        cost_estimate=pl.CostEstimate(flops=2 * 10**9, bytes_accessed=10**6, transcendentals=0),
    )(lists, totals, *stores, second_new, begun, wavefunction)
    got = lax.ppermute(give, "ops", pairs)
    chip_masks = (1, 3, 2)
    chip_sum = jax.ShapeDtypeStruct((own_blocks * share, right_width), F32)
    note, mine, *outgoing = pl.pallas_call(
        functools.partial(chip_kernel, chip_masks),
        out_shape=(jax.ShapeDtypeStruct((holders, 128), F32),) + (chip_sum,) * 4,
        in_specs=[vmem, vmem],
        out_specs=(vmem,) * 5,
        compiler_params=pltpu.CompilerParams(vmem_limit_bytes=4 * 2**20),
        name="chip_sum",
    )(keep, got)

    def along_y(x, mask):
        return lax.ppermute(x, "ops", [(i, i ^ (2 * mask)) for i in range(groups)])

    notes = [note] + [along_y(note, mask) for mask in chip_masks]
    arrived = [along_y(x, mask) for x, mask in zip(outgoing, chip_masks)]
    first_sums = lax.all_to_all(
        (notes[0] + notes[1]) + (notes[2] + notes[3]), "blk", 0, 0, tiled=True
    )
    devices = groups * holders
    row_sums = jax.ShapeDtypeStruct((devices, 128), F32)
    shard = jax.ShapeDtypeStruct((own_blocks, share, right_width), F32)
    sigma_vector, scaled, second_sums = pl.pallas_call(
        combine_kernel,
        out_shape=(shard, shard, row_sums),
        in_specs=[smem, smem] + [vmem] * 7,
        out_specs=(vmem, vmem, vmem),
        compiler_params=pltpu.CompilerParams(vmem_limit_bytes=4 * 2**20),
        name="combine",
    )(left_dims, right_dims, mine, *arrived, first_sums, wavefunction, h_diagonal)
    second_sums = lax.all_to_all(second_sums, ("ops", "blk"), 0, 0, tiled=True)
    correction = pl.pallas_call(
        functools.partial(finish_kernel, left_dims.shape[0] * left_width * right_width),
        out_shape=shard,
        in_specs=[vmem, vmem, vmem, vmem],
        out_specs=vmem,
        compiler_params=pltpu.CompilerParams(vmem_limit_bytes=4 * 2**20),
        name="finish",
    )(second_sums, first_sums, scaled, wavefunction)
    return (sigma_vector, correction)


def solution(mesh):
    in_specs = (
        P("blk", None, None),
        P(),
        P(),
        P("ops", "blk", None, None),
        P("ops", "blk", None, None),
        P("ops", "blk"),
        P("ops", "blk"),
        P("ops", "blk"),
        P("ops", "blk"),
        P("ops", "blk"),
        P("blk", "ops", None),
    )
    out_specs = (P("blk", "ops", None), P("blk", "ops", None))
    return jax.shard_map(body, mesh=mesh, in_specs=in_specs, out_specs=out_specs, check_vma=False)
```

```python
import functools

import jax
import jax.numpy as jnp
from jax import lax
from jax.experimental import pallas as pl
from jax.experimental.pallas import tpu as pltpu
from jax.sharding import PartitionSpec as P

UNROLL = 16
TAIL = 4
LIST = 528
SPARE = 4
KINDS = 3
NOTE = 8
LEFT, RIGHT, TARGET, GROUP = 4, 9, 14, 17
MASKS = (((1, 3), (3, 1), (4, 12), (12, 4)), ((4, 12), (12, 4), (1, 3), (3, 1)))
F32 = jnp.float32
BF16 = jnp.bfloat16


def run_copies(copies):
    for copy in copies:
        copy.start()
    for copy in copies:
        copy.wait()


def pick_kernel(own, first, second, sems):
    core = lax.rem(lax.axis_index("ops"), 2)
    run_copies([
        pltpu.make_async_copy(own.at[pl.ds(2 * core + i, 1)], target, sems.at[i])
        for i, target in enumerate((first, second))
    ])


def place_kernel(tables, other, lists, totals, staged, scalars, sems):
    core = lax.rem(lax.axis_index("ops"), 2)
    holder = lax.axis_index("blk")
    slots = tables.shape[2]

    def code(bits):
        gray = bits ^ (bits >> 1)
        return jnp.where(core == 0, gray, ((gray & 1) << 1) | (gray >> 1))

    row = lax.broadcasted_iota(jnp.int32, (8, slots), 0)
    earlier = lax.broadcasted_iota(jnp.int32, (slots, slots), 0)
    later = lax.broadcasted_iota(jnp.int32, (slots, slots), 1)
    ahead = jnp.where(earlier <= later, 1.0, 0.0).astype(BF16)
    before = jnp.zeros((8, 1), jnp.int32)
    lives = []
    for group, table in enumerate((tables, other)):
        block, target = table[0, 0:1, :], table[0, 1:2, :]
        away, within = (block >> 2) ^ holder, block & 3
        along_x, along_z = code(away & 3), code(away >> 2)
        stream = within & 1
        entry = jnp.where(stream == 0, along_x | (along_z << 2), along_z | (along_x << 2))
        kind = jnp.where(entry < 8, 0, 1 + stream)
        kind = jnp.where(((within >> 1) == core) & (target < SPARE), kind, KINDS)
        word = (
            (entry & 7)
            | (stream << 3)
            | (table[0, 2:3, :] << LEFT)
            | (table[0, 3:4, :] << RIGHT)
            | (target << TARGET)
            | (group << GROUP)
        )
        chosen = row == kind
        counts = jnp.dot(
            jnp.where(chosen, 1.0, 0.0).astype(BF16), ahead, preferred_element_type=F32
        ).astype(jnp.int32)
        where = jnp.where(chosen, counts - 1 + row * LIST + before, 0)
        where = jnp.where(kind < KINDS, jnp.sum(where[:KINDS], axis=0, keepdims=True), KINDS * LIST)
        before = counts[:, slots - 1:]
        staged[group] = jnp.where(row < KINDS, counts, jnp.where(row == KINDS, word, where))
        lives.append(jnp.sum(jnp.where(target < SPARE, 1, 0)))
    run_copies([pltpu.make_async_copy(staged, scalars, sems.at[0])])
    for group in range(2):

        def places(i, carry, group=group):
            for u in range(16):
                lists[0, scalars[group, KINDS + 1, 16 * i + u]] = scalars[group, KINDS, 16 * i + u]
            return carry

        lax.fori_loop(0, (lives[group] + 15) // 16, places, 0)
    for i in range(KINDS):
        length = scalars[0, i, slots - 1] + scalars[1, i, slots - 1]
        totals[0, i] = length
        for u in range(UNROLL):
            lists[0, i * LIST + length + u] = SPARE << TARGET


def run_slots(lists, totals, which, lefts, rights, blocks, acc):
    def many(i, carry, width, offset):
        for u in range(width):
            word = lists[0, offset + i * width + u]
            own = (word >> GROUP) == 0
            left, right = (word >> LEFT) & 31, (word >> RIGHT) & 31
            psi = blocks[0][word & 7]
            if len(blocks) == 2:
                psi = jnp.where(((word >> 3) & 1) == 0, psi, blocks[1][word & 7])
            product = jnp.dot(
                jnp.where(own, lefts[0][0, left], lefts[1][0, left]), psi,
                preferred_element_type=F32,
            ).astype(BF16)
            acc[(word >> TARGET) & 7] += lax.dot_general(
                product, jnp.where(own, rights[0][0, right], rights[1][0, right]),
                (((1,), (1,)), ((), ())), preferred_element_type=F32,
            )
        return carry

    live, base = totals[0, which], which * LIST
    turns = (live + UNROLL - 1 - 2 * TAIL) // UNROLL
    lax.fori_loop(0, turns, functools.partial(many, width=UNROLL, offset=base), 0)
    rest = jnp.maximum(live - turns * UNROLL, 0)
    lax.fori_loop(
        0,
        (rest + TAIL - 1) // TAIL,
        functools.partial(many, width=TAIL, offset=base + turns * UNROLL),
        0,
    )


def early_kernel(lists, totals, left0, left1, right0, right1, first, second, acc):
    acc[...] = jnp.zeros_like(acc)
    run_slots(lists, totals, 0, (left0, left1), (right0, right1), (first, second), acc)


def late_kernel(lists, totals, left0, left1, right0, right1, first, begun, acc):
    del begun
    run_slots(lists, totals, 1, (left0, left1), (right0, right1), (first,), acc)


def last_kernel(
    groups, lists, totals, left0, left1, right0, right1, second, begun, own, acc, keep, give
):
    del begun
    run_slots(lists, totals, 2, (left0, left1), (right0, right1), (second,), acc)
    core = lax.rem(lax.axis_index("ops"), 2)
    chips, width = keep.shape[0], keep.shape[2]
    share = (keep.shape[1] - NOTE) // SPARE
    energy = jnp.zeros((8, width), F32)
    norm = jnp.zeros((8, width), F32)
    for b in range(SPARE):
        wide = own[b].astype(F32)
        energy += jnp.sum((acc[b] * wide).reshape(-1, 8, width), axis=0)
        norm += jnp.sum((wide * wide).reshape(-1, 8, width), axis=0)
        for y in range(chips):
            for out, place in ((keep, core), (give, 1 - core)):
                start = pl.multiple_of((2 * y + place) * share, share)
                out[y, b * share:(b + 1) * share] = acc[b, pl.ds(start, share), :]
    energy = jnp.sum(energy, keepdims=True)
    norm = jnp.sum(norm, keepdims=True)
    lane = lax.broadcasted_iota(jnp.int32, (NOTE, width), 1)
    note = jnp.where(lane == 0, energy, jnp.where(lane == 1, norm / groups, 0.0))
    for y in range(chips):
        for out in (keep, give):
            out[y, SPARE * share:] = note


def chip_kernel(masks, keep, got, note, mine, *outs):
    chip = lax.axis_index("ops") // 2
    rows = mine.shape[0]
    total = keep[0, rows:, :128] + got[0, rows:, :128]
    for i in range(note.shape[0] // NOTE):
        note[i * NOTE:(i + 1) * NOTE] = total
    for mask, out in zip((0,) + masks, (mine,) + outs):
        out[...] = keep[chip ^ mask, :rows] + got[chip ^ mask, :rows]


def combine_kernel(
    left_dims, right_dims, mine, near, far, across, totals, own, diagonal, sigma, scaled, sums
):
    group_rank, holder = lax.axis_index("ops"), lax.axis_index("blk")
    blocks, share, width = sigma.shape
    whole = jnp.sum(totals[...], axis=0, keepdims=True)
    rayleigh = whole[0:1, 0:1] / whole[0:1, 1:2]
    row = lax.broadcasted_iota(jnp.int32, (share, width), 0) + group_rank * share
    column = lax.broadcasted_iota(jnp.int32, (share, width), 1)
    start = pl.multiple_of(group_rank * share, share)
    along = jnp.zeros((share, width), F32)
    square = jnp.zeros((share, width), F32)
    for b in range(blocks):
        ident = holder * blocks + b
        inside = (row < left_dims[ident]) & (column < right_dims[ident])
        rows = slice(b * share, (b + 1) * share)
        total = (mine[rows] + near[rows]) + (far[rows] + across[rows])
        total = jnp.where(inside, total, 0.0)
        sigma[b] = total
        state = own[b, pl.ds(start, share), :].astype(F32)
        value = (total - rayleigh * state) / jnp.maximum(jnp.abs(diagonal[b] - rayleigh), 1.0)
        scaled[b] = value
        along += state * value
        square += value * value
    along = jnp.sum(along, keepdims=True)
    square = jnp.sum(square, keepdims=True)
    lane = lax.broadcasted_iota(jnp.int32, sums.shape, 1)
    sums[...] = jnp.where(lane == 0, along, jnp.where(lane == 1, square, 0.0))


def finish_kernel(slots_total, arrived, totals, scaled, own, correction):
    blocks, share, width = scaled.shape
    sums = jnp.sum(arrived[...], axis=0, keepdims=True)
    along, square = sums[0:1, 0:1], sums[0:1, 1:2]
    ratio = along / jnp.sum(totals[...], axis=0, keepdims=True)[0:1, 1:2]
    length_sq = jnp.maximum(square - along * ratio, 0.0)
    factor = jnp.sqrt(length_sq / slots_total + 1e-06)
    start = pl.multiple_of(lax.axis_index("ops") * share, share)
    for b in range(blocks):
        state = own[b, pl.ds(start, share), :].astype(F32)
        correction[b] = (scaled[b] - ratio * state) / factor


def body(
    wavefunction,
    left_dims,
    right_dims,
    left_ops,
    right_ops,
    source_block,
    target_slot,
    left_index,
    right_index,
    pair_count,
    h_diagonal,
):
    groups = lax.axis_size("ops")
    holders = lax.axis_size("blk")
    own_blocks, left_width, right_width = wavefunction.shape
    share = left_width // groups
    smem = pl.BlockSpec(memory_space=pltpu.SMEM)
    vmem = pl.BlockSpec(memory_space=pltpu.VMEM)
    anywhere = pl.BlockSpec(memory_space=pl.ANY)

    def in_vmem(x):
        return pltpu.with_memory_space_constraint(x, pltpu.VMEM)

    pairs = [(i, i ^ 1) for i in range(groups)]
    alive = lax.broadcasted_iota(jnp.int32, target_slot.shape, 1) < pair_count
    tables = jnp.stack(
        [source_block, jnp.where(alive, target_slot, SPARE), left_index, right_index], axis=1
    )
    tables_other = lax.ppermute(tables, "ops", pairs)

    def exchange(x, mask):
        return lax.ppermute(
            x,
            ("ops", "blk"),
            [
                (g * holders + h, g * holders + (h ^ mask[g % 2]))
                for g in range(groups)
                for h in range(holders)
            ],
        )

    block = jax.ShapeDtypeStruct((1, left_width, right_width), BF16)
    first, second = pl.pallas_call(
        pick_kernel,
        out_shape=(block, block),
        in_specs=[pl.BlockSpec(memory_space=pltpu.HBM)],
        out_specs=(vmem, vmem),
        scratch_shapes=[pltpu.SemaphoreType.DMA((2,))],
        compiler_params=pltpu.CompilerParams(vmem_limit_bytes=2**20),
        name="pick",
    )(pltpu.with_memory_space_constraint(wavefunction, pltpu.HBM))
    first, left_here, right_here = lax.optimization_barrier((first, left_ops, right_ops))
    left_other = lax.ppermute(left_here, "ops", pairs)
    right_other = lax.ppermute(right_here, "ops", pairs)
    for step, (one, two) in enumerate(zip(*MASKS)):
        first_new, second_new = exchange(first, one), exchange(second, two)
        if step == 1:
            second_new, tables_other = lax.optimization_barrier((second_new, tables_other))
            lists, totals = pl.pallas_call(
                place_kernel,
                out_shape=(
                    jax.ShapeDtypeStruct((1, KINDS * LIST + 1), jnp.int32),
                    jax.ShapeDtypeStruct((1, KINDS), jnp.int32),
                ),
                in_specs=[vmem, vmem],
                out_specs=(smem, smem),
                scratch_shapes=[
                    pltpu.VMEM((2, 8, tables.shape[2]), jnp.int32),
                    pltpu.SMEM((2, 8, tables.shape[2]), jnp.int32),
                    pltpu.SemaphoreType.DMA((1,)),
                ],
                compiler_params=pltpu.CompilerParams(vmem_limit_bytes=2 * 2**20),
                name="place",
                cost_estimate=pl.CostEstimate(
                    flops=10**9, bytes_accessed=10**4, transcendentals=0
                ),
            )(tables, tables_other)
        if step == 2:
            first_new, lists, totals = lax.optimization_barrier((first_new, lists, totals))
        if step < 3:
            first = jnp.concatenate([first, first_new])
            second = jnp.concatenate([second, second_new])

    stores = [in_vmem(x) for x in (left_ops, left_other, right_ops, right_other)]
    partial_shape = (own_blocks + 1, left_width, right_width)
    begun = pl.pallas_call(
        early_kernel,
        out_shape=jax.ShapeDtypeStruct(partial_shape, F32),
        in_specs=[smem, smem] + [vmem] * 6,
        out_specs=vmem,
        compiler_params=pltpu.CompilerParams(vmem_limit_bytes=6 * 2**20),
        name="early",
        cost_estimate=pl.CostEstimate(flops=8 * 10**9, bytes_accessed=10**6, transcendentals=0),
    )(lists, totals, *stores, first, second)
    chips = groups // 2
    begun = pl.pallas_call(
        late_kernel,
        out_shape=jax.ShapeDtypeStruct(partial_shape, F32),
        in_specs=[smem, smem] + [vmem] * 6,
        out_specs=vmem,
        input_output_aliases={7: 0},
        compiler_params=pltpu.CompilerParams(vmem_limit_bytes=6 * 2**20),
        name="late",
        cost_estimate=pl.CostEstimate(flops=2 * 10**9, bytes_accessed=10**6, transcendentals=0),
    )(lists, totals, *stores, first_new, begun)
    halves = jax.ShapeDtypeStruct((chips, own_blocks * share + NOTE, right_width), F32)
    _, keep, give = pl.pallas_call(
        functools.partial(last_kernel, groups),
        out_shape=(jax.ShapeDtypeStruct(partial_shape, F32), halves, halves),
        in_specs=[smem, smem] + [vmem] * 7,
        out_specs=(vmem,) * 3,
        input_output_aliases={7: 0},
        compiler_params=pltpu.CompilerParams(vmem_limit_bytes=6 * 2**20),
        name="last",
        cost_estimate=pl.CostEstimate(flops=2 * 10**9, bytes_accessed=10**6, transcendentals=0),
    )(lists, totals, *stores, second_new, begun, wavefunction)
    got = lax.ppermute(give, "ops", pairs)
    chip_masks = (1, 3, 2)
    chip_sum = jax.ShapeDtypeStruct((own_blocks * share, right_width), F32)
    note, mine, *outgoing = pl.pallas_call(
        functools.partial(chip_kernel, chip_masks),
        out_shape=(jax.ShapeDtypeStruct((holders, 128), F32),) + (chip_sum,) * 4,
        in_specs=[vmem, vmem],
        out_specs=(vmem,) * 5,
        compiler_params=pltpu.CompilerParams(vmem_limit_bytes=4 * 2**20),
        name="chip_sum",
    )(keep, got)

    def along_y(x, mask):
        return lax.ppermute(x, "ops", [(i, i ^ (2 * mask)) for i in range(groups)])

    notes = [note] + [along_y(note, mask) for mask in chip_masks]
    arrived = [along_y(x, mask) for x, mask in zip(outgoing, chip_masks)]
    first_sums = lax.all_to_all(
        (notes[0] + notes[1]) + (notes[2] + notes[3]), "blk", 0, 0, tiled=True
    )
    devices = groups * holders
    row_sums = jax.ShapeDtypeStruct((devices, 128), F32)
    shard = jax.ShapeDtypeStruct((own_blocks, share, right_width), F32)
    sigma_vector, scaled, second_sums = pl.pallas_call(
        combine_kernel,
        out_shape=(shard, shard, row_sums),
        in_specs=[smem, smem] + [vmem] * 7,
        out_specs=(vmem, vmem, vmem),
        compiler_params=pltpu.CompilerParams(vmem_limit_bytes=4 * 2**20),
        name="combine",
    )(left_dims, right_dims, mine, *arrived, first_sums, wavefunction, h_diagonal)
    second_sums = lax.all_to_all(second_sums, ("ops", "blk"), 0, 0, tiled=True)
    correction = pl.pallas_call(
        functools.partial(finish_kernel, left_dims.shape[0] * left_width * right_width),
        out_shape=shard,
        in_specs=[vmem, vmem, vmem, vmem],
        out_specs=vmem,
        compiler_params=pltpu.CompilerParams(vmem_limit_bytes=4 * 2**20),
        name="finish",
    )(second_sums, first_sums, scaled, wavefunction)
    return (sigma_vector, correction)


def solution(mesh):
    in_specs = (
        P("blk", None, None),
        P(),
        P(),
        P("ops", "blk", None, None),
        P("ops", "blk", None, None),
        P("ops", "blk"),
        P("ops", "blk"),
        P("ops", "blk"),
        P("ops", "blk"),
        P("ops", "blk"),
        P("blk", "ops", None),
    )
    out_specs = (P("blk", "ops", None), P("blk", "ops", None))
    return jax.shard_map(body, mesh=mesh, in_specs=in_specs, out_specs=out_specs, check_vma=False)
```

```python
import functools

import jax
import jax.numpy as jnp
from jax import lax
from jax.experimental import pallas as pl
from jax.experimental.pallas import tpu as pltpu
from jax.sharding import PartitionSpec as P

UNROLL = 16
TAIL = 4
LIST = 528
SPARE = 4
KINDS = 3
NOTE = 8
LEFT, RIGHT, TARGET, GROUP = 4, 9, 14, 17
MASKS = (((1, 3), (3, 1), (4, 12), (12, 4)), ((4, 12), (12, 4), (1, 3), (3, 1)))
F32 = jnp.float32
BF16 = jnp.bfloat16


def run_copies(copies):
    for copy in copies:
        copy.start()
    for copy in copies:
        copy.wait()


def pick_kernel(own, first, second, sems):
    core = lax.rem(lax.axis_index("ops"), 2)
    run_copies([
        pltpu.make_async_copy(own.at[pl.ds(2 * core + i, 1)], target, sems.at[i])
        for i, target in enumerate((first, second))
    ])


def place_kernel(tables, other, lists, totals, staged, scalars, sems):
    core = lax.rem(lax.axis_index("ops"), 2)
    holder = lax.axis_index("blk")
    slots = tables.shape[2]

    def code(bits):
        gray = bits ^ (bits >> 1)
        return jnp.where(core == 0, gray, ((gray & 1) << 1) | (gray >> 1))

    row = lax.broadcasted_iota(jnp.int32, (8, slots), 0)
    earlier = lax.broadcasted_iota(jnp.int32, (slots, slots), 0)
    later = lax.broadcasted_iota(jnp.int32, (slots, slots), 1)
    ahead = jnp.where(earlier <= later, 1.0, 0.0).astype(BF16)
    before = jnp.zeros((8, 1), jnp.int32)
    lives = []
    for group, table in enumerate((tables, other)):
        block, target = table[0, 0:1, :], table[0, 1:2, :]
        away, within = (block >> 2) ^ holder, block & 3
        along_x, along_z = code(away & 3), code(away >> 2)
        stream = within & 1
        entry = jnp.where(stream == 0, along_x | (along_z << 2), along_z | (along_x << 2))
        kind = jnp.where(entry < 8, 0, 1 + stream)
        kind = jnp.where(((within >> 1) == core) & (target < SPARE), kind, KINDS)
        word = (
            (entry & 7)
            | (stream << 3)
            | (table[0, 2:3, :] << LEFT)
            | (table[0, 3:4, :] << RIGHT)
            | (target << TARGET)
            | (group << GROUP)
        )
        chosen = row == kind
        counts = jnp.dot(
            jnp.where(chosen, 1.0, 0.0).astype(BF16), ahead, preferred_element_type=F32
        ).astype(jnp.int32)
        where = jnp.where(chosen, counts - 1 + row * LIST + before, 0)
        where = jnp.where(kind < KINDS, jnp.sum(where[:KINDS], axis=0, keepdims=True), KINDS * LIST)
        before = counts[:, slots - 1:]
        staged[group] = jnp.where(row < KINDS, counts, jnp.where(row == KINDS, word, where))
        lives.append(jnp.sum(jnp.where(target < SPARE, 1, 0)))
    run_copies([pltpu.make_async_copy(staged, scalars, sems.at[0])])
    for group in range(2):

        def places(i, carry, group=group):
            for u in range(16):
                lists[0, scalars[group, KINDS + 1, 16 * i + u]] = scalars[group, KINDS, 16 * i + u]
            return carry

        lax.fori_loop(0, (lives[group] + 15) // 16, places, 0)
    for i in range(KINDS):
        length = scalars[0, i, slots - 1] + scalars[1, i, slots - 1]
        totals[0, i] = length
        for u in range(UNROLL):
            lists[0, i * LIST + length + u] = SPARE << TARGET


def run_slots(lists, totals, which, lefts, rights, blocks, acc):
    def many(i, carry, width, offset):
        for u in range(width):
            word = lists[0, offset + i * width + u]
            own = (word >> GROUP) == 0
            left, right = (word >> LEFT) & 31, (word >> RIGHT) & 31
            psi = blocks[0][word & 7]
            if len(blocks) == 2:
                psi = jnp.where(((word >> 3) & 1) == 0, psi, blocks[1][word & 7])
            product = jnp.dot(
                jnp.where(own, lefts[0][0, left], lefts[1][0, left]), psi,
                preferred_element_type=F32,
            ).astype(BF16)
            acc[(word >> TARGET) & 7] += lax.dot_general(
                product, jnp.where(own, rights[0][0, right], rights[1][0, right]),
                (((1,), (1,)), ((), ())), preferred_element_type=F32,
            )
        return carry

    live, base = totals[0, which], which * LIST
    turns = (live + UNROLL - 1 - 2 * TAIL) // UNROLL
    lax.fori_loop(0, turns, functools.partial(many, width=UNROLL, offset=base), 0)
    rest = jnp.maximum(live - turns * UNROLL, 0)
    lax.fori_loop(
        0,
        (rest + TAIL - 1) // TAIL,
        functools.partial(many, width=TAIL, offset=base + turns * UNROLL),
        0,
    )


def early_kernel(lists, totals, left0, left1, right0, right1, first, second, acc):
    acc[...] = jnp.zeros_like(acc)
    run_slots(lists, totals, 0, (left0, left1), (right0, right1), (first, second), acc)


def late_kernel(lists, totals, left0, left1, right0, right1, first, begun, acc):
    del begun
    run_slots(lists, totals, 1, (left0, left1), (right0, right1), (first,), acc)


def last_kernel(
    groups, lists, totals, left0, left1, right0, right1, second, begun, own, acc, keep, give
):
    del begun
    run_slots(lists, totals, 2, (left0, left1), (right0, right1), (second,), acc)
    core = lax.rem(lax.axis_index("ops"), 2)
    chips, width = keep.shape[0], keep.shape[2]
    share = (keep.shape[1] - NOTE) // SPARE
    energy = jnp.zeros((8, width), F32)
    norm = jnp.zeros((8, width), F32)
    for b in range(SPARE):
        wide = own[b].astype(F32)
        energy += jnp.sum((acc[b] * wide).reshape(-1, 8, width), axis=0)
        norm += jnp.sum((wide * wide).reshape(-1, 8, width), axis=0)
        for y in range(chips):
            for out, place in ((keep, core), (give, 1 - core)):
                start = pl.multiple_of((2 * y + place) * share, share)
                out[y, b * share:(b + 1) * share] = acc[b, pl.ds(start, share), :]
    energy = jnp.sum(energy, keepdims=True)
    norm = jnp.sum(norm, keepdims=True)
    lane = lax.broadcasted_iota(jnp.int32, (NOTE, width), 1)
    note = jnp.where(lane == 0, energy, jnp.where(lane == 1, norm / groups, 0.0))
    for y in range(chips):
        for out in (keep, give):
            out[y, SPARE * share:] = note


def chip_kernel(masks, keep, got, note, mine, *outs):
    chip = lax.axis_index("ops") // 2
    rows = mine.shape[0]
    total = keep[0, rows:, :128] + got[0, rows:, :128]
    for i in range(note.shape[0] // NOTE):
        note[i * NOTE:(i + 1) * NOTE] = total
    for mask, out in zip((0,) + masks, (mine,) + outs):
        out[...] = keep[chip ^ mask, :rows] + got[chip ^ mask, :rows]


def combine_kernel(
    left_dims, right_dims, mine, near, far, across, totals, own, diagonal, sigma, scaled, sums
):
    group_rank, holder = lax.axis_index("ops"), lax.axis_index("blk")
    blocks, share, width = sigma.shape
    whole = jnp.sum(totals[...], axis=0, keepdims=True)
    rayleigh = whole[0:1, 0:1] / whole[0:1, 1:2]
    row = lax.broadcasted_iota(jnp.int32, (share, width), 0) + group_rank * share
    column = lax.broadcasted_iota(jnp.int32, (share, width), 1)
    start = pl.multiple_of(group_rank * share, share)
    along = jnp.zeros((share, width), F32)
    square = jnp.zeros((share, width), F32)
    for b in range(blocks):
        ident = holder * blocks + b
        inside = (row < left_dims[ident]) & (column < right_dims[ident])
        rows = slice(b * share, (b + 1) * share)
        total = (mine[rows] + near[rows]) + (far[rows] + across[rows])
        total = jnp.where(inside, total, 0.0)
        sigma[b] = total
        state = own[b, pl.ds(start, share), :].astype(F32)
        value = (total - rayleigh * state) / jnp.maximum(jnp.abs(diagonal[b] - rayleigh), 1.0)
        scaled[b] = value
        along += state * value
        square += value * value
    along = jnp.sum(along, keepdims=True)
    square = jnp.sum(square, keepdims=True)
    lane = lax.broadcasted_iota(jnp.int32, sums.shape, 1)
    sums[...] = jnp.where(lane == 0, along, jnp.where(lane == 1, square, 0.0))


def finish_kernel(slots_total, arrived, totals, scaled, own, correction):
    blocks, share, width = scaled.shape
    sums = jnp.sum(arrived[...], axis=0, keepdims=True)
    along, square = sums[0:1, 0:1], sums[0:1, 1:2]
    ratio = along / jnp.sum(totals[...], axis=0, keepdims=True)[0:1, 1:2]
    length_sq = jnp.maximum(square - along * ratio, 0.0)
    factor = jnp.sqrt(length_sq / slots_total + 1e-06)
    start = pl.multiple_of(lax.axis_index("ops") * share, share)
    for b in range(blocks):
        state = own[b, pl.ds(start, share), :].astype(F32)
        correction[b] = (scaled[b] - ratio * state) / factor


def body(
    wavefunction,
    left_dims,
    right_dims,
    left_ops,
    right_ops,
    source_block,
    target_slot,
    left_index,
    right_index,
    pair_count,
    h_diagonal,
):
    groups = lax.axis_size("ops")
    holders = lax.axis_size("blk")
    own_blocks, left_width, right_width = wavefunction.shape
    share = left_width // groups
    smem = pl.BlockSpec(memory_space=pltpu.SMEM)
    vmem = pl.BlockSpec(memory_space=pltpu.VMEM)
    anywhere = pl.BlockSpec(memory_space=pl.ANY)

    def in_vmem(x):
        return pltpu.with_memory_space_constraint(x, pltpu.VMEM)

    pairs = [(i, i ^ 1) for i in range(groups)]
    alive = lax.broadcasted_iota(jnp.int32, target_slot.shape, 1) < pair_count
    tables = jnp.stack(
        [source_block, jnp.where(alive, target_slot, SPARE), left_index, right_index], axis=1
    )
    tables_other = lax.ppermute(tables, "ops", pairs)

    def exchange(x, mask):
        return lax.ppermute(
            x,
            ("ops", "blk"),
            [
                (g * holders + h, g * holders + (h ^ mask[g % 2]))
                for g in range(groups)
                for h in range(holders)
            ],
        )

    block = jax.ShapeDtypeStruct((1, left_width, right_width), BF16)
    first, second = pl.pallas_call(
        pick_kernel,
        out_shape=(block, block),
        in_specs=[pl.BlockSpec(memory_space=pltpu.HBM)],
        out_specs=(vmem, vmem),
        scratch_shapes=[pltpu.SemaphoreType.DMA((2,))],
        compiler_params=pltpu.CompilerParams(vmem_limit_bytes=2**20),
        name="pick",
    )(pltpu.with_memory_space_constraint(wavefunction, pltpu.HBM))
    first, left_here, right_here = lax.optimization_barrier((first, left_ops, right_ops))
    left_other = lax.ppermute(left_here, "ops", pairs)
    right_other = lax.ppermute(right_here, "ops", pairs)
    for step, (one, two) in enumerate(zip(*MASKS)):
        first_new, second_new = exchange(first, one), exchange(second, two)
        if step == 1:
            second_new, tables_other = lax.optimization_barrier((second_new, tables_other))
            lists, totals = pl.pallas_call(
                place_kernel,
                out_shape=(
                    jax.ShapeDtypeStruct((1, KINDS * LIST + 1), jnp.int32),
                    jax.ShapeDtypeStruct((1, KINDS), jnp.int32),
                ),
                in_specs=[vmem, vmem],
                out_specs=(smem, smem),
                scratch_shapes=[
                    pltpu.VMEM((2, 8, tables.shape[2]), jnp.int32),
                    pltpu.SMEM((2, 8, tables.shape[2]), jnp.int32),
                    pltpu.SemaphoreType.DMA((1,)),
                ],
                compiler_params=pltpu.CompilerParams(vmem_limit_bytes=2 * 2**20),
                name="place",
                cost_estimate=pl.CostEstimate(
                    flops=10**9, bytes_accessed=10**4, transcendentals=0
                ),
            )(tables, tables_other)
        if step == 2:
            first_new, lists, totals = lax.optimization_barrier((first_new, lists, totals))
        if step < 3:
            first = jnp.concatenate([first, first_new])
            second = jnp.concatenate([second, second_new])

    stores = [in_vmem(x) for x in (left_ops, left_other, right_ops, right_other)]
    partial_shape = (own_blocks + 1, left_width, right_width)
    begun = pl.pallas_call(
        early_kernel,
        out_shape=jax.ShapeDtypeStruct(partial_shape, F32),
        in_specs=[smem, smem] + [vmem] * 6,
        out_specs=vmem,
        compiler_params=pltpu.CompilerParams(vmem_limit_bytes=6 * 2**20),
        name="early",
        cost_estimate=pl.CostEstimate(flops=8 * 10**9, bytes_accessed=10**6, transcendentals=0),
    )(lists, totals, *stores, first, second)
    chips = groups // 2
    begun = pl.pallas_call(
        late_kernel,
        out_shape=jax.ShapeDtypeStruct(partial_shape, F32),
        in_specs=[smem, smem] + [vmem] * 6,
        out_specs=vmem,
        input_output_aliases={7: 0},
        compiler_params=pltpu.CompilerParams(vmem_limit_bytes=6 * 2**20),
        name="late",
        cost_estimate=pl.CostEstimate(flops=2 * 10**9, bytes_accessed=10**6, transcendentals=0),
    )(lists, totals, *stores, first_new, begun)
    halves = jax.ShapeDtypeStruct((chips, own_blocks * share + NOTE, right_width), F32)
    _, keep, give = pl.pallas_call(
        functools.partial(last_kernel, groups),
        out_shape=(jax.ShapeDtypeStruct(partial_shape, F32), halves, halves),
        in_specs=[smem, smem] + [vmem] * 7,
        out_specs=(vmem,) * 3,
        input_output_aliases={7: 0},
        compiler_params=pltpu.CompilerParams(vmem_limit_bytes=6 * 2**20),
        name="last",
        cost_estimate=pl.CostEstimate(flops=2 * 10**9, bytes_accessed=10**6, transcendentals=0),
    )(lists, totals, *stores, second_new, begun, wavefunction)
    got = lax.ppermute(give, "ops", pairs)
    chip_masks = (2, 3, 1)
    chip_sum = jax.ShapeDtypeStruct((own_blocks * share, right_width), F32)
    note, mine, *outgoing = pl.pallas_call(
        functools.partial(chip_kernel, chip_masks),
        out_shape=(jax.ShapeDtypeStruct((holders, 128), F32),) + (chip_sum,) * 4,
        in_specs=[vmem, vmem],
        out_specs=(vmem,) * 5,
        compiler_params=pltpu.CompilerParams(vmem_limit_bytes=4 * 2**20),
        name="chip_sum",
    )(keep, got)

    def along_y(x, mask):
        return lax.ppermute(x, "ops", [(i, i ^ (2 * mask)) for i in range(groups)])

    notes = [note] + [along_y(note, mask) for mask in chip_masks]
    arrived = [along_y(x, mask) for x, mask in zip(outgoing, chip_masks)]
    first_sums = lax.all_to_all(
        (notes[0] + notes[1]) + (notes[2] + notes[3]), "blk", 0, 0, tiled=True
    )
    devices = groups * holders
    row_sums = jax.ShapeDtypeStruct((devices, 128), F32)
    shard = jax.ShapeDtypeStruct((own_blocks, share, right_width), F32)
    sigma_vector, scaled, second_sums = pl.pallas_call(
        combine_kernel,
        out_shape=(shard, shard, row_sums),
        in_specs=[smem, smem] + [vmem] * 7,
        out_specs=(vmem, vmem, vmem),
        compiler_params=pltpu.CompilerParams(vmem_limit_bytes=4 * 2**20),
        name="combine",
    )(left_dims, right_dims, mine, *arrived, first_sums, wavefunction, h_diagonal)
    second_sums = lax.all_to_all(second_sums, ("ops", "blk"), 0, 0, tiled=True)
    correction = pl.pallas_call(
        functools.partial(finish_kernel, left_dims.shape[0] * left_width * right_width),
        out_shape=shard,
        in_specs=[vmem, vmem, vmem, vmem],
        out_specs=vmem,
        compiler_params=pltpu.CompilerParams(vmem_limit_bytes=4 * 2**20),
        name="finish",
    )(second_sums, first_sums, scaled, wavefunction)
    return (sigma_vector, correction)


def solution(mesh):
    in_specs = (
        P("blk", None, None),
        P(),
        P(),
        P("ops", "blk", None, None),
        P("ops", "blk", None, None),
        P("ops", "blk"),
        P("ops", "blk"),
        P("ops", "blk"),
        P("ops", "blk"),
        P("ops", "blk"),
        P("blk", "ops", None),
    )
    out_specs = (P("blk", "ops", None), P("blk", "ops", None))
    return jax.shard_map(body, mesh=mesh, in_specs=in_specs, out_specs=out_specs, check_vma=False)
```
